256 devices in a mesh: dp: 64 (over z, y, core), tensor: 4 (over x).
Axes of the slice: x: 4, y: 4, z: 8, core: 2. Of those that a mesh axis runs over, the one named last changes fastest.
Arguments:
- inputs: bfloat16 [24576, 4096], P('dp'), may hold values from -6 to 6
- out_grads: bfloat16 [24576, 1024], P('dp', 'tensor'), may hold values from -0.3125 to 0.3125
- error_buffer: float32 [64, 4096, 1024], P('dp', None, 'tensor'), may hold values from -4 to 4
- start_basis: float32 [1024, 64], P('tensor'), may hold values from -4.2 to 4.2
Outputs:
- p_basis: float32 [4096, 64], replicated
- q_factor: float32 [1024, 64], P('tensor')
- new_error: float32 [64, 4096, 1024], P('dp', None, 'tensor')
The draws below stay inside these ranges and needn't reach their ends.
All inputs are finite; a program needn't handle non-finite values.
Results may differ from the reference program's by a relative error of at most 0.0003.
Values sent between devices are 32-bit elements; how exact they have to be, the bound alone decides.
No kernel may reach another device: no remote copies, remote signals or barrier semaphores. Data moves between devices by JAX's collectives and lax.ppermute only.
A program may use at most 64 MiB of HBM per device.

```python
import jax
import jax.numpy as jnp
from jax import lax

DW = 4096
KV = 1024
R = 64
TOK_DEV = 384
TOKENS = 24576
N_DP = 64


def draw_start_basis(key, part):
    key = jax.random.fold_in(key, 7)
    shared_key, column_key = jax.random.split(key)
    shared = jnp.clip(jax.random.normal(shared_key, (KV, 1), jnp.float32), -4.0, 4.0)
    private = jnp.clip(jax.random.normal(column_key, (KV, R), jnp.float32), -4.0, 4.0)
    spread = 0.02
    return shared + spread * private


def levels(stream_key, extent, cuts, low, largest):
    def one(position, shards_of):
        draws = jax.random.uniform(jax.random.fold_in(jax.random.fold_in(stream_key, 6), position), (shards_of,), jnp.float32, low / len(cuts), largest / len(cuts))
        return jnp.repeat(jnp.exp(draws), extent[position] // shards_of).reshape((-1,) + (1,) * (len(extent) - position - 1))

    loudness = one(*cuts[0])
    for cut in cuts[1:]:
        loudness = loudness * one(*cut)
    return loudness


def scatter_about(own_key, shape, width, limit, pieces=(), held_as=jnp.bfloat16):
    array = width * jax.random.normal(own_key, shape, jnp.float32)
    if pieces:
        array = array * levels(own_key, shape, pieces, -0.22, 0.18)
    return jnp.clip(array, -limit, limit).astype(held_as)


def setup_inputs(seed: int = 0) -> dict:
    key_list = jax.random.split(jax.random.key(seed), 5)
    inputs = scatter_about(key_list[0], (TOKENS, DW), 1.0, 6.0, ((0, 64),))
    out_grads = scatter_about(key_list[1], (TOKENS, KV), TOK_DEV ** -0.5, 0.3125, ((0, 64), (1, 4)))
    error_buffer = scatter_about(key_list[2], (N_DP, DW, KV), 0.5, 4.0, ((0, 64), (2, 4)), jnp.float32)
    start_basis = draw_start_basis(jax.random.fold_in(key_list[4], 71), 0)
    return dict(inputs=inputs, out_grads=out_grads, error_buffer=error_buffer, start_basis=start_basis)


def cholesky_step(block):
    gram_matrix = jnp.dot(block.T, block, precision=lax.Precision.HIGHEST)
    lower = jnp.linalg.cholesky(gram_matrix)
    return lax.linalg.triangular_solve(lower, block, left_side=False, lower=True, transpose_a=True)

def reference(inputs, out_grads, error_buffer, start_basis):
    input_blocks = inputs.reshape(N_DP, TOK_DEV, DW)
    grad_blocks = out_grads.reshape(N_DP, TOK_DEV, KV)

    def one_replica(items):
        left, right, stored = items
        product = jnp.einsum('td,tk->dk', left.astype(jnp.float32), right.astype(jnp.float32), precision=lax.Precision.HIGHEST)
        return product + stored
    moments = lax.map(one_replica, (input_blocks, grad_blocks, error_buffer))
    p_term = jnp.einsum('ndk,kr->dr', moments, start_basis, precision=lax.Precision.HIGHEST)
    p_basis = cholesky_step(cholesky_step(p_term))
    q_factor = jnp.einsum('ndk,dr->kr', moments, p_basis, precision=lax.Precision.HIGHEST) / N_DP
    rebuilt = jnp.dot(p_basis, q_factor.T, precision=lax.Precision.HIGHEST)
    new_error = moments - rebuilt[None]
    return (p_basis, q_factor, new_error)
```

```python
import jax
import jax.numpy as jnp
from jax import lax
from jax.sharding import Mesh, PartitionSpec as P

HIGH = lax.Precision.HIGHEST
NZ, NY, NC, NX = 8, 4, 2, 4
SWAP = [(0, 1), (1, 0)]


def cholesky_apply(block, gram_matrix):
    lower = jnp.linalg.cholesky(gram_matrix)
    return lax.linalg.triangular_solve(lower, block, left_side=False, lower=True, transpose_a=True)


def exchange(parts, axes):
    return lax.all_to_all(parts, axes, split_axis=0, concat_axis=0, tiled=True)


def sum_replicated(block, axis, size):
    return jnp.sum(exchange(jnp.broadcast_to(block[None], (size,) + block.shape), axis), axis=0)


def halves(array, core):
    half = array.shape[0] // 2
    own = lax.dynamic_slice_in_dim(array, core * half, half, 0)
    other = lax.dynamic_slice_in_dim(array, (1 - core) * half, half, 0)
    return own, other


def join(own, core):
    other = lax.ppermute(own, "c", SWAP)
    return jnp.concatenate([jnp.where(core == 0, own, other), jnp.where(core == 0, other, own)], axis=0)


def reduce_p(p_blocks, core):
    own, other = halves(p_blocks, core)
    own = own + lax.ppermute(other, "c", SWAP)
    block = jnp.sum(exchange(own, ("y", "x")).reshape(NY * NX, 1, 64, 128), axis=0)[0]
    block = sum_replicated(block, "z", NZ)
    gathered = exchange(jnp.broadcast_to(block[None], (NY * NX, 64, 128)), ("y", "x"))
    return join(gathered, core)


def reduce_q(q_rows, core):
    own, other = halves(q_rows, core)
    own = own + lax.ppermute(other, "c", SWAP)
    own = sum_replicated(own, "y", NY)
    own = sum_replicated(own, "z", NZ)
    return join(own, core)


def shards(inputs, out_grads, error_buffer, start_basis):
    core = lax.axis_index("c")
    moment = jnp.einsum("td,tk->dk", inputs, out_grads, preferred_element_type=jnp.float32) + error_buffer[0]
    p_rows = lax.dot_general(start_basis, moment, (((0,), (1,)), ((), ())), precision=HIGH)
    p_blocks = p_rows.reshape(64, 32, 128).transpose(1, 0, 2)
    p_blocks = reduce_p(p_blocks, core)
    p_basis = p_blocks.transpose(0, 2, 1).reshape(4096, 64)
    for sweep in range(2):
        p_basis = cholesky_apply(p_basis, jnp.dot(p_basis.T, p_basis, precision=HIGH))
    q_rows = lax.dot_general(p_basis, moment, (((0,), (0,)), ((), ())), precision=HIGH)
    q_factor = reduce_q(q_rows, core).T / (NZ * NY * NC)
    new_error = moment - jnp.dot(p_basis, q_factor.T, precision=HIGH)
    return (p_basis, q_factor, new_error[None])


def solution(mesh):
    fine = Mesh(mesh.devices.reshape(NZ, NY, NC, NX), ("z", "y", "c", "x"))
    dp = ("z", "y", "c")
    in_specs = (P(dp, None), P(dp, "x"), P(dp, None, "x"), P("x", None))
    out_specs = (P(), P("x", None), P(dp, None, "x"))
    return jax.shard_map(shards, mesh=fine, in_specs=in_specs, out_specs=out_specs, check_vma=False)
```

```python
import jax
import jax.numpy as jnp
from jax import lax
from jax.experimental import pallas as pl
from jax.experimental.pallas import tpu as pltpu
from jax.sharding import Mesh, PartitionSpec as P

HIGH = lax.Precision.HIGHEST
NZ, NY, NC, NX = 8, 4, 2, 4
DW, KV, R, TOK = 4096, 256, 64, 384
BF, F32 = jnp.bfloat16, jnp.float32
SWAP = [(0, 1), (1, 0)]
NN = (((1,), (0,)), ((), ()))
NT = (((1,), (1,)), ((), ()))
TN = (((0,), (0,)), ((), ()))
WHOLE = pl.BlockSpec(memory_space=pltpu.VMEM)


def dot(a, b, dims=NN):
    return lax.dot_general(a, b, dims, preferred_element_type=F32)


def dot_high(a, b, dims=NN):
    return lax.dot_general(a, b, dims, precision=HIGH, preferred_element_type=F32)


def split2(x):
    high = x.astype(BF)
    return high, (x - high.astype(F32)).astype(BF)


def split3(x):
    high = x.astype(BF)
    rest = x - high.astype(F32)
    middle = rest.astype(BF)
    return high, middle, (rest - middle.astype(F32)).astype(BF)


def moment_kernel(x_ref, g_ref, e_ref, s_ref, m_ref, p_ref):
    moment = dot(x_ref[...], g_ref[...], TN) + e_ref[...]
    m_ref[...] = moment
    s1, s2, s3 = split3(s_ref[...])
    m1, m2, m3 = split3(moment)
    t1 = dot(jnp.concatenate([s1, s2, s3], 0), m1, NT)
    t2 = dot(jnp.concatenate([s1, s2], 0), m2, NT)
    t3 = dot(s1, m3, NT)
    p_rows = (t1[2 * R:] + t2[R:] + t3) + (t1[R:2 * R] + t2[:R]) + t1[:R]
    for j in range(p_ref.shape[0]):
        p_ref[j] = p_rows[:, j * 128:(j + 1) * 128]


def moment_and_p(x, g, e, s_rows, cols=1024):
    return pl.pallas_call(
        moment_kernel,
        grid=(DW // cols,),
        in_specs=[
            pl.BlockSpec((TOK, cols), lambda i: (0, i)),
            pl.BlockSpec((TOK, KV), lambda i: (0, 0)),
            pl.BlockSpec((cols, KV), lambda i: (i, 0)),
            pl.BlockSpec((R, KV), lambda i: (0, 0)),
        ],
        out_specs=[
            pl.BlockSpec((cols, KV), lambda i: (i, 0)),
            pl.BlockSpec((cols // 128, R, 128), lambda i: (i, 0, 0)),
        ],
        out_shape=[jax.ShapeDtypeStruct((DW, KV), F32), jax.ShapeDtypeStruct((DW // 128, R, 128), F32)],
        compiler_params=pltpu.CompilerParams(vmem_limit_bytes=58 << 20),
        name="moment",
    )(x, g, e, s_rows)


def inverse_factor(gram):
    rows = lax.broadcasted_iota(jnp.int32, (8, 128), 0)
    lanes = lax.broadcasted_iota(jnp.int32, (8, 128), 1)
    zero = jnp.zeros((8, R), F32)
    groups = [
        jnp.where(lanes == rows + R + 8 * i, 1.0, jnp.concatenate([gram[8 * i:8 * i + 8], zero], axis=1))
        for i in range(R // 8)
    ]
    pivots = []
    for b in range(R // 8):
        columns = [
            [jnp.broadcast_to(groups[i][:, 8 * b + c:8 * b + c + 1], (8, 128)) for i in range(b, R // 8)]
            for c in range(8)
        ]
        diagonal = jnp.zeros((8, 128), F32)
        for j in range(8):
            head = columns[j][0]
            pivot = jnp.broadcast_to(head[j:j + 1], (8, 128))
            inverse = 1.0 / pivot
            diagonal = jnp.where(rows == j, pivot, diagonal)
            factors = [column * inverse for column in columns[j]]
            factors[0] = jnp.where(rows > j, factors[0], 0.0)
            row = jnp.broadcast_to(groups[b][j:j + 1], (8, 128))
            for c in range(j + 1, 8):
                weight = jnp.broadcast_to(head[c:c + 1], (8, 128))
                columns[c] = [column - factor * weight for column, factor in zip(columns[c], factors)]
            for i in range(b, R // 8):
                groups[i] = groups[i] - factors[i - b] * row
        pivots.append(diagonal)
    return jnp.concatenate([(a * lax.rsqrt(d))[:, R:] for a, d in zip(groups, pivots)], axis=0)


def basis_kernel(core_ref, own_ref, other_ref, m_ref, p_ref, q_ref, moment, block, sem):
    fetch = pltpu.make_async_copy(m_ref, moment, sem)
    fetch.start()
    core = core_ref[0]
    half = DW // 2
    for j in range(half // 128):
        block[:, pl.ds(pl.multiple_of(core * half + j * 128, 128), 128)] = own_ref[j]
        block[:, pl.ds(pl.multiple_of((1 - core) * half + j * 128, 128), 128)] = other_ref[j]
    rows = block[...]
    rows = dot_high(inverse_factor(dot_high(rows, rows, NT)), rows)
    block[...] = rows
    rows = block[...]
    p_ref[...] = dot_high(inverse_factor(dot_high(rows, rows, NT)), rows)
    fetch.wait()
    total = jnp.zeros((R, KV), F32)
    for t in range(8):
        p1, p2 = split2(p_ref[:, t * 512:(t + 1) * 512])
        m1, m2 = split2(moment[t * 512:(t + 1) * 512, :])
        u = dot(jnp.concatenate([p1, p2], 0), m1)
        total = total + (u[:R] + (u[R:] + dot(p1, m2)))
    q_ref[...] = total


def basis_and_q(core, own, other, moment):
    return pl.pallas_call(
        basis_kernel,
        in_specs=[pl.BlockSpec(memory_space=pltpu.SMEM), WHOLE, WHOLE, pl.BlockSpec(memory_space=pl.ANY)],
        out_specs=[WHOLE, WHOLE],
        out_shape=[jax.ShapeDtypeStruct((R, DW), F32), jax.ShapeDtypeStruct((R, KV), F32)],
        scratch_shapes=[pltpu.VMEM((DW, KV), F32), pltpu.VMEM((R, DW), F32), pltpu.SemaphoreType.DMA],
        compiler_params=pltpu.CompilerParams(vmem_limit_bytes=40 << 20),
        name="basis",
    )(core.reshape(1), own, other, moment)


def update_kernel(m_ref, p_ref, q_ref, e_ref):
    p1, p2 = split2(p_ref[...])
    q1, q2 = split2(q_ref[...])
    e_ref[...] = m_ref[...] - dot(jnp.concatenate([p1, p1, p2], 0), jnp.concatenate([q1, q2, q1], 0), TN)


def update(moment, p_rows, q_rows, cols=1024):
    return pl.pallas_call(
        update_kernel,
        grid=(DW // cols,),
        in_specs=[
            pl.BlockSpec((cols, KV), lambda i: (i, 0)),
            pl.BlockSpec((R, cols), lambda i: (0, i)),
            pl.BlockSpec((R, KV), lambda i: (0, 0)),
        ],
        out_specs=pl.BlockSpec((cols, KV), lambda i: (i, 0)),
        out_shape=jax.ShapeDtypeStruct((DW, KV), F32),
        compiler_params=pltpu.CompilerParams(vmem_limit_bytes=40 << 20),
        name="update",
    )(moment, p_rows, q_rows)


def exchange(parts, axes):
    return lax.all_to_all(parts, axes, split_axis=0, concat_axis=0, tiled=True)


def sum_replicated(block, axis, size):
    return jnp.sum(exchange(jnp.broadcast_to(block[None], (size,) + block.shape), axis), axis=0)


def halves(array, core):
    half = array.shape[0] // 2
    own = lax.dynamic_slice_in_dim(array, core * half, half, 0)
    other = lax.dynamic_slice_in_dim(array, (1 - core) * half, half, 0)
    return own, other


def swap(array):
    return lax.ppermute(array, "c", SWAP)


def shards(inputs, out_grads, error_buffer, start_basis):
    core = lax.axis_index("c")
    moment, p_blocks = moment_and_p(inputs, out_grads, error_buffer[0], start_basis.T)

    own, other = halves(p_blocks, core)
    block = jnp.sum(exchange(own + swap(other), ("y", "x")), axis=0)
    block = sum_replicated(block, "z", NZ)
    own = exchange(jnp.broadcast_to(block[None], (NY * NX, R, 128)), ("y", "x"))
    p_rows, q_rows = basis_and_q(core, own, swap(own), moment)

    own, other = halves(q_rows, core)
    own = sum_replicated(own + swap(other), "y", NY)
    own = sum_replicated(own, "z", NZ) / (NZ * NY * NC)
    other = swap(own)
    q_rows = jnp.concatenate([jnp.where(core == 0, own, other), jnp.where(core == 0, other, own)], axis=0)
    return (p_rows.T, q_rows.T, update(moment, p_rows, q_rows)[None])


def solution(mesh):
    fine = Mesh(mesh.devices.reshape(NZ, NY, NC, NX), ("z", "y", "c", "x"))
    dp = ("z", "y", "c")
    in_specs = (P(dp, None), P(dp, "x"), P(dp, None, "x"), P("x", None))
    out_specs = (P(), P("x", None), P(dp, None, "x"))
    return jax.shard_map(shards, mesh=fine, in_specs=in_specs, out_specs=out_specs, check_vma=False)
```

```python
import functools

import jax
import jax.numpy as jnp
from jax import lax
from jax.experimental import pallas as pl
from jax.experimental.pallas import tpu as pltpu
from jax.sharding import Mesh, PartitionSpec as P

HIGH = lax.Precision.HIGHEST
NZ, NY, NC, NX = 8, 4, 2, 4
DW, KV, R, TOK = 4096, 256, 64, 384
HALF, BLOCKS = DW // 2, DW // 256
BF, F32 = jnp.bfloat16, jnp.float32
SWAP = [(0, 1), (1, 0)]
NN = (((1,), (0,)), ((), ()))
NT = (((1,), (1,)), ((), ()))
TN = (((0,), (0,)), ((), ()))
VMEM = pl.BlockSpec(memory_space=pltpu.VMEM)
SMEM = pl.BlockSpec(memory_space=pltpu.SMEM)
HBM = pl.BlockSpec(memory_space=pltpu.HBM)
LIMIT = pltpu.CompilerParams(vmem_limit_bytes=24 << 20)


def shape(*dims, dtype=F32):
    return jax.ShapeDtypeStruct(dims, dtype)


def dot(a, b, dims=NN):
    return lax.dot_general(a, b, dims, preferred_element_type=F32)


def dot_high(a, b, dims=NN):
    return lax.dot_general(a, b, dims, precision=HIGH, preferred_element_type=F32)


def lanes(start, size):
    return pl.ds(pl.multiple_of(start, size), size)


def split2(x):
    high = x.astype(BF)
    return high, (x - high.astype(F32)).astype(BF)


def split3(x):
    high = x.astype(BF)
    rest = x - high.astype(F32)
    middle = rest.astype(BF)
    return high, middle, (rest - middle.astype(F32)).astype(BF)


COLS = 512


def moment_kernel(half_ref, x_hbm, g_hbm, e_hbm, s_hbm, m_ref, p_ref, x_buf, g_buf, s_buf, sems):
    base = half_ref[0] * HALF
    steps = HALF // COLS
    small = [
        pltpu.make_async_copy(g_hbm, g_buf, sems.at[0]),
        pltpu.make_async_copy(s_hbm, s_buf, sems.at[1]),
    ]
    copies = []
    for j in range(steps):
        at = lanes(base + j * COLS, COLS)
        copies.append((
            pltpu.make_async_copy(x_hbm.at[:, at], x_buf.at[j], sems.at[2 + 2 * j]),
            pltpu.make_async_copy(e_hbm.at[at, :], m_ref.at[pl.ds(j * COLS, COLS), :], sems.at[3 + 2 * j]),
        ))
    for copy in small:
        copy.start()
    for pair in copies:
        pair[0].start()
        pair[1].start()
    for copy in small:
        copy.wait()
    g = g_buf[...]
    s1, s2, s3 = split3(s_buf[...])
    s123, s12 = jnp.concatenate([s1, s2, s3], 0), jnp.concatenate([s1, s2], 0)
    for j in range(steps):
        copies[j][0].wait()
        product = dot(x_buf[j], g, TN)
        copies[j][1].wait()
        at = pl.ds(j * COLS, COLS)
        moment = product + m_ref[at, :]
        m_ref[at, :] = moment
        m1, m2, m3 = split3(moment)
        t1, t2, t3 = dot(m1, s123, NT).T, dot(m2, s12, NT).T, dot(m3, s1, NT).T
        p_rows = (t1[2 * R:] + t2[R:] + t3) + (t1[R:2 * R] + t2[:R]) + t1[:R]
        for i in range(COLS // 128):
            p_ref[j * (COLS // 128) + i] = p_rows[:, i * 128:(i + 1) * 128]


def moment_half(half, x, g, e, s_rows):
    steps = HALF // COLS
    return pl.pallas_call(
        moment_kernel,
        in_specs=[SMEM, HBM, HBM, HBM, HBM],
        out_specs=[VMEM, VMEM],
        out_shape=[shape(HALF, KV), shape(BLOCKS, R, 128)],
        scratch_shapes=[
            pltpu.VMEM((steps, TOK, COLS), BF),
            pltpu.VMEM((TOK, KV), BF),
            pltpu.VMEM((R, KV), F32),
            pltpu.SemaphoreType.DMA((2 + 2 * steps,)),
        ],
        compiler_params=LIMIT,
        cost_estimate=pl.CostEstimate(flops=10 ** 9, bytes_accessed=4 << 20, transcendentals=0),
        name="moment",
    )(half.reshape(1), x, g, e, s_rows)


def inverse_factor(gram):
    rows = lax.broadcasted_iota(jnp.int32, (8, 128), 0)
    lanes = lax.broadcasted_iota(jnp.int32, (8, 128), 1)
    zero = jnp.zeros((8, R), F32)
    groups = [
        jnp.where(lanes == rows + R + 8 * i, 1.0, jnp.concatenate([gram[8 * i:8 * i + 8], zero], axis=1))
        for i in range(R // 8)
    ]
    pivots = []
    for b in range(R // 8):
        columns = [
            [jnp.broadcast_to(groups[i][:, 8 * b + c:8 * b + c + 1], (8, 128)) for i in range(b, R // 8)]
            for c in range(8)
        ]
        diagonal = jnp.zeros((8, 128), F32)
        for j in range(8):
            head = columns[j][0]
            pivot = jnp.broadcast_to(head[j:j + 1], (8, 128))
            inverse = 1.0 / pivot
            diagonal = jnp.where(rows == j, pivot, diagonal)
            factors = [column * inverse for column in columns[j]]
            factors[0] = jnp.where(rows > j, factors[0], 0.0)
            row = jnp.broadcast_to(groups[b][j:j + 1], (8, 128))
            for c in range(j + 1, 8):
                weight = jnp.broadcast_to(head[c:c + 1], (8, 128))
                columns[c] = [column - factor * weight for column, factor in zip(columns[c], factors)]
            for i in range(b, R // 8):
                groups[i] = groups[i] - factors[i - b] * row
        pivots.append(diagonal)
    return jnp.concatenate([(a * lax.rsqrt(d))[:, R:] for a, d in zip(groups, pivots)], axis=0)


def gram_matrix(rows):
    a1, a2, a3 = split3(rows)
    t = dot(jnp.concatenate([a1, a2, a3], 0), jnp.concatenate([a1, a2], 0), NT)
    t21, t31 = t[R:2 * R, :R], t[2 * R:, :R]
    return t[:R, :R] + ((t21 + t21.T) + (t[R:2 * R, R:] + (t31 + t31.T)))


def first_round_kernel(core_ref, own_ref, other_ref, m_own_ref, m_other_ref, b_ref, w_own_ref, w_other_ref, w_ref):
    starts = core_ref[0] * HALF, HALF - core_ref[0] * HALF
    for j in range(BLOCKS):
        b_ref[:, lanes(starts[0] + j * 128, 128)] = own_ref[j]
        b_ref[:, lanes(starts[1] + j * 128, 128)] = other_ref[j]
    rows = b_ref[...]
    b_ref[...] = dot_high(inverse_factor(gram_matrix(rows)), rows)
    total = jnp.zeros((R, KV), F32)
    for start, m_ref in zip(starts, (m_own_ref, m_other_ref)):
        for t in range(0, HALF, COLS):
            b1, b2 = split2(b_ref[:, lanes(start + t, COLS)])
            m1, m2 = split2(m_ref[t:t + COLS, :])
            u = dot(jnp.concatenate([b1, b2], 0), m1)
            total = total + (u[:R] + (u[R:] + dot(b1, m2)))
    w_ref[...] = total
    mine = core_ref[0] * (R // 2)
    w_own_ref[...] = w_ref[lanes(mine, R // 2), :]
    w_other_ref[...] = w_ref[lanes(R // 2 - mine, R // 2), :]


def first_round(core, own, other, m_own, m_other):
    return pl.pallas_call(
        first_round_kernel,
        in_specs=[SMEM] + [VMEM] * 4,
        out_specs=[VMEM] * 3,
        out_shape=[shape(R, DW), shape(R // 2, KV), shape(R // 2, KV)],
        scratch_shapes=[pltpu.VMEM((R, KV), F32)],
        compiler_params=LIMIT,
        cost_estimate=pl.CostEstimate(flops=2 * 10 ** 9, bytes_accessed=6 << 20, transcendentals=0),
        name="first_round",
    )(core.reshape(1), own, other, m_own, m_other)


def second_round_kernel(b_ref, after_ref, p_hbm, p1_ref, p2_ref, l_ref, p_buf, sem):
    del after_ref
    rows = b_ref[...]
    factor = inverse_factor(gram_matrix(rows))
    l_ref[...] = factor
    p_buf[...] = dot_high(factor, rows)
    copy = pltpu.make_async_copy(p_buf, p_hbm, sem)
    copy.start()
    p1_ref[...], p2_ref[...] = split2(p_buf[...])
    copy.wait()


def second_round(basis, after):
    return pl.pallas_call(
        second_round_kernel,
        in_specs=[VMEM, pl.BlockSpec(memory_space=pl.ANY)],
        out_specs=[HBM, VMEM, VMEM, VMEM],
        out_shape=[shape(R, DW), shape(R, DW, dtype=BF), shape(R, DW, dtype=BF), shape(R, R)],
        scratch_shapes=[pltpu.VMEM((R, DW), F32), pltpu.SemaphoreType.DMA],
        compiler_params=LIMIT,
        cost_estimate=pl.CostEstimate(flops=10 ** 9, bytes_accessed=4 << 20, transcendentals=0),
        name="second_round",
    )(basis, after)


def update_kernel(core_ref, m_own_ref, m_other_ref, p1_ref, p2_ref, l_ref, w_own_ref, w_other_ref, e_hbm, q_ref, w_ref, out, sems):
    core = core_ref[0]
    mine = core * (R // 2)
    w_ref[lanes(mine, R // 2), :] = w_own_ref[...]
    w_ref[lanes(R // 2 - mine, R // 2), :] = w_other_ref[...]
    q = dot_high(l_ref[...], w_ref[...]) * (1.0 / (NZ * NY * NC))
    q_ref[...] = q
    q1, q2 = split2(q)
    q121 = jnp.concatenate([q1, q2, q1], 0)
    copies = []
    for part, m_ref in ((0, m_own_ref), (1, m_other_ref)):
        base = core * HALF if part == 0 else HALF - core * HALF
        for t in range(0, HALF, COLS):
            here = part * HALF + t
            p1, p2 = p1_ref[:, lanes(base + t, COLS)], p2_ref[:, lanes(base + t, COLS)]
            out[here:here + COLS, :] = m_ref[t:t + COLS, :] - dot(jnp.concatenate([p1, p1, p2], 0), q121, TN)
            target = e_hbm.at[lanes(base + t, COLS), :]
            copies.append(pltpu.make_async_copy(out.at[pl.ds(here, COLS), :], target, sems.at[len(copies)]))
            copies[-1].start()
    for copy in copies:
        copy.wait()


def update(core, m_own, m_other, p1, p2, factor, w_own, w_other):
    return pl.pallas_call(
        update_kernel,
        in_specs=[SMEM] + [VMEM] * 7,
        out_specs=[HBM, VMEM],
        out_shape=[shape(DW, KV), shape(R, KV)],
        scratch_shapes=[pltpu.VMEM((R, KV), F32), pltpu.VMEM((DW, KV), F32), pltpu.SemaphoreType.DMA((DW // COLS,))],
        compiler_params=LIMIT,
        name="update",
    )(core.reshape(1), m_own, m_other, p1, p2, factor, w_own, w_other)


def sum_y_kernel(w_ref, s1_ref, s2_ref, s3_ref, after_ref, out_ref):
    del after_ref
    total = (w_ref[...] + s2_ref[...]) + (s1_ref[...] + s3_ref[...])
    for i in range(NZ):
        out_ref[i] = total


def sum_y(w, shifted, after):
    return pl.pallas_call(
        sum_y_kernel,
        in_specs=[VMEM] * 4 + [pl.BlockSpec(memory_space=pl.ANY)],
        out_specs=VMEM,
        out_shape=shape(NZ, R // 2, KV),
        compiler_params=LIMIT,
        name="sum_y",
    )(w, *shifted, after)


def exchange(parts, axes):
    return lax.all_to_all(parts, axes, split_axis=0, concat_axis=0, tiled=True)


def sum_replicated(block, axis, size):
    return jnp.sum(exchange(jnp.broadcast_to(block[None], (size,) + block.shape), axis), axis=0)


def swap(array):
    return lax.ppermute(array, "c", SWAP)


def shift_y(array, by):
    return lax.ppermute(array, "y", [(i, (i + by) % NY) for i in range(NY)])


def shards(inputs, out_grads, error_buffer, start_basis):
    core = lax.axis_index("c")
    arguments = (inputs, out_grads, error_buffer[0], start_basis.T)
    x, g, e, s_rows = [pltpu.with_memory_space_constraint(array, pltpu.HBM) for array in arguments]
    half = functools.partial(moment_half, x=x, g=g, e=e, s_rows=s_rows)
    m_other, p_other = half(1 - core)
    arrived = swap(p_other)
    m_own, p_own = half(core)

    block = jnp.sum(exchange(p_own + arrived, ("y", "x")), axis=0)
    block = sum_replicated(block, "z", NZ)
    own = exchange(jnp.broadcast_to(block[None], (NY * NX, R, 128)), ("y", "x"))
    basis, w_own, w_other = first_round(core, own, swap(own), m_own, m_other)

    w = w_own + swap(w_other)
    shifted = [shift_y(w, by) for by in (1, 2, 3)]
    p_rows, p1, p2, factor = second_round(basis, w)
    w = jnp.sum(exchange(sum_y(w, shifted, factor), "z"), axis=0)
    error, q_rows = update(core, m_own, m_other, p1, p2, factor, w, swap(w))
    return (p_rows.T, q_rows.T, error[None])


def solution(mesh):
    fine = Mesh(mesh.devices.reshape(NZ, NY, NC, NX), ("z", "y", "c", "x"))
    dp = ("z", "y", "c")
    in_specs = (P(dp, None), P(dp, "x"), P(dp, None, "x"), P("x", None))
    out_specs = (P(), P("x", None), P(dp, None, "x"))
    return jax.shard_map(shards, mesh=fine, in_specs=in_specs, out_specs=out_specs, check_vma=False)
```

```python
import jax
import jax.numpy as jnp
from jax import lax
from jax.experimental import pallas as pl
from jax.experimental.pallas import tpu as pltpu
from jax.sharding import Mesh, PartitionSpec as P

HIGH = lax.Precision.HIGHEST
NZ, NY, NC, NX = 8, 4, 2, 4
DW, KV, R, TOK = 4096, 256, 64, 384
HALF, BLOCKS = DW // 2, DW // 256
BF, F32 = jnp.bfloat16, jnp.float32
SWAP = [(0, 1), (1, 0)]
NN = (((1,), (0,)), ((), ()))
NT = (((1,), (1,)), ((), ()))
TN = (((0,), (0,)), ((), ()))
VMEM = pl.BlockSpec(memory_space=pltpu.VMEM)
SMEM = pl.BlockSpec(memory_space=pltpu.SMEM)
HBM = pl.BlockSpec(memory_space=pltpu.HBM)
LIMIT = pltpu.CompilerParams(vmem_limit_bytes=24 << 20)
SMALL = pltpu.CompilerParams(vmem_limit_bytes=8 << 20)


def shape(*dims, dtype=F32):
    return jax.ShapeDtypeStruct(dims, dtype)


def dot(a, b, dims=NN):
    return lax.dot_general(a, b, dims, preferred_element_type=F32)


def dot_high(a, b, dims=NN):
    return lax.dot_general(a, b, dims, precision=HIGH, preferred_element_type=F32)


def lanes(start, size):
    return pl.ds(pl.multiple_of(start, size), size)


def split2(x):
    high = x.astype(BF)
    return high, (x - high.astype(F32)).astype(BF)


def split3(x):
    high = x.astype(BF)
    rest = x - high.astype(F32)
    middle = rest.astype(BF)
    return high, middle, (rest - middle.astype(F32)).astype(BF)


COLS = 512
LOAD = 1024


def split_basis(s):
    s1, s2, s3 = split3(s)
    return jnp.concatenate([s1, s2, s3], 0), jnp.concatenate([s1, s2], 0), s1


def p_half(moment, basis, p_ref):
    m1, m2, m3 = split3(moment)
    s123, s12, s1 = split_basis(basis)
    t1, t2, t3 = dot(m1, s123, NT).T, dot(m2, s12, NT).T, dot(m3, s1, NT).T
    rows = (t1[2 * R:] + t2[R:] + t3) + (t1[R:2 * R] + t2[:R]) + t1[:R]
    for i in range(BLOCKS):
        p_ref[i] = rows[:, i * 128:(i + 1) * 128]


def moment_kernel(core_ref, x_hbm, g_hbm, e_hbm, s_hbm, m_ref, p_ref, s_ref, x_buf, g_buf, sems):
    other = HALF - core_ref[0] * HALF
    starts = [lax.rem(other + j * LOAD, DW) for j in range(DW // LOAD)]
    small = [
        pltpu.make_async_copy(g_hbm, g_buf, sems.at[0]),
        pltpu.make_async_copy(s_hbm, s_ref, sems.at[1]),
    ]
    large = [
        (
            pltpu.make_async_copy(x_hbm.at[:, lanes(start, LOAD)], x_buf.at[j], sems.at[2 + 2 * j]),
            pltpu.make_async_copy(e_hbm.at[lanes(start, LOAD), :], m_ref.at[lanes(start, LOAD), :], sems.at[3 + 2 * j]),
        )
        for j, start in enumerate(starts)
    ]
    for copy in small:
        copy.start()
    for pair in large:
        pair[0].start()
        pair[1].start()
    for copy in small:
        copy.wait()
    g = g_buf[...]
    for j, start in enumerate(starts):
        large[j][0].wait()
        large[j][1].wait()
        at = lanes(start, LOAD)
        m_ref[at, :] = dot(x_buf[j], g, TN) + m_ref[at, :]
        if (j + 1) * LOAD == HALF:
            p_half(m_ref[lanes(other, HALF), :], s_ref[...], p_ref)


def moment_and_other(core, x, g, e, s_rows):
    steps = DW // LOAD
    return pl.pallas_call(
        moment_kernel,
        in_specs=[SMEM, HBM, HBM, HBM, HBM],
        out_specs=[VMEM] * 3,
        out_shape=[shape(DW, KV), shape(BLOCKS, R, 128), shape(R, KV)],
        scratch_shapes=[
            pltpu.VMEM((steps, TOK, LOAD), BF),
            pltpu.VMEM((TOK, KV), BF),
            pltpu.SemaphoreType.DMA((2 + 2 * steps,)),
        ],
        compiler_params=LIMIT,
        name="moment",
    )(core.reshape(1), x, g, e, s_rows)


def own_kernel(core_ref, m_ref, s_ref, p_ref):
    p_half(m_ref[lanes(core_ref[0] * HALF, HALF), :], s_ref[...], p_ref)


def p_own_half(core, moment, s_rows):
    return pl.pallas_call(
        own_kernel,
        in_specs=[SMEM, VMEM, VMEM],
        out_specs=VMEM,
        out_shape=shape(BLOCKS, R, 128),
        compiler_params=LIMIT,
        cost_estimate=pl.CostEstimate(flops=10 ** 9, bytes_accessed=4 << 20, transcendentals=0),
        name="p_own",
    )(core.reshape(1), moment, s_rows)


def inverse_factor(gram):
    rows = lax.broadcasted_iota(jnp.int32, (8, 128), 0)
    lanes = lax.broadcasted_iota(jnp.int32, (8, 128), 1)
    zero = jnp.zeros((8, R), F32)
    groups = [
        jnp.where(lanes == rows + R + 8 * i, 1.0, jnp.concatenate([gram[8 * i:8 * i + 8], zero], axis=1))
        for i in range(R // 8)
    ]
    pivots = []
    for b in range(R // 8):
        columns = [
            [jnp.broadcast_to(groups[i][:, 8 * b + c:8 * b + c + 1], (8, 128)) for i in range(b, R // 8)]
            for c in range(8)
        ]
        diagonal = jnp.zeros((8, 128), F32)
        for j in range(8):
            head = columns[j][0]
            pivot = jnp.broadcast_to(head[j:j + 1], (8, 128))
            inverse = 1.0 / pivot
            diagonal = jnp.where(rows == j, pivot, diagonal)
            factors = [column * inverse for column in columns[j]]
            factors[0] = jnp.where(rows > j, factors[0], 0.0)
            row = jnp.broadcast_to(groups[b][j:j + 1], (8, 128))
            for c in range(j + 1, 8):
                weight = jnp.broadcast_to(head[c:c + 1], (8, 128))
                columns[c] = [column - factor * weight for column, factor in zip(columns[c], factors)]
            for i in range(b, R // 8):
                groups[i] = groups[i] - factors[i - b] * row
        pivots.append(diagonal)
    return jnp.concatenate([(a * lax.rsqrt(d))[:, R:] for a, d in zip(groups, pivots)], axis=0)


def gram_matrix(rows):
    a1, a2, a3 = split3(rows)
    t = dot(jnp.concatenate([a1, a2, a3], 0), jnp.concatenate([a1, a2], 0), NT)
    t21, t31 = t[R:2 * R, :R], t[2 * R:, :R]
    return t[:R, :R] + ((t21 + t21.T) + (t[R:2 * R, R:] + (t31 + t31.T)))


def gram_kernel(own_ref, gram_ref):
    gram_ref[...] = gram_matrix(jnp.concatenate([own_ref[j] for j in range(BLOCKS)], axis=1))


def gram_half(own):
    return pl.pallas_call(
        gram_kernel,
        in_specs=[VMEM],
        out_specs=VMEM,
        out_shape=shape(R, R),
        compiler_params=LIMIT,
        cost_estimate=pl.CostEstimate(flops=10 ** 9, bytes_accessed=4 << 20, transcendentals=0),
        name="gram_half",
    )(own)


def first_round_kernel(core_ref, own_ref, other_ref, gram_ref, m_ref, b_ref, w_own_ref, w_other_ref, w_ref):
    core = core_ref[0]
    for j in range(BLOCKS):
        b_ref[:, lanes(core * HALF + j * 128, 128)] = own_ref[j]
        b_ref[:, lanes(HALF - core * HALF + j * 128, 128)] = other_ref[j]
    gram = gram_ref[...] + gram_matrix(jnp.concatenate([other_ref[j] for j in range(BLOCKS)], axis=1))
    b_ref[...] = dot_high(inverse_factor(gram), b_ref[...])
    total = jnp.zeros((R, KV), F32)
    for t in range(0, DW, LOAD):
        b1, b2 = split2(b_ref[:, t:t + LOAD])
        m1, m2 = split2(m_ref[t:t + LOAD, :])
        u = dot(jnp.concatenate([b1, b2], 0), m1)
        total = total + (u[:R] + (u[R:] + dot(b1, m2)))
    w_ref[...] = total
    mine = core * (R // 2)
    w_own_ref[...] = w_ref[lanes(mine, R // 2), :]
    w_other_ref[...] = w_ref[lanes(R // 2 - mine, R // 2), :]


def first_round(core, own, other, gram, moment):
    return pl.pallas_call(
        first_round_kernel,
        in_specs=[SMEM] + [VMEM] * 4,
        out_specs=[VMEM] * 3,
        out_shape=[shape(R, DW), shape(R // 2, KV), shape(R // 2, KV)],
        scratch_shapes=[pltpu.VMEM((R, KV), F32)],
        compiler_params=LIMIT,
        cost_estimate=pl.CostEstimate(flops=2 * 10 ** 9, bytes_accessed=6 << 20, transcendentals=0),
        name="first_round",
    )(core.reshape(1), own, other, gram, moment)


def second_round_kernel(b_ref, after_ref, p_hbm, p1_ref, p2_ref, l_ref, p_buf, sems):
    del after_ref
    rows = b_ref[...]
    factor = inverse_factor(gram_matrix(rows))
    l_ref[...] = factor
    f1, f2, f3 = split3(factor)
    f = jnp.concatenate([f1, f2, f3, f1, f2, f1], 1)
    copies = []
    for i in range(2):
        at = pl.ds(i * HALF, HALF)
        b1, b2, b3 = split3(b_ref[:, at])
        p = dot(f, jnp.concatenate([b1, b1, b1, b2, b2, b3], 0))
        p_buf[:, at] = p
        copies.append(pltpu.make_async_copy(p_buf.at[:, at], p_hbm.at[:, at], sems.at[i]))
        copies[-1].start()
        p1_ref[:, at], p2_ref[:, at] = split2(p)
    for copy in copies:
        copy.wait()


def second_round(basis, after):
    return pl.pallas_call(
        second_round_kernel,
        in_specs=[VMEM, pl.BlockSpec(memory_space=pl.ANY)],
        out_specs=[HBM, VMEM, VMEM, VMEM],
        out_shape=[shape(R, DW), shape(R, DW, dtype=BF), shape(R, DW, dtype=BF), shape(R, R)],
        scratch_shapes=[pltpu.VMEM((R, DW), F32), pltpu.SemaphoreType.DMA((2,))],
        compiler_params=LIMIT,
        cost_estimate=pl.CostEstimate(flops=10 ** 9, bytes_accessed=4 << 20, transcendentals=0),
        name="second_round",
    )(basis, after)


def update_kernel(core_ref, m_ref, p1_ref, p2_ref, l_ref, w_own_ref, w_other_ref, e_hbm, q_ref, w_ref, out, sems):
    mine = core_ref[0] * (R // 2)
    w_ref[lanes(mine, R // 2), :] = w_own_ref[...]
    w_ref[lanes(R // 2 - mine, R // 2), :] = w_other_ref[...]
    q = dot_high(l_ref[...], w_ref[...]) * (1.0 / (NZ * NY * NC))
    q_ref[...] = q
    q1, q2 = split2(q)
    q121 = jnp.concatenate([q1, q2, q1], 0)
    copies = []
    for j in range(DW // COLS):
        at = pl.ds(j * COLS, COLS)
        p1, p2 = p1_ref[:, at], p2_ref[:, at]
        out[at, :] = m_ref[at, :] - dot(jnp.concatenate([p1, p1, p2], 0), q121, TN)
        copies.append(pltpu.make_async_copy(out.at[at, :], e_hbm.at[at, :], sems.at[j]))
        copies[-1].start()
    for copy in copies:
        copy.wait()


def update(core, moment, p1, p2, factor, w_own, w_other):
    return pl.pallas_call(
        update_kernel,
        in_specs=[SMEM] + [VMEM] * 6,
        out_specs=[HBM, VMEM],
        out_shape=[shape(DW, KV), shape(R, KV)],
        scratch_shapes=[pltpu.VMEM((R, KV), F32), pltpu.VMEM((DW, KV), F32), pltpu.SemaphoreType.DMA((DW // COLS,))],
        compiler_params=LIMIT,
        name="update",
    )(core.reshape(1), moment, p1, p2, factor, w_own, w_other)


def sum_y_kernel(w_ref, s1_ref, s2_ref, s3_ref, after_ref, out_ref):
    del after_ref
    total = (w_ref[...] + s2_ref[...]) + (s1_ref[...] + s3_ref[...])
    for i in range(NZ):
        out_ref[i] = total


def sum_y(w, shifted, after):
    return pl.pallas_call(
        sum_y_kernel,
        in_specs=[VMEM] * 4 + [pl.BlockSpec(memory_space=pl.ANY)],
        out_specs=VMEM,
        out_shape=shape(NZ, R // 2, KV),
        compiler_params=SMALL,
        name="sum_y",
    )(w, *shifted, after)


def exchange(parts, axes):
    return lax.all_to_all(parts, axes, split_axis=0, concat_axis=0, tiled=True)


def sum_kernel(parts_ref, out_ref):
    total = parts_ref[0]
    for i in range(1, parts_ref.shape[0]):
        total = total + parts_ref[i]
    for i in range(out_ref.shape[0]):
        out_ref[i] = total


def sum_parts(parts, copies):
    return pl.pallas_call(
        sum_kernel,
        in_specs=[VMEM],
        out_specs=VMEM,
        out_shape=shape(copies, *parts.shape[1:]),
        compiler_params=SMALL,
        name="sum_parts",
    )(parts)


def swap(array):
    return lax.ppermute(array, "c", SWAP)


def shift_y(array, by):
    return lax.ppermute(array, "y", [(i, (i + by) % NY) for i in range(NY)])


def shards(inputs, out_grads, error_buffer, start_basis):
    core = lax.axis_index("c")
    arguments = (inputs, out_grads, error_buffer[0], start_basis.T)
    x, g, e, s_rows = [pltpu.with_memory_space_constraint(array, pltpu.HBM) for array in arguments]
    moment, p_other, s_rows = moment_and_other(core, x, g, e, s_rows)
    arrived = swap(p_other)
    p_own = p_own_half(core, moment, s_rows)

    parts = exchange(p_own + arrived, ("y", "x"))
    parts = exchange(sum_parts(parts, NZ), "z")
    own = exchange(sum_parts(parts, NY * NX), ("y", "x"))
    other = swap(own)
    basis, w_own, w_other = first_round(core, own, other, gram_half(own), moment)

    w = w_own + swap(w_other)
    shifted = [shift_y(w, by) for by in (1, 2, 3)]
    p_rows, p1, p2, factor = second_round(basis, w)
    w = sum_parts(exchange(sum_y(w, shifted, factor), "z"), 1)[0]
    error, q_rows = update(core, moment, p1, p2, factor, w, swap(w))
    return (p_rows.T, q_rows.T, error[None])


def solution(mesh):
    fine = Mesh(mesh.devices.reshape(NZ, NY, NC, NX), ("z", "y", "c", "x"))
    dp = ("z", "y", "c")
    in_specs = (P(dp, None), P(dp, "x"), P(dp, None, "x"), P("x", None))
    out_specs = (P(), P("x", None), P(dp, None, "x"))
    return jax.shard_map(shards, mesh=fine, in_specs=in_specs, out_specs=out_specs, check_vma=False)
```

```python
import jax
import jax.numpy as jnp
from jax import lax
from jax.experimental import pallas as pl
from jax.experimental.pallas import tpu as pltpu
from jax.sharding import Mesh, PartitionSpec as P

HIGH = lax.Precision.HIGHEST
NZ, NY, NC, NX = 8, 4, 2, 4
DW, KV, R, TOK = 4096, 256, 64, 384
HALF, BLOCKS = DW // 2, DW // 256
BF, F32 = jnp.bfloat16, jnp.float32
SWAP = [(0, 1), (1, 0)]
NN = (((1,), (0,)), ((), ()))
NT = (((1,), (1,)), ((), ()))
TN = (((0,), (0,)), ((), ()))
VMEM = pl.BlockSpec(memory_space=pltpu.VMEM)
SMEM = pl.BlockSpec(memory_space=pltpu.SMEM)
HBM = pl.BlockSpec(memory_space=pltpu.HBM)
LIMIT = pltpu.CompilerParams(vmem_limit_bytes=24 << 20)
SMALL = pltpu.CompilerParams(vmem_limit_bytes=8 << 20)


def shape(*dims, dtype=F32):
    return jax.ShapeDtypeStruct(dims, dtype)


def dot(a, b, dims=NN):
    return lax.dot_general(a, b, dims, preferred_element_type=F32)


def dot_high(a, b, dims=NN):
    return lax.dot_general(a, b, dims, precision=HIGH, preferred_element_type=F32)


def lanes(start, size):
    return pl.ds(pl.multiple_of(start, size), size)


def split2(x):
    high = x.astype(BF)
    return high, (x - high.astype(F32)).astype(BF)


def split3(x):
    high = x.astype(BF)
    rest = x - high.astype(F32)
    middle = rest.astype(BF)
    return high, middle, (rest - middle.astype(F32)).astype(BF)


COLS = 512
LOAD = 1024


def split_basis(s):
    s1, s2, s3 = split3(s)
    return jnp.concatenate([s1, s2, s3], 0), jnp.concatenate([s1, s2], 0), s1


def p_half(moment, basis, p_ref):
    m1, m2, m3 = split3(moment)
    s123, s12, s1 = split_basis(basis)
    t1, t2, t3 = dot(m1, s123, NT).T, dot(m2, s12, NT).T, dot(m3, s1, NT).T
    rows = (t1[2 * R:] + t2[R:] + t3) + (t1[R:2 * R] + t2[:R]) + t1[:R]
    for i in range(BLOCKS):
        p_ref[i] = rows[:, i * 128:(i + 1) * 128]


def moment_kernel(core_ref, x_hbm, g_hbm, e_hbm, s_hbm, m_ref, p_ref, s_ref, x_buf, g_buf, sems):
    other = HALF - core_ref[0] * HALF
    starts = [lax.rem(other + j * LOAD, DW) for j in range(DW // LOAD)]
    small = [
        pltpu.make_async_copy(g_hbm, g_buf, sems.at[0]),
        pltpu.make_async_copy(s_hbm, s_ref, sems.at[1]),
    ]
    large = [
        (
            pltpu.make_async_copy(x_hbm.at[:, lanes(start, LOAD)], x_buf.at[j], sems.at[2 + 2 * j]),
            pltpu.make_async_copy(e_hbm.at[lanes(start, LOAD), :], m_ref.at[lanes(start, LOAD), :], sems.at[3 + 2 * j]),
        )
        for j, start in enumerate(starts)
    ]
    for copy in small:
        copy.start()
    for pair in large:
        pair[0].start()
        pair[1].start()
    for copy in small:
        copy.wait()
    g = g_buf[...]
    for j, start in enumerate(starts):
        large[j][0].wait()
        large[j][1].wait()
        at = lanes(start, LOAD)
        m_ref[at, :] = dot(x_buf[j], g, TN) + m_ref[at, :]
        if (j + 1) * LOAD == HALF:
            p_half(m_ref[lanes(other, HALF), :], s_ref[...], p_ref)


def moment_and_other(core, x, g, e, s_rows):
    steps = DW // LOAD
    return pl.pallas_call(
        moment_kernel,
        in_specs=[SMEM, HBM, HBM, HBM, HBM],
        out_specs=[VMEM] * 3,
        out_shape=[shape(DW, KV), shape(BLOCKS, R, 128), shape(R, KV)],
        scratch_shapes=[
            pltpu.VMEM((steps, TOK, LOAD), BF),
            pltpu.VMEM((TOK, KV), BF),
            pltpu.SemaphoreType.DMA((2 + 2 * steps,)),
        ],
        compiler_params=LIMIT,
        name="moment",
    )(core.reshape(1), x, g, e, s_rows)


def own_kernel(core_ref, m_ref, s_ref, p_ref):
    p_half(m_ref[lanes(core_ref[0] * HALF, HALF), :], s_ref[...], p_ref)


def p_own_half(core, moment, s_rows):
    return pl.pallas_call(
        own_kernel,
        in_specs=[SMEM, VMEM, VMEM],
        out_specs=VMEM,
        out_shape=shape(BLOCKS, R, 128),
        compiler_params=LIMIT,
        cost_estimate=pl.CostEstimate(flops=10 ** 9, bytes_accessed=4 << 20, transcendentals=0),
        name="p_own",
    )(core.reshape(1), moment, s_rows)


def inverse_factor(gram):
    rows = lax.broadcasted_iota(jnp.int32, (8, 128), 0)
    lanes = lax.broadcasted_iota(jnp.int32, (8, 128), 1)
    zero = jnp.zeros((8, R), F32)
    groups = [
        jnp.where(lanes == rows + R + 8 * i, 1.0, jnp.concatenate([gram[8 * i:8 * i + 8], zero], axis=1))
        for i in range(R // 8)
    ]
    pivots = []
    for b in range(R // 8):
        columns = [
            [jnp.broadcast_to(groups[i][:, 8 * b + c:8 * b + c + 1], (8, 128)) for i in range(b, R // 8)]
            for c in range(8)
        ]
        diagonal = jnp.zeros((8, 128), F32)
        for j in range(8):
            head = columns[j][0]
            pivot = jnp.broadcast_to(head[j:j + 1], (8, 128))
            inverse = 1.0 / pivot
            diagonal = jnp.where(rows == j, pivot, diagonal)
            factors = [column * inverse for column in columns[j]]
            factors[0] = jnp.where(rows > j, factors[0], 0.0)
            row = jnp.broadcast_to(groups[b][j:j + 1], (8, 128))
            for c in range(j + 1, 8):
                weight = jnp.broadcast_to(head[c:c + 1], (8, 128))
                columns[c] = [column - factor * weight for column, factor in zip(columns[c], factors)]
            for i in range(b, R // 8):
                groups[i] = groups[i] - factors[i - b] * row
        pivots.append(diagonal)
    return jnp.concatenate([(a * lax.rsqrt(d))[:, R:] for a, d in zip(groups, pivots)], axis=0)


def gram_matrix(rows):
    a1, a2, a3 = split3(rows)
    t = dot(jnp.concatenate([a1, a2, a3], 0), jnp.concatenate([a1, a2], 0), NT)
    t21, t31 = t[R:2 * R, :R], t[2 * R:, :R]
    return t[:R, :R] + ((t21 + t21.T) + (t[R:2 * R, R:] + (t31 + t31.T)))


def wide(blocks_ref):
    return jnp.concatenate([blocks_ref[j] for j in range(BLOCKS)], axis=1)


def product(p, m):
    p1, p2, p3 = split3(p)
    m1, m2, m3 = split3(m)
    t1 = dot(jnp.concatenate([p1, p2, p3], 0), m1)
    t2 = dot(jnp.concatenate([p1, p2], 0), m2)
    return t1[:R] + ((t1[R:2 * R] + t2[:R]) + ((t1[2 * R:] + t2[R:]) + dot(p1, m3)))


def own_terms_kernel(core_ref, own_ref, m_ref, gram_ref, w_ref):
    own = wide(own_ref)
    gram_ref[...] = gram_matrix(own)
    w_ref[...] = product(own, m_ref[lanes(core_ref[0] * HALF, HALF), :])


def own_terms(core, own, moment):
    return pl.pallas_call(
        own_terms_kernel,
        in_specs=[SMEM, VMEM, VMEM],
        out_specs=[VMEM, VMEM],
        out_shape=[shape(R, R), shape(R, KV)],
        compiler_params=LIMIT,
        cost_estimate=pl.CostEstimate(flops=10 ** 9, bytes_accessed=4 << 20, transcendentals=0),
        name="own_terms",
    )(core.reshape(1), own, moment)


def other_term_kernel(core_ref, other_ref, m_ref, part_ref, w_own_ref, w_other_ref, w_ref):
    core = core_ref[0]
    w_ref[...] = part_ref[...] + product(wide(other_ref), m_ref[lanes(HALF - core * HALF, HALF), :])
    w_own_ref[...] = w_ref[lanes(core * (R // 2), R // 2), :]
    w_other_ref[...] = w_ref[lanes(R // 2 - core * (R // 2), R // 2), :]


def other_term(core, other, moment, part):
    return pl.pallas_call(
        other_term_kernel,
        in_specs=[SMEM, VMEM, VMEM, VMEM],
        out_specs=[VMEM, VMEM],
        out_shape=[shape(R // 2, KV), shape(R // 2, KV)],
        scratch_shapes=[pltpu.VMEM((R, KV), F32)],
        compiler_params=LIMIT,
        name="other_term",
    )(core.reshape(1), other, moment, part)


def first_round_kernel(core_ref, own_ref, other_ref, gram_ref, after_ref, b_ref, l_ref):
    del after_ref
    core = core_ref[0]
    for j in range(BLOCKS):
        b_ref[:, lanes(core * HALF + j * 128, 128)] = own_ref[j]
        b_ref[:, lanes(HALF - core * HALF + j * 128, 128)] = other_ref[j]
    factor = inverse_factor(gram_ref[...] + gram_matrix(wide(other_ref)))
    l_ref[...] = factor
    b_ref[...] = dot_high(factor, b_ref[...])


def first_round(core, own, other, gram, after):
    return pl.pallas_call(
        first_round_kernel,
        in_specs=[SMEM] + [VMEM] * 3 + [pl.BlockSpec(memory_space=pl.ANY)],
        out_specs=[VMEM] * 2,
        out_shape=[shape(R, DW), shape(R, R)],
        compiler_params=LIMIT,
        cost_estimate=pl.CostEstimate(flops=10 ** 9, bytes_accessed=4 << 20, transcendentals=0),
        name="first_round",
    )(core.reshape(1), own, other, gram, after)


def second_round_kernel(b_ref, after_ref, p_hbm, p1_ref, p2_ref, l_ref, p_buf, sems):
    del after_ref
    rows = b_ref[...]
    factor = inverse_factor(gram_matrix(rows))
    l_ref[...] = factor
    f1, f2, f3 = split3(factor)
    f = jnp.concatenate([f1, f2, f3, f1, f2, f1], 1)
    copies = []
    for i in range(2):
        at = pl.ds(i * HALF, HALF)
        b1, b2, b3 = split3(b_ref[:, at])
        p = dot(f, jnp.concatenate([b1, b1, b1, b2, b2, b3], 0))
        p_buf[:, at] = p
        copies.append(pltpu.make_async_copy(p_buf.at[:, at], p_hbm.at[:, at], sems.at[i]))
        copies[-1].start()
        p1_ref[:, at], p2_ref[:, at] = split2(p)
    for copy in copies:
        copy.wait()


def second_round(basis, after):
    return pl.pallas_call(
        second_round_kernel,
        in_specs=[VMEM, pl.BlockSpec(memory_space=pl.ANY)],
        out_specs=[HBM, VMEM, VMEM, VMEM],
        out_shape=[shape(R, DW), shape(R, DW, dtype=BF), shape(R, DW, dtype=BF), shape(R, R)],
        scratch_shapes=[pltpu.VMEM((R, DW), F32), pltpu.SemaphoreType.DMA((2,))],
        compiler_params=LIMIT,
        cost_estimate=pl.CostEstimate(flops=10 ** 9, bytes_accessed=4 << 20, transcendentals=0),
        name="second_round",
    )(basis, after)


def update_kernel(core_ref, m_ref, p1_ref, p2_ref, l1_ref, l2_ref, w_own_ref, w_other_ref, e_hbm, q_ref, w_ref, out, sems):
    mine = core_ref[0] * (R // 2)
    w_ref[lanes(mine, R // 2), :] = w_own_ref[...]
    w_ref[lanes(R // 2 - mine, R // 2), :] = w_other_ref[...]
    q = dot_high(l2_ref[...], dot_high(l1_ref[...], w_ref[...])) * (1.0 / (NZ * NY * NC))
    q_ref[...] = q
    q1, q2 = split2(q)
    q121 = jnp.concatenate([q1, q2, q1], 0)
    copies = []
    for j in range(DW // COLS):
        at = pl.ds(j * COLS, COLS)
        p1, p2 = p1_ref[:, at], p2_ref[:, at]
        out[at, :] = m_ref[at, :] - dot(jnp.concatenate([p1, p1, p2], 0), q121, TN)
        copies.append(pltpu.make_async_copy(out.at[at, :], e_hbm.at[at, :], sems.at[j]))
        copies[-1].start()
    for copy in copies:
        copy.wait()


def update(core, moment, p1, p2, factor1, factor2, w_own, w_other):
    return pl.pallas_call(
        update_kernel,
        in_specs=[SMEM] + [VMEM] * 7,
        out_specs=[HBM, VMEM],
        out_shape=[shape(DW, KV), shape(R, KV)],
        scratch_shapes=[pltpu.VMEM((R, KV), F32), pltpu.VMEM((DW, KV), F32), pltpu.SemaphoreType.DMA((DW // COLS,))],
        compiler_params=LIMIT,
        name="update",
    )(core.reshape(1), moment, p1, p2, factor1, factor2, w_own, w_other)


def pair_kernel(w_ref, arrived_ref, after_ref, out_ref):
    del after_ref
    total = w_ref[...] + arrived_ref[...]
    for i in range(out_ref.shape[0]):
        out_ref[i] = total


def sum_pair(w, arrived, after, copies):
    return pl.pallas_call(
        pair_kernel,
        in_specs=[VMEM] * 2 + [pl.BlockSpec(memory_space=pl.ANY)],
        out_specs=VMEM,
        out_shape=shape(copies, *w.shape),
        compiler_params=SMALL,
        name="sum_pair",
    )(w, arrived, after)


def exchange(parts, axes):
    return lax.all_to_all(parts, axes, split_axis=0, concat_axis=0, tiled=True)


def sum_kernel(parts_ref, out_ref):
    total = parts_ref[0]
    for i in range(1, parts_ref.shape[0]):
        total = total + parts_ref[i]
    for i in range(out_ref.shape[0]):
        out_ref[i] = total


def sum_parts(parts, copies):
    return pl.pallas_call(
        sum_kernel,
        in_specs=[VMEM],
        out_specs=VMEM,
        out_shape=shape(copies, *parts.shape[1:]),
        compiler_params=SMALL,
        name="sum_parts",
    )(parts)


def swap(array):
    return lax.ppermute(array, "c", SWAP)


def swap_y(array, distance):
    return lax.ppermute(array, "y", [(i, i ^ distance) for i in range(NY)])


def shards(inputs, out_grads, error_buffer, start_basis):
    core = lax.axis_index("c")
    arguments = (inputs, out_grads, error_buffer[0], start_basis.T)
    x, g, e, s_rows = [pltpu.with_memory_space_constraint(array, pltpu.HBM) for array in arguments]
    moment, p_other, s_rows = moment_and_other(core, x, g, e, s_rows)
    arrived = swap(p_other)
    p_own = p_own_half(core, moment, s_rows)

    parts = exchange(p_own + arrived, ("y", "x"))
    parts = exchange(sum_parts(parts, NZ), "z")
    own = exchange(sum_parts(parts, NY * NX), ("y", "x"))
    other = swap(own)
    gram, part = own_terms(core, own, moment)
    w_own, w_other = other_term(core, other, moment, part)

    w = w_own + swap(w_other)
    arrived = swap_y(w, 1)
    basis, factor1 = first_round(core, own, other, gram, w)
    w = sum_pair(w, arrived, factor1, 1)[0]
    arrived = swap_y(w, 2)
    p_rows, p1, p2, factor2 = second_round(basis, w)
    w = sum_parts(exchange(sum_pair(w, arrived, factor2, NZ), "z"), 1)[0]
    error, q_rows = update(core, moment, p1, p2, factor1, factor2, w, swap(w))
    return (p_rows.T, q_rows.T, error[None])


def solution(mesh):
    fine = Mesh(mesh.devices.reshape(NZ, NY, NC, NX), ("z", "y", "c", "x"))
    dp = ("z", "y", "c")
    in_specs = (P(dp, None), P(dp, "x"), P(dp, None, "x"), P("x", None))
    out_specs = (P(), P("x", None), P(dp, None, "x"))
    return jax.shard_map(shards, mesh=fine, in_specs=in_specs, out_specs=out_specs, check_vma=False)
```

```python
import jax
import jax.numpy as jnp
from jax import lax
from jax.experimental import pallas as pl
from jax.experimental.pallas import tpu as pltpu
from jax.sharding import Mesh, PartitionSpec as P

HIGH = lax.Precision.HIGHEST
NZ, NY, NC, NX = 8, 4, 2, 4
DW, KV, R, TOK = 4096, 256, 64, 384
HALF, BLOCKS = DW // 2, DW // 256
BF, F32 = jnp.bfloat16, jnp.float32
SWAP = [(0, 1), (1, 0)]
NN = (((1,), (0,)), ((), ()))
NT = (((1,), (1,)), ((), ()))
TN = (((0,), (0,)), ((), ()))
VMEM = pl.BlockSpec(memory_space=pltpu.VMEM)
SMEM = pl.BlockSpec(memory_space=pltpu.SMEM)
HBM = pl.BlockSpec(memory_space=pltpu.HBM)
ANY = pl.BlockSpec(memory_space=pl.ANY)
BESIDE = pl.CostEstimate(flops=10 ** 9, bytes_accessed=4 << 20, transcendentals=0)
LIMIT = pltpu.CompilerParams(vmem_limit_bytes=24 << 20)
SMALL = pltpu.CompilerParams(vmem_limit_bytes=8 << 20)


def shape(*dims, dtype=F32):
    return jax.ShapeDtypeStruct(dims, dtype)


def dot(a, b, dims=NN):
    return lax.dot_general(a, b, dims, preferred_element_type=F32)


def dot_high(a, b, dims=NN):
    return lax.dot_general(a, b, dims, precision=HIGH, preferred_element_type=F32)


def lanes(start, size):
    return pl.ds(pl.multiple_of(start, size), size)


def split2(x):
    high = x.astype(BF)
    return high, (x - high.astype(F32)).astype(BF)


def split3(x):
    high = x.astype(BF)
    rest = x - high.astype(F32)
    middle = rest.astype(BF)
    return high, middle, (rest - middle.astype(F32)).astype(BF)


COLS = 512
LOAD = 1024


def split_basis(s):
    s1, s2, s3 = split3(s)
    return jnp.concatenate([s1, s2, s3], 0), jnp.concatenate([s1, s2], 0), s1


def p_half(moment, basis, p_ref):
    m1, m2, m3 = split3(moment)
    s123, s12, s1 = split_basis(basis)
    t1, t2, t3 = dot(m1, s123, NT).T, dot(m2, s12, NT).T, dot(m3, s1, NT).T
    rows = (t1[2 * R:] + t2[R:] + t3) + (t1[R:2 * R] + t2[:R]) + t1[:R]
    for i in range(BLOCKS):
        p_ref[i] = rows[:, i * 128:(i + 1) * 128]


def moment_kernel(core_ref, x_hbm, g_hbm, e_hbm, s_hbm, m_ref, p_ref, s_ref, x_buf, g_buf, sems):
    other = HALF - core_ref[0] * HALF
    starts = [lax.rem(other + j * LOAD, DW) for j in range(DW // LOAD)]
    small = [
        pltpu.make_async_copy(g_hbm, g_buf, sems.at[0]),
        pltpu.make_async_copy(s_hbm, s_ref, sems.at[1]),
    ]
    large = [
        (
            pltpu.make_async_copy(x_hbm.at[:, lanes(start, LOAD)], x_buf.at[j], sems.at[2 + 2 * j]),
            pltpu.make_async_copy(e_hbm.at[lanes(start, LOAD), :], m_ref.at[lanes(start, LOAD), :], sems.at[3 + 2 * j]),
        )
        for j, start in enumerate(starts)
    ]
    for copy in small:
        copy.start()
    for pair in large:
        pair[0].start()
        pair[1].start()
    for copy in small:
        copy.wait()
    g = g_buf[...]
    for j, start in enumerate(starts):
        large[j][0].wait()
        large[j][1].wait()
        at = lanes(start, LOAD)
        m_ref[at, :] = dot(x_buf[j], g, TN) + m_ref[at, :]
        if (j + 1) * LOAD == HALF:
            p_half(m_ref[lanes(other, HALF), :], s_ref[...], p_ref)


def moment_and_other(core, x, g, e, s_rows):
    steps = DW // LOAD
    return pl.pallas_call(
        moment_kernel,
        in_specs=[SMEM, HBM, HBM, HBM, HBM],
        out_specs=[VMEM] * 3,
        out_shape=[shape(DW, KV), shape(BLOCKS, R, 128), shape(R, KV)],
        scratch_shapes=[
            pltpu.VMEM((steps, TOK, LOAD), BF),
            pltpu.VMEM((TOK, KV), BF),
            pltpu.SemaphoreType.DMA((2 + 2 * steps,)),
        ],
        compiler_params=LIMIT,
        name="moment",
    )(core.reshape(1), x, g, e, s_rows)


def own_kernel(core_ref, m_ref, s_ref, p_ref):
    p_half(m_ref[lanes(core_ref[0] * HALF, HALF), :], s_ref[...], p_ref)


def p_own_half(core, moment, s_rows):
    return pl.pallas_call(
        own_kernel,
        in_specs=[SMEM, VMEM, VMEM],
        out_specs=VMEM,
        out_shape=shape(BLOCKS, R, 128),
        compiler_params=LIMIT,
        cost_estimate=BESIDE,
        name="p_own",
    )(core.reshape(1), moment, s_rows)


def inverse_factor(gram):
    rows = lax.broadcasted_iota(jnp.int32, (8, 128), 0)
    lanes = lax.broadcasted_iota(jnp.int32, (8, 128), 1)
    zero = jnp.zeros((8, R), F32)
    groups = [
        jnp.where(lanes == rows + R + 8 * i, 1.0, jnp.concatenate([gram[8 * i:8 * i + 8], zero], axis=1))
        for i in range(R // 8)
    ]
    pivots = []
    for b in range(R // 8):
        columns = [
            [jnp.broadcast_to(groups[i][:, 8 * b + c:8 * b + c + 1], (8, 128)) for i in range(b, R // 8)]
            for c in range(8)
        ]
        diagonal = jnp.zeros((8, 128), F32)
        for j in range(8):
            head = columns[j][0]
            pivot = jnp.broadcast_to(head[j:j + 1], (8, 128))
            inverse = 1.0 / pivot
            diagonal = jnp.where(rows == j, pivot, diagonal)
            factors = [column * inverse for column in columns[j]]
            factors[0] = jnp.where(rows > j, factors[0], 0.0)
            row = jnp.broadcast_to(groups[b][j:j + 1], (8, 128))
            for c in range(j + 1, 8):
                weight = jnp.broadcast_to(head[c:c + 1], (8, 128))
                columns[c] = [column - factor * weight for column, factor in zip(columns[c], factors)]
            for i in range(b, R // 8):
                groups[i] = groups[i] - factors[i - b] * row
        pivots.append(diagonal)
    return jnp.concatenate([(a * lax.rsqrt(d))[:, R:] for a, d in zip(groups, pivots)], axis=0)


def gram_matrix(rows):
    a1, a2, a3 = split3(rows)
    t = dot(jnp.concatenate([a1, a2, a3], 0), jnp.concatenate([a1, a2], 0), NT)
    t21, t31 = t[R:2 * R, :R], t[2 * R:, :R]
    return t[:R, :R] + ((t21 + t21.T) + (t[R:2 * R, R:] + (t31 + t31.T)))


def wide(blocks_ref):
    return jnp.concatenate([blocks_ref[j] for j in range(BLOCKS)], axis=1)


def product(p, m):
    p1, p2, p3 = split3(p)
    m1, m2, m3 = split3(m)
    t1 = dot(jnp.concatenate([p1, p2, p3], 0), m1)
    t2 = dot(jnp.concatenate([p1, p2], 0), m2)
    return t1[:R] + ((t1[R:2 * R] + t2[:R]) + ((t1[2 * R:] + t2[R:]) + dot(p1, m3)))


def own_terms_kernel(core_ref, own_ref, m_ref, gram_ref, w_ref):
    own = wide(own_ref)
    gram_ref[...] = gram_matrix(own)
    w_ref[...] = product(own, m_ref[lanes(core_ref[0] * HALF, HALF), :])


def own_terms(core, own, moment):
    return pl.pallas_call(
        own_terms_kernel,
        in_specs=[SMEM, VMEM, VMEM],
        out_specs=[VMEM, VMEM],
        out_shape=[shape(R, R), shape(R, KV)],
        compiler_params=LIMIT,
        cost_estimate=BESIDE,
        name="own_terms",
    )(core.reshape(1), own, moment)


def other_term_kernel(core_ref, other_ref, m_ref, part_ref, w_own_ref, w_other_ref, w_ref):
    core = core_ref[0]
    w_ref[...] = part_ref[...] + product(wide(other_ref), m_ref[lanes(HALF - core * HALF, HALF), :])
    w_own_ref[...] = w_ref[lanes(core * (R // 2), R // 2), :]
    w_other_ref[...] = w_ref[lanes(R // 2 - core * (R // 2), R // 2), :]


def other_term(core, other, moment, part):
    return pl.pallas_call(
        other_term_kernel,
        in_specs=[SMEM, VMEM, VMEM, VMEM],
        out_specs=[VMEM, VMEM],
        out_shape=[shape(R // 2, KV), shape(R // 2, KV)],
        scratch_shapes=[pltpu.VMEM((R, KV), F32)],
        compiler_params=LIMIT,
        name="other_term",
    )(core.reshape(1), other, moment, part)


def other_gram_kernel(other_ref, part_ref, after_ref, gram_ref):
    del after_ref
    gram_ref[...] = part_ref[...] + gram_matrix(wide(other_ref))


def other_gram(other, part, after):
    return pl.pallas_call(
        other_gram_kernel,
        in_specs=[VMEM, VMEM, ANY],
        out_specs=VMEM,
        out_shape=shape(R, R),
        compiler_params=LIMIT,
        cost_estimate=BESIDE,
        name="other_gram",
    )(other, part, after)


def first_round_kernel(core_ref, own_ref, other_ref, gram_ref, after_ref, b_ref, l_ref):
    del after_ref
    core = core_ref[0]
    for j in range(BLOCKS):
        b_ref[:, lanes(core * HALF + j * 128, 128)] = own_ref[j]
        b_ref[:, lanes(HALF - core * HALF + j * 128, 128)] = other_ref[j]
    factor = inverse_factor(gram_ref[...])
    l_ref[...] = factor
    b_ref[...] = dot_high(factor, b_ref[...])


def first_round(core, own, other, gram, after):
    return pl.pallas_call(
        first_round_kernel,
        in_specs=[SMEM] + [VMEM] * 3 + [ANY],
        out_specs=[VMEM] * 2,
        out_shape=[shape(R, DW), shape(R, R)],
        compiler_params=LIMIT,
        cost_estimate=BESIDE,
        name="first_round",
    )(core.reshape(1), own, other, gram, after)


def second_round_kernel(b_ref, l1_ref, after_ref, l2_ref, f_ref):
    del after_ref
    factor = inverse_factor(gram_matrix(b_ref[...]))
    l2_ref[...] = factor
    both = dot_high(factor, l1_ref[...]) * (1.0 / (NZ * NY * NC))
    f_ref[:R, :] = both
    f_ref[R:, :] = dot_high(factor, both, TN)


def second_round(basis, factor, after):
    return pl.pallas_call(
        second_round_kernel,
        in_specs=[VMEM, VMEM, ANY],
        out_specs=[VMEM, VMEM],
        out_shape=[shape(R, R), shape(2 * R, R)],
        compiler_params=LIMIT,
        cost_estimate=BESIDE,
        name="second_round",
    )(basis, factor, after)


def finish_kernel(b_ref, l_ref, after_ref, p_hbm, token_ref, p_buf, sems):
    del after_ref
    f1, f2, f3 = split3(l_ref[...])
    f = jnp.concatenate([f1, f2, f3, f1, f2, f1], 1)
    copies = []
    for i in range(DW // LOAD):
        at = pl.ds(i * LOAD, LOAD)
        b1, b2, b3 = split3(b_ref[:, at])
        p_buf[:, at] = dot(f, jnp.concatenate([b1, b1, b1, b2, b2, b3], 0))
        copies.append(pltpu.make_async_copy(p_buf.at[:, at], p_hbm.at[:, at], sems.at[i]))
        copies[-1].start()
    token_ref[...] = jnp.zeros_like(token_ref)
    for copy in copies:
        copy.wait()


def finish(basis, factor, after):
    return pl.pallas_call(
        finish_kernel,
        in_specs=[VMEM, VMEM, ANY],
        out_specs=[HBM, VMEM],
        out_shape=[shape(R, DW), shape(8, 128)],
        scratch_shapes=[pltpu.VMEM((R, DW), F32), pltpu.SemaphoreType.DMA((DW // LOAD,))],
        compiler_params=LIMIT,
        cost_estimate=BESIDE,
        name="finish",
    )(basis, factor, after)


def update_kernel(core_ref, m_ref, b_ref, f_ref, w_own_ref, w_other_ref, after_ref, e_hbm, q_ref, w_ref, out, sems):
    del after_ref
    mine = core_ref[0] * (R // 2)
    w_ref[lanes(mine, R // 2), :] = w_own_ref[...]
    w_ref[lanes(R // 2 - mine, R // 2), :] = w_other_ref[...]
    qr = dot_high(f_ref[...], w_ref[...])
    q_ref[...] = qr[:R]
    r1, r2 = split2(qr[R:])
    r121 = jnp.concatenate([r1, r2, r1], 0)
    copies = []
    for j in range(DW // COLS):
        at = pl.ds(j * COLS, COLS)
        b1, b2 = split2(b_ref[:, at])
        out[at, :] = m_ref[at, :] - dot(jnp.concatenate([b1, b1, b2], 0), r121, TN)
        copies.append(pltpu.make_async_copy(out.at[at, :], e_hbm.at[at, :], sems.at[j]))
        copies[-1].start()
    for copy in copies:
        copy.wait()


def update(core, moment, basis, factors, w_own, w_other, after):
    return pl.pallas_call(
        update_kernel,
        in_specs=[SMEM] + [VMEM] * 6,
        out_specs=[HBM, VMEM],
        out_shape=[shape(DW, KV), shape(R, KV)],
        scratch_shapes=[pltpu.VMEM((R, KV), F32), pltpu.VMEM((DW, KV), F32), pltpu.SemaphoreType.DMA((DW // COLS,))],
        compiler_params=LIMIT,
        name="update",
    )(core.reshape(1), moment, basis, factors, w_own, w_other, after)


def pair_kernel(w_ref, arrived_ref, after_ref, out_ref):
    del after_ref
    total = w_ref[...] + arrived_ref[...]
    for i in range(out_ref.shape[0]):
        out_ref[i] = total


def sum_pair(w, arrived, after, copies):
    return pl.pallas_call(
        pair_kernel,
        in_specs=[VMEM] * 2 + [ANY],
        out_specs=VMEM,
        out_shape=shape(copies, *w.shape),
        compiler_params=SMALL,
        name="sum_pair",
    )(w, arrived, after)


def exchange(parts, axes):
    return lax.all_to_all(parts, axes, split_axis=0, concat_axis=0, tiled=True)


def sum_kernel(parts_ref, out_ref):
    total = parts_ref[0]
    for i in range(1, parts_ref.shape[0]):
        total = total + parts_ref[i]
    for i in range(out_ref.shape[0]):
        out_ref[i] = total


def sum_parts(parts, copies):
    return pl.pallas_call(
        sum_kernel,
        in_specs=[VMEM],
        out_specs=VMEM,
        out_shape=shape(copies, *parts.shape[1:]),
        compiler_params=SMALL,
        name="sum_parts",
    )(parts)


def swap(array):
    return lax.ppermute(array, "c", SWAP)


def swap_y(array, distance):
    return lax.ppermute(array, "y", [(i, i ^ distance) for i in range(NY)])


def shards(inputs, out_grads, error_buffer, start_basis):
    core = lax.axis_index("c")
    arguments = (inputs, out_grads, error_buffer[0], start_basis.T)
    x, g, e, s_rows = [pltpu.with_memory_space_constraint(array, pltpu.HBM) for array in arguments]
    moment, p_other, s_rows = moment_and_other(core, x, g, e, s_rows)
    arrived = swap(p_other)
    p_own = p_own_half(core, moment, s_rows)

    parts = exchange(p_own + arrived, ("y", "x"))
    parts = exchange(sum_parts(parts, NZ), "z")
    own = exchange(sum_parts(parts, NY * NX), ("y", "x"))
    other = swap(own)
    gram, part = own_terms(core, own, moment)
    w_own, w_other = other_term(core, other, moment, part)

    w = w_own + swap(w_other)
    gram = other_gram(other, gram, w_own)
    arrived = swap_y(w, 1)
    basis, factor1 = first_round(core, own, other, gram, w)
    w = sum_pair(w, arrived, factor1, 1)[0]
    arrived = swap_y(w, 2)
    factor2, factors = second_round(basis, factor1, w)
    w = sum_parts(exchange(sum_pair(w, arrived, factor2, NZ), "z"), 1)[0]
    p_rows, token = finish(basis, factor2, w)
    error, q_rows = update(core, moment, basis, factors, w, swap(w), token)
    return (p_rows.T, q_rows.T, error[None])


def solution(mesh):
    fine = Mesh(mesh.devices.reshape(NZ, NY, NC, NX), ("z", "y", "c", "x"))
    dp = ("z", "y", "c")
    in_specs = (P(dp, None), P(dp, "x"), P(dp, None, "x"), P("x", None))
    out_specs = (P(), P("x", None), P(dp, None, "x"))
    return jax.shard_map(shards, mesh=fine, in_specs=in_specs, out_specs=out_specs, check_vma=False)
```

```python
import jax
import jax.numpy as jnp
from jax import lax
from jax.experimental import pallas as pl
from jax.experimental.pallas import tpu as pltpu
from jax.sharding import Mesh, PartitionSpec as P

HIGH = lax.Precision.HIGHEST
NZ, NY, NC, NX = 8, 4, 2, 4
DW, KV, R, TOK = 4096, 256, 64, 384
HALF, BLOCKS = DW // 2, DW // 256
BF, F32 = jnp.bfloat16, jnp.float32
SWAP = [(0, 1), (1, 0)]
NN = (((1,), (0,)), ((), ()))
NT = (((1,), (1,)), ((), ()))
TN = (((0,), (0,)), ((), ()))
VMEM = pl.BlockSpec(memory_space=pltpu.VMEM)
SMEM = pl.BlockSpec(memory_space=pltpu.SMEM)
HBM = pl.BlockSpec(memory_space=pltpu.HBM)
ANY = pl.BlockSpec(memory_space=pl.ANY)
BESIDE = pl.CostEstimate(flops=10 ** 9, bytes_accessed=4 << 20, transcendentals=0)
LIMIT = pltpu.CompilerParams(vmem_limit_bytes=24 << 20)
SMALL = pltpu.CompilerParams(vmem_limit_bytes=8 << 20)


def shape(*dims, dtype=F32):
    return jax.ShapeDtypeStruct(dims, dtype)


def dot(a, b, dims=NN):
    return lax.dot_general(a, b, dims, preferred_element_type=F32)


def dot_high(a, b, dims=NN):
    return lax.dot_general(a, b, dims, precision=HIGH, preferred_element_type=F32)


def lanes(start, size):
    return pl.ds(pl.multiple_of(start, size), size)


def split2(x):
    high = x.astype(BF)
    return high, (x - high.astype(F32)).astype(BF)


def split3(x):
    high = x.astype(BF)
    rest = x - high.astype(F32)
    middle = rest.astype(BF)
    return high, middle, (rest - middle.astype(F32)).astype(BF)


COLS = 512
LOAD = 1024


def p_half(moment, basis, p_ref):
    s1, s2, s3 = split3(basis)
    none = jnp.zeros_like(s1)
    orders = (s3, s2, s1), (s2, s1, none), (s1, none, none)
    weights = jnp.concatenate([jnp.concatenate(order, 1) for order in orders], 0)
    t = dot(jnp.concatenate(split3(moment), 1), weights, NT).T
    rows = (t[:R] + t[R:2 * R]) + t[2 * R:]
    for i in range(BLOCKS):
        p_ref[i] = rows[:, i * 128:(i + 1) * 128]


def moment_kernel(core_ref, x_hbm, g_hbm, e_hbm, s_hbm, m_ref, p_ref, e_ref, x_ref, g_ref, s_ref, x_buf, sems):
    core = core_ref[0]
    steps = HALF // LOAD
    copies = [pltpu.make_async_copy(g_hbm, g_ref, sems.at[0]), pltpu.make_async_copy(s_hbm, s_ref, sems.at[1])]
    for base, x_to, e_to in ((HALF - core * HALF, x_buf, m_ref), (core * HALF, x_ref, e_ref)):
        for j in range(steps):
            at, to = lanes(base + j * LOAD, LOAD), pl.ds(j * LOAD, LOAD)
            copies.append(pltpu.make_async_copy(x_hbm.at[:, at], x_to.at[j], sems.at[len(copies)]))
            copies.append(pltpu.make_async_copy(e_hbm.at[at, :], e_to.at[to, :], sems.at[len(copies)]))
    for copy in copies:
        copy.start()
    copies[0].wait()
    copies[1].wait()
    g = g_ref[...]
    for j in range(steps):
        copies[2 + 2 * j].wait()
        copies[3 + 2 * j].wait()
        at = pl.ds(j * LOAD, LOAD)
        m_ref[at, :] = dot(x_buf[j], g, TN) + m_ref[at, :]
    p_half(m_ref[...], s_ref[...], p_ref)
    for copy in copies[2 + 2 * steps:]:
        copy.wait()


def moment_of_other(core, x, g, e, s_rows):
    steps = HALF // LOAD
    return pl.pallas_call(
        moment_kernel,
        in_specs=[SMEM, HBM, HBM, HBM, HBM],
        out_specs=[VMEM] * 6,
        out_shape=[
            shape(HALF, KV),
            shape(BLOCKS, R, 128),
            shape(HALF, KV),
            shape(steps, TOK, LOAD, dtype=BF),
            shape(TOK, KV, dtype=BF),
            shape(R, KV),
        ],
        scratch_shapes=[pltpu.VMEM((steps, TOK, LOAD), BF), pltpu.SemaphoreType.DMA((2 + 4 * steps,))],
        compiler_params=LIMIT,
        name="moment_other",
    )(core.reshape(1), x, g, e, s_rows)


def own_kernel(x_ref, g_ref, e_ref, s_ref, m_ref, p_ref):
    g = g_ref[...]
    for j in range(HALF // LOAD):
        at = pl.ds(j * LOAD, LOAD)
        m_ref[at, :] = dot(x_ref[j], g, TN) + e_ref[at, :]
    p_half(m_ref[...], s_ref[...], p_ref)


def moment_of_own(x, g, e, s_rows):
    return pl.pallas_call(
        own_kernel,
        in_specs=[VMEM] * 4,
        out_specs=[VMEM] * 2,
        out_shape=[shape(HALF, KV), shape(BLOCKS, R, 128)],
        compiler_params=LIMIT,
        cost_estimate=BESIDE,
        name="moment_own",
    )(x, g, e, s_rows)


def inverse_factor(gram):
    rows = lax.broadcasted_iota(jnp.int32, (8, 128), 0)
    lanes = lax.broadcasted_iota(jnp.int32, (8, 128), 1)
    zero = jnp.zeros((8, R), F32)
    groups = [
        jnp.where(lanes == rows + R + 8 * i, 1.0, jnp.concatenate([gram[8 * i:8 * i + 8], zero], axis=1))
        for i in range(R // 8)
    ]
    pivots = []
    for b in range(R // 8):
        columns = [
            [jnp.broadcast_to(groups[i][:, 8 * b + c:8 * b + c + 1], (8, 128)) for i in range(b, R // 8)]
            for c in range(8)
        ]
        diagonal = jnp.zeros((8, 128), F32)
        for j in range(8):
            head = columns[j][0]
            pivot = jnp.broadcast_to(head[j:j + 1], (8, 128))
            inverse = 1.0 / pivot
            diagonal = jnp.where(rows == j, pivot, diagonal)
            factors = [column * inverse for column in columns[j]]
            factors[0] = jnp.where(rows > j, factors[0], 0.0)
            row = jnp.broadcast_to(groups[b][j:j + 1], (8, 128))
            for c in range(j + 1, 8):
                weight = jnp.broadcast_to(head[c:c + 1], (8, 128))
                columns[c] = [column - factor * weight for column, factor in zip(columns[c], factors)]
            for i in range(b, R // 8):
                groups[i] = groups[i] - factors[i - b] * row
        pivots.append(diagonal)
    return jnp.concatenate([(a * lax.rsqrt(d))[:, R:] for a, d in zip(groups, pivots)], axis=0)


def gram_matrix(rows):
    a1, a2, a3 = split3(rows)
    t = dot(jnp.concatenate([a1, a2, a3], 0), jnp.concatenate([a1, a2], 0), NT)
    t21, t31 = t[R:2 * R, :R], t[2 * R:, :R]
    return t[:R, :R] + ((t21 + t21.T) + (t[R:2 * R, R:] + (t31 + t31.T)))


def wide(blocks_ref):
    return jnp.concatenate([blocks_ref[j] for j in range(BLOCKS)], axis=1)


def product(p, m):
    p1, p2, p3 = split3(p)
    m1, m2, m3 = split3(m)
    t1 = dot(jnp.concatenate([p1, p2, p3], 0), m1)
    t2 = dot(jnp.concatenate([p1, p2], 0), m2)
    return t1[:R] + ((t1[R:2 * R] + t2[:R]) + ((t1[2 * R:] + t2[R:]) + dot(p1, m3)))


def own_terms_kernel(core_ref, own_ref, m_ref, arrived_ref, gram_ref, w_own_ref, w_other_ref, w_ref):
    own = wide(own_ref)
    w_ref[...] = product(own, m_ref[...] + arrived_ref[...])
    mine = core_ref[0] * (R // 2)
    w_own_ref[...] = w_ref[lanes(mine, R // 2), :]
    w_other_ref[...] = w_ref[lanes(R // 2 - mine, R // 2), :]
    gram_ref[...] = gram_matrix(own)


def own_terms(core, own, moment, arrived):
    return pl.pallas_call(
        own_terms_kernel,
        in_specs=[SMEM] + [VMEM] * 3,
        out_specs=[VMEM] * 3,
        out_shape=[shape(R, R), shape(R // 2, KV), shape(R // 2, KV)],
        scratch_shapes=[pltpu.VMEM((R, KV), F32)],
        compiler_params=LIMIT,
        cost_estimate=BESIDE,
        name="own_terms",
    )(core.reshape(1), own, moment, arrived)


def other_gram_kernel(other_ref, part_ref, after_ref, gram_ref):
    del after_ref
    gram_ref[...] = part_ref[...] + gram_matrix(wide(other_ref))


def other_gram(other, part, after):
    return pl.pallas_call(
        other_gram_kernel,
        in_specs=[VMEM, VMEM, ANY],
        out_specs=VMEM,
        out_shape=shape(R, R),
        compiler_params=LIMIT,
        cost_estimate=BESIDE,
        name="other_gram",
    )(other, part, after)


def first_round_kernel(core_ref, own_ref, other_ref, gram_ref, after_ref, b_ref, l_ref):
    del after_ref
    core = core_ref[0]
    for j in range(BLOCKS):
        b_ref[:, lanes(core * HALF + j * 128, 128)] = own_ref[j]
        b_ref[:, lanes(HALF - core * HALF + j * 128, 128)] = other_ref[j]
    factor = inverse_factor(gram_ref[...])
    l_ref[...] = factor
    b_ref[...] = dot_high(factor, b_ref[...])


def first_round(core, own, other, gram, after):
    return pl.pallas_call(
        first_round_kernel,
        in_specs=[SMEM] + [VMEM] * 3 + [ANY],
        out_specs=[VMEM] * 2,
        out_shape=[shape(R, DW), shape(R, R)],
        compiler_params=LIMIT,
        cost_estimate=BESIDE,
        name="first_round",
    )(core.reshape(1), own, other, gram, after)


def second_round_kernel(b_ref, l1_ref, after_ref, l2_ref, f_ref):
    del after_ref
    factor = inverse_factor(gram_matrix(b_ref[...]))
    l2_ref[...] = factor
    both = dot_high(factor, l1_ref[...]) * (1.0 / (NZ * NY * NC))
    f_ref[:R, :] = both
    f_ref[R:, :] = dot_high(factor, both, TN)


def second_round(basis, factor, after):
    return pl.pallas_call(
        second_round_kernel,
        in_specs=[VMEM, VMEM, ANY],
        out_specs=[VMEM, VMEM],
        out_shape=[shape(R, R), shape(2 * R, R)],
        compiler_params=LIMIT,
        cost_estimate=BESIDE,
        name="second_round",
    )(basis, factor, after)


def finish_kernel(b_ref, l_ref, after_ref, p_ref):
    del after_ref
    f1, f2, f3 = split3(l_ref[...])
    b1, b2, b3 = split3(b_ref[...])
    f = jnp.concatenate([f1, f2, f3, f1, f2, f1], 1)
    p_ref[...] = dot(f, jnp.concatenate([b1, b1, b1, b2, b2, b3], 0))


def finish(basis, factor, after):
    return pl.pallas_call(
        finish_kernel,
        in_specs=[VMEM, VMEM, ANY],
        out_specs=VMEM,
        out_shape=shape(R, DW),
        compiler_params=LIMIT,
        cost_estimate=BESIDE,
        name="finish",
    )(basis, factor, after)


def update_kernel(core_ref, m_own_ref, m_other_ref, b_ref, f_ref, w_own_ref, w_other_ref, p_ref, e_hbm, q_ref, p_hbm, w_ref, out, sems):
    core = core_ref[0]
    copies = [pltpu.make_async_copy(p_ref, p_hbm, sems.at[0])]
    copies[0].start()
    w_ref[lanes(core * (R // 2), R // 2), :] = w_own_ref[...]
    w_ref[lanes(R // 2 - core * (R // 2), R // 2), :] = w_other_ref[...]
    qr = dot_high(f_ref[...], w_ref[...])
    q_ref[...] = qr[:R]
    r1, r2 = split2(qr[R:])
    r121 = jnp.concatenate([r1, r2, r1], 0)
    for part, (base, m_ref) in enumerate(((core * HALF, m_own_ref), (HALF - core * HALF, m_other_ref))):
        for t in range(0, HALF, COLS):
            at, here = lanes(base + t, COLS), pl.ds(part * HALF + t, COLS)
            b1, b2 = split2(b_ref[:, at])
            out[here, :] = m_ref[t:t + COLS, :] - dot(jnp.concatenate([b1, b1, b2], 0), r121, TN)
            copies.append(pltpu.make_async_copy(out.at[here, :], e_hbm.at[at, :], sems.at[len(copies)]))
            copies[-1].start()
    for copy in copies:
        copy.wait()


def update(core, m_own, m_other, basis, factors, w_own, w_other, p_rows):
    return pl.pallas_call(
        update_kernel,
        in_specs=[SMEM] + [VMEM] * 7,
        out_specs=[HBM, VMEM, HBM],
        out_shape=[shape(DW, KV), shape(R, KV), shape(R, DW)],
        scratch_shapes=[
            pltpu.VMEM((R, KV), F32),
            pltpu.VMEM((DW, KV), F32),
            pltpu.SemaphoreType.DMA((1 + DW // COLS,)),
        ],
        compiler_params=LIMIT,
        name="update",
    )(core.reshape(1), m_own, m_other, basis, factors, w_own, w_other, p_rows)


def pair_kernel(w_ref, arrived_ref, after_ref, out_ref):
    del after_ref
    total = w_ref[...] + arrived_ref[...]
    for i in range(out_ref.shape[0]):
        out_ref[i] = total


def sum_pair(w, arrived, after, copies):
    return pl.pallas_call(
        pair_kernel,
        in_specs=[VMEM] * 2 + [ANY],
        out_specs=VMEM,
        out_shape=shape(copies, *w.shape),
        compiler_params=SMALL,
        name="sum_pair",
    )(w, arrived, after)


def exchange(parts, axes):
    return lax.all_to_all(parts, axes, split_axis=0, concat_axis=0, tiled=True)


def sum_kernel(parts_ref, out_ref):
    total = parts_ref[0]
    for i in range(1, parts_ref.shape[0]):
        total = total + parts_ref[i]
    for i in range(out_ref.shape[0]):
        out_ref[i] = total


def sum_parts(parts, copies):
    return pl.pallas_call(
        sum_kernel,
        in_specs=[VMEM],
        out_specs=VMEM,
        out_shape=shape(copies, *parts.shape[1:]),
        compiler_params=SMALL,
        name="sum_parts",
    )(parts)


def swap(array):
    return lax.ppermute(array, "c", SWAP)


def swap_y(array, distance):
    return lax.ppermute(array, "y", [(i, i ^ distance) for i in range(NY)])


def shards(inputs, out_grads, error_buffer, start_basis):
    core = lax.axis_index("c")
    arguments = (inputs, out_grads, error_buffer[0], start_basis.T)
    x, g, e, s_rows = [pltpu.with_memory_space_constraint(array, pltpu.HBM) for array in arguments]
    m_other, p_other, *rest = moment_of_other(core, x, g, e, s_rows)
    arrived = swap(p_other)
    e_own, x_own, g, s_rows = rest
    m_own, p_own = moment_of_own(x_own, g, e_own, s_rows)
    m_arrived = swap(m_other)

    parts = exchange(p_own + arrived, ("y", "x"))
    parts = exchange(sum_parts(parts, NZ), "z")
    own = exchange(sum_parts(parts, NY * NX), ("y", "x"))
    other = swap(own)
    gram, w_own, w_other = own_terms(core, own, m_own, m_arrived)

    w = w_own + swap(w_other)
    gram = other_gram(other, gram, w_own)
    arrived = swap_y(w, 1)
    basis, factor1 = first_round(core, own, other, gram, w)
    w = sum_pair(w, arrived, factor1, 1)[0]
    arrived = swap_y(w, 2)
    factor2, factors = second_round(basis, factor1, w)
    w = sum_parts(exchange(sum_pair(w, arrived, factor2, NZ), "z"), 1)[0]
    p_rows = finish(basis, factor2, w)
    error, q_rows, p_rows = update(core, m_own, m_other, basis, factors, w, swap(w), p_rows)
    return (p_rows.T, q_rows.T, error[None])


def solution(mesh):
    fine = Mesh(mesh.devices.reshape(NZ, NY, NC, NX), ("z", "y", "c", "x"))
    dp = ("z", "y", "c")
    in_specs = (P(dp, None), P(dp, "x"), P(dp, None, "x"), P("x", None))
    out_specs = (P(), P("x", None), P(dp, None, "x"))
    return jax.shard_map(shards, mesh=fine, in_specs=in_specs, out_specs=out_specs, check_vma=False)
```

```python
import jax
import jax.numpy as jnp
from jax import lax
from jax.experimental import pallas as pl
from jax.experimental.pallas import tpu as pltpu
from jax.sharding import Mesh, PartitionSpec as P

HIGH = lax.Precision.HIGHEST
NZ, NY, NC, NX = 8, 4, 2, 4
DW, KV, R, TOK = 4096, 256, 64, 384
HALF, BLOCKS = DW // 2, DW // 256
BF, F32 = jnp.bfloat16, jnp.float32
SWAP = [(0, 1), (1, 0)]
NN = (((1,), (0,)), ((), ()))
NT = (((1,), (1,)), ((), ()))
TN = (((0,), (0,)), ((), ()))
VMEM = pl.BlockSpec(memory_space=pltpu.VMEM)
SMEM = pl.BlockSpec(memory_space=pltpu.SMEM)
HBM = pl.BlockSpec(memory_space=pltpu.HBM)
ANY = pl.BlockSpec(memory_space=pl.ANY)
BESIDE = pl.CostEstimate(flops=10 ** 9, bytes_accessed=4 << 20, transcendentals=0)
LIMIT = pltpu.CompilerParams(vmem_limit_bytes=24 << 20)
SMALL = pltpu.CompilerParams(vmem_limit_bytes=8 << 20)


def shape(*dims, dtype=F32):
    return jax.ShapeDtypeStruct(dims, dtype)


def dot(a, b, dims=NN):
    return lax.dot_general(a, b, dims, preferred_element_type=F32)


def dot_high(a, b, dims=NN):
    return lax.dot_general(a, b, dims, precision=HIGH, preferred_element_type=F32)


def lanes(start, size):
    return pl.ds(pl.multiple_of(start, size), size)


def split2(x):
    high = x.astype(BF)
    return high, (x - high.astype(F32)).astype(BF)


def split3(x):
    high = x.astype(BF)
    rest = x - high.astype(F32)
    middle = rest.astype(BF)
    return high, middle, (rest - middle.astype(F32)).astype(BF)


COLS = 512
LOAD = 1024


def p_half(moment, basis, p_ref):
    s1, s2, s3 = split3(basis)
    none = jnp.zeros_like(s1)
    orders = (s3, s2, s1), (s2, s1, none), (s1, none, none)
    weights = jnp.concatenate([jnp.concatenate(order, 1) for order in orders], 0)
    t = dot(jnp.concatenate(split3(moment), 1), weights, NT).T
    rows = (t[:R] + t[R:2 * R]) + t[2 * R:]
    for i in range(BLOCKS):
        p_ref[i] = rows[:, i * 128:(i + 1) * 128]


def moment_kernel(core_ref, x_hbm, g_hbm, e_hbm, s_hbm, m_ref, p_ref, e_ref, x_ref, g_ref, s_ref, x_buf, sems):
    core = core_ref[0]
    steps = HALF // LOAD
    copies = [pltpu.make_async_copy(g_hbm, g_ref, sems.at[0]), pltpu.make_async_copy(s_hbm, s_ref, sems.at[1])]
    for base, x_to, e_to in ((HALF - core * HALF, x_buf, m_ref), (core * HALF, x_ref, e_ref)):
        for j in range(steps):
            at, to = lanes(base + j * LOAD, LOAD), pl.ds(j * LOAD, LOAD)
            copies.append(pltpu.make_async_copy(x_hbm.at[:, at], x_to.at[j], sems.at[len(copies)]))
            copies.append(pltpu.make_async_copy(e_hbm.at[at, :], e_to.at[to, :], sems.at[len(copies)]))
    for copy in copies:
        copy.start()
    copies[0].wait()
    copies[1].wait()
    g = g_ref[...]
    for j in range(steps):
        copies[2 + 2 * j].wait()
        copies[3 + 2 * j].wait()
        at = pl.ds(j * LOAD, LOAD)
        m_ref[at, :] = dot(x_buf[j], g, TN) + m_ref[at, :]
    p_half(m_ref[...], s_ref[...], p_ref)
    for copy in copies[2 + 2 * steps:]:
        copy.wait()


def moment_of_other(core, x, g, e, s_rows):
    steps = HALF // LOAD
    return pl.pallas_call(
        moment_kernel,
        in_specs=[SMEM, HBM, HBM, HBM, HBM],
        out_specs=[VMEM] * 6,
        out_shape=[
            shape(HALF, KV),
            shape(BLOCKS, R, 128),
            shape(HALF, KV),
            shape(steps, TOK, LOAD, dtype=BF),
            shape(TOK, KV, dtype=BF),
            shape(R, KV),
        ],
        scratch_shapes=[pltpu.VMEM((steps, TOK, LOAD), BF), pltpu.SemaphoreType.DMA((2 + 4 * steps,))],
        compiler_params=LIMIT,
        name="moment_other",
    )(core.reshape(1), x, g, e, s_rows)


def own_kernel(x_ref, g_ref, e_ref, s_ref, m_ref, p_ref):
    g = g_ref[...]
    for j in range(HALF // LOAD):
        at = pl.ds(j * LOAD, LOAD)
        m_ref[at, :] = dot(x_ref[j], g, TN) + e_ref[at, :]
    p_half(m_ref[...], s_ref[...], p_ref)


def moment_of_own(x, g, e, s_rows):
    return pl.pallas_call(
        own_kernel,
        in_specs=[VMEM] * 4,
        out_specs=[VMEM] * 2,
        out_shape=[shape(HALF, KV), shape(BLOCKS, R, 128)],
        compiler_params=LIMIT,
        cost_estimate=BESIDE,
        name="moment_own",
    )(x, g, e, s_rows)


def inverse_factor(gram):
    rows = lax.broadcasted_iota(jnp.int32, (8, 128), 0)
    lanes = lax.broadcasted_iota(jnp.int32, (8, 128), 1)
    zero = jnp.zeros((8, R), F32)
    groups = [
        jnp.where(lanes == rows + R + 8 * i, 1.0, jnp.concatenate([gram[8 * i:8 * i + 8], zero], axis=1))
        for i in range(R // 8)
    ]
    pivots = []
    for b in range(R // 8):
        columns = [
            [jnp.broadcast_to(groups[i][:, 8 * b + c:8 * b + c + 1], (8, 128)) for i in range(b, R // 8)]
            for c in range(8)
        ]
        diagonal = jnp.zeros((8, 128), F32)
        for j in range(8):
            head = columns[j][0]
            pivot = jnp.broadcast_to(head[j:j + 1], (8, 128))
            inverse = 1.0 / pivot
            diagonal = jnp.where(rows == j, pivot, diagonal)
            factors = [column * inverse for column in columns[j]]
            factors[0] = jnp.where(rows > j, factors[0], 0.0)
            row = jnp.broadcast_to(groups[b][j:j + 1], (8, 128))
            for c in range(j + 1, 8):
                weight = jnp.broadcast_to(head[c:c + 1], (8, 128))
                columns[c] = [column - factor * weight for column, factor in zip(columns[c], factors)]
            for i in range(b, R // 8):
                groups[i] = groups[i] - factors[i - b] * row
        pivots.append(diagonal)
    return jnp.concatenate([(a * lax.rsqrt(d))[:, R:] for a, d in zip(groups, pivots)], axis=0)


def gram_matrix(rows):
    a1, a2, a3 = split3(rows)
    t = dot(jnp.concatenate([a1, a2, a3], 0), jnp.concatenate([a1, a2], 0), NT)
    t21, t31 = t[R:2 * R, :R], t[2 * R:, :R]
    return t[:R, :R] + ((t21 + t21.T) + (t[R:2 * R, R:] + (t31 + t31.T)))


def wide(blocks_ref):
    return jnp.concatenate([blocks_ref[j] for j in range(BLOCKS)], axis=1)


def product(p, m):
    p1, p2, p3 = split3(p)
    m1, m2, m3 = split3(m)
    t1 = dot(jnp.concatenate([p1, p2, p3], 0), m1)
    t2 = dot(jnp.concatenate([p1, p2], 0), m2)
    return t1[:R] + ((t1[R:2 * R] + t2[:R]) + ((t1[2 * R:] + t2[R:]) + dot(p1, m3)))


def own_term_kernel(core_ref, own_ref, m_ref, arrived_ref, w_own_ref, w_other_ref, w_ref):
    w_ref[...] = product(wide(own_ref), m_ref[...] + arrived_ref[...])
    mine = core_ref[0] * (R // 2)
    w_own_ref[...] = w_ref[lanes(mine, R // 2), :]
    w_other_ref[...] = w_ref[lanes(R // 2 - mine, R // 2), :]


def own_term(core, own, moment, arrived):
    return pl.pallas_call(
        own_term_kernel,
        in_specs=[SMEM] + [VMEM] * 3,
        out_specs=[VMEM] * 2,
        out_shape=[shape(R // 2, KV), shape(R // 2, KV)],
        scratch_shapes=[pltpu.VMEM((R, KV), F32)],
        compiler_params=LIMIT,
        cost_estimate=BESIDE,
        name="own_term",
    )(core.reshape(1), own, moment, arrived)


def own_gram_kernel(own_ref, after_ref, gram_ref):
    del after_ref
    gram_ref[...] = gram_matrix(wide(own_ref))


def own_gram(own, after):
    return pl.pallas_call(
        own_gram_kernel,
        in_specs=[VMEM, ANY],
        out_specs=VMEM,
        out_shape=shape(R, R),
        compiler_params=LIMIT,
        cost_estimate=BESIDE,
        name="own_gram",
    )(own, after)


def other_gram_kernel(other_ref, part_ref, gram_ref):
    gram_ref[...] = part_ref[...] + gram_matrix(wide(other_ref))


def other_gram(other, part):
    return pl.pallas_call(
        other_gram_kernel,
        in_specs=[VMEM, VMEM],
        out_specs=VMEM,
        out_shape=shape(R, R),
        compiler_params=LIMIT,
        cost_estimate=BESIDE,
        name="other_gram",
    )(other, part)


def first_round_kernel(core_ref, own_ref, other_ref, gram_ref, after_ref, b_ref, l_ref, part_ref):
    del after_ref
    core = core_ref[0]
    for j in range(BLOCKS):
        b_ref[:, lanes(core * HALF + j * 128, 128)] = own_ref[j]
        b_ref[:, lanes(HALF - core * HALF + j * 128, 128)] = other_ref[j]
    factor = inverse_factor(gram_ref[...])
    l_ref[...] = factor
    b_ref[...] = dot_high(factor, b_ref[...])
    part_ref[...] = gram_matrix(b_ref[:, :HALF])


def first_round(core, own, other, gram, after):
    return pl.pallas_call(
        first_round_kernel,
        in_specs=[SMEM] + [VMEM] * 3 + [ANY],
        out_specs=[VMEM] * 3,
        out_shape=[shape(R, DW), shape(R, R), shape(R, R)],
        compiler_params=LIMIT,
        cost_estimate=BESIDE,
        name="first_round",
    )(core.reshape(1), own, other, gram, after)


def second_factor_kernel(b_ref, part_ref, after_ref, l_ref):
    del after_ref
    l_ref[...] = inverse_factor(part_ref[...] + gram_matrix(b_ref[:, HALF:]))


def second_factor(basis, part, after):
    return pl.pallas_call(
        second_factor_kernel,
        in_specs=[VMEM, VMEM, ANY],
        out_specs=VMEM,
        out_shape=shape(R, R),
        compiler_params=LIMIT,
        cost_estimate=BESIDE,
        name="second_factor",
    )(basis, part, after)


def finish_kernel(b_ref, l1_ref, l2_ref, after_ref, p_ref, f_ref):
    del after_ref
    factor = l2_ref[...]
    both = dot_high(factor, l1_ref[...]) * (1.0 / (NZ * NY * NC))
    f_ref[:R, :] = both
    f_ref[R:, :] = dot_high(factor, both, TN)
    f1, f2, f3 = split3(factor)
    b1, b2, b3 = split3(b_ref[...])
    f = jnp.concatenate([f1, f2, f3, f1, f2, f1], 1)
    p_ref[...] = dot(f, jnp.concatenate([b1, b1, b1, b2, b2, b3], 0))


def finish(basis, factor1, factor2, after):
    return pl.pallas_call(
        finish_kernel,
        in_specs=[VMEM] * 3 + [ANY],
        out_specs=[VMEM] * 2,
        out_shape=[shape(R, DW), shape(2 * R, R)],
        compiler_params=LIMIT,
        cost_estimate=BESIDE,
        name="finish",
    )(basis, factor1, factor2, after)


def update_kernel(core_ref, m_own_ref, m_other_ref, b_ref, f_ref, w_own_ref, w_other_ref, p_ref, e_hbm, q_ref, p_hbm, w_ref, out, sems):
    core = core_ref[0]
    copies = [pltpu.make_async_copy(p_ref, p_hbm, sems.at[0])]
    copies[0].start()
    w_ref[lanes(core * (R // 2), R // 2), :] = w_own_ref[...]
    w_ref[lanes(R // 2 - core * (R // 2), R // 2), :] = w_other_ref[...]
    qr = dot_high(f_ref[...], w_ref[...])
    q_ref[...] = qr[:R]
    r1, r2 = split2(qr[R:])
    r121 = jnp.concatenate([r1, r2, r1], 0)
    for part, (base, m_ref) in enumerate(((core * HALF, m_own_ref), (HALF - core * HALF, m_other_ref))):
        for t in range(0, HALF, COLS):
            at, here = lanes(base + t, COLS), pl.ds(part * HALF + t, COLS)
            b1, b2 = split2(b_ref[:, at])
            out[here, :] = m_ref[t:t + COLS, :] - dot(jnp.concatenate([b1, b1, b2], 0), r121, TN)
            copies.append(pltpu.make_async_copy(out.at[here, :], e_hbm.at[at, :], sems.at[len(copies)]))
            copies[-1].start()
    for copy in copies:
        copy.wait()


def update(core, m_own, m_other, basis, factors, w_own, w_other, p_rows):
    return pl.pallas_call(
        update_kernel,
        in_specs=[SMEM] + [VMEM] * 7,
        out_specs=[HBM, VMEM, HBM],
        out_shape=[shape(DW, KV), shape(R, KV), shape(R, DW)],
        scratch_shapes=[
            pltpu.VMEM((R, KV), F32),
            pltpu.VMEM((DW, KV), F32),
            pltpu.SemaphoreType.DMA((1 + DW // COLS,)),
        ],
        compiler_params=LIMIT,
        name="update",
    )(core.reshape(1), m_own, m_other, basis, factors, w_own, w_other, p_rows)


def pair_kernel(w_ref, arrived_ref, after_ref, out_ref):
    del after_ref
    total = w_ref[...] + arrived_ref[...]
    for i in range(out_ref.shape[0]):
        out_ref[i] = total


def sum_pair(w, arrived, after, copies):
    return pl.pallas_call(
        pair_kernel,
        in_specs=[VMEM] * 2 + [ANY],
        out_specs=VMEM,
        out_shape=shape(copies, *w.shape),
        compiler_params=SMALL,
        name="sum_pair",
    )(w, arrived, after)


def exchange(parts, axes):
    return lax.all_to_all(parts, axes, split_axis=0, concat_axis=0, tiled=True)


def sum_kernel(parts_ref, out_ref):
    total = parts_ref[0]
    for i in range(1, parts_ref.shape[0]):
        total = total + parts_ref[i]
    for i in range(out_ref.shape[0]):
        out_ref[i] = total


def sum_parts(parts, copies):
    return pl.pallas_call(
        sum_kernel,
        in_specs=[VMEM],
        out_specs=VMEM,
        out_shape=shape(copies, *parts.shape[1:]),
        compiler_params=SMALL,
        name="sum_parts",
    )(parts)


def swap(array):
    return lax.ppermute(array, "c", SWAP)


def swap_y(array, distance):
    return lax.ppermute(array, "y", [(i, i ^ distance) for i in range(NY)])


def shards(inputs, out_grads, error_buffer, start_basis):
    core = lax.axis_index("c")
    arguments = (inputs, out_grads, error_buffer[0], start_basis.T)
    x, g, e, s_rows = [pltpu.with_memory_space_constraint(array, pltpu.HBM) for array in arguments]
    m_other, p_other, *rest = moment_of_other(core, x, g, e, s_rows)
    arrived = swap(p_other)
    e_own, x_own, g, s_rows = rest
    m_own, p_own = moment_of_own(x_own, g, e_own, s_rows)
    m_arrived = swap(m_other)

    parts = exchange(p_own + arrived, ("y", "x"))
    parts = exchange(sum_parts(parts, NZ), "z")
    own = exchange(sum_parts(parts, NY * NX), ("y", "x"))
    other = swap(own)
    w_own, w_other = own_term(core, own, m_own, m_arrived)

    arrived = swap(w_other)
    gram = other_gram(other, own_gram(own, w_own))
    w = sum_pair(w_own, arrived, gram, 1)[0]
    arrived = swap_y(w, 1)
    basis, factor1, part = first_round(core, own, other, gram, w)
    w = sum_pair(w, arrived, factor1, 1)[0]
    arrived = swap_y(w, 2)
    factor2 = second_factor(basis, part, w)
    w = sum_parts(exchange(sum_pair(w, arrived, factor2, NZ), "z"), 1)[0]
    p_rows, factors = finish(basis, factor1, factor2, w)
    error, q_rows, p_rows = update(core, m_own, m_other, basis, factors, w, swap(w), p_rows)
    return (p_rows.T, q_rows.T, error[None])


def solution(mesh):
    fine = Mesh(mesh.devices.reshape(NZ, NY, NC, NX), ("z", "y", "c", "x"))
    dp = ("z", "y", "c")
    in_specs = (P(dp, None), P(dp, "x"), P(dp, None, "x"), P("x", None))
    out_specs = (P(), P("x", None), P(dp, None, "x"))
    return jax.shard_map(shards, mesh=fine, in_specs=in_specs, out_specs=out_specs, check_vma=False)
```

```python
import jax
import jax.numpy as jnp
from jax import lax
from jax.experimental import pallas as pl
from jax.experimental.pallas import tpu as pltpu
from jax.sharding import Mesh, PartitionSpec as P

HIGH = lax.Precision.HIGHEST
NZ, NY, NC, NX = 8, 4, 2, 4
DW, KV, R, TOK = 4096, 256, 64, 384
HALF, BLOCKS = DW // 2, DW // 256
BF, F32 = jnp.bfloat16, jnp.float32
SWAP = [(0, 1), (1, 0)]
NN = (((1,), (0,)), ((), ()))
NT = (((1,), (1,)), ((), ()))
TN = (((0,), (0,)), ((), ()))
VMEM = pl.BlockSpec(memory_space=pltpu.VMEM)
SMEM = pl.BlockSpec(memory_space=pltpu.SMEM)
HBM = pl.BlockSpec(memory_space=pltpu.HBM)
ANY = pl.BlockSpec(memory_space=pl.ANY)
BESIDE = pl.CostEstimate(flops=10 ** 9, bytes_accessed=4 << 20, transcendentals=0)
LIMIT = pltpu.CompilerParams(vmem_limit_bytes=24 << 20)
SMALL = pltpu.CompilerParams(vmem_limit_bytes=8 << 20)


def shape(*dims, dtype=F32):
    return jax.ShapeDtypeStruct(dims, dtype)


def dot(a, b, dims=NN):
    return lax.dot_general(a, b, dims, preferred_element_type=F32)


def dot_high(a, b, dims=NN):
    return lax.dot_general(a, b, dims, precision=HIGH, preferred_element_type=F32)


def lanes(start, size):
    return pl.ds(pl.multiple_of(start, size), size)


def split2(x):
    high = x.astype(BF)
    return high, (x - high.astype(F32)).astype(BF)


def split3(x):
    high = x.astype(BF)
    rest = x - high.astype(F32)
    middle = rest.astype(BF)
    return high, middle, (rest - middle.astype(F32)).astype(BF)


COLS = 512
LOAD = 1024


def p_half(moment, basis, p_ref):
    s1, s2, s3 = split3(basis)
    none = jnp.zeros_like(s1)
    orders = (s3, s2, s1), (s2, s1, none), (s1, none, none)
    weights = jnp.concatenate([jnp.concatenate(order, 1) for order in orders], 0)
    t = dot(jnp.concatenate(split3(moment), 1), weights, NT).T
    rows = (t[:R] + t[R:2 * R]) + t[2 * R:]
    for i in range(BLOCKS):
        p_ref[i] = rows[:, i * 128:(i + 1) * 128]


def moment_kernel(core_ref, x_hbm, g_hbm, e_hbm, s_hbm, m_ref, p_ref, e_ref, x_ref, g_ref, s_ref, x_buf, sems):
    core = core_ref[0]
    steps = HALF // LOAD
    copies = [pltpu.make_async_copy(g_hbm, g_ref, sems.at[0]), pltpu.make_async_copy(s_hbm, s_ref, sems.at[1])]
    for base, x_to, e_to in ((HALF - core * HALF, x_buf, m_ref), (core * HALF, x_ref, e_ref)):
        for j in range(steps):
            at, to = lanes(base + j * LOAD, LOAD), pl.ds(j * LOAD, LOAD)
            copies.append(pltpu.make_async_copy(x_hbm.at[:, at], x_to.at[j], sems.at[len(copies)]))
            copies.append(pltpu.make_async_copy(e_hbm.at[at, :], e_to.at[to, :], sems.at[len(copies)]))
    for copy in copies:
        copy.start()
    copies[0].wait()
    copies[1].wait()
    g = g_ref[...]
    for j in range(steps):
        copies[2 + 2 * j].wait()
        copies[3 + 2 * j].wait()
        at = pl.ds(j * LOAD, LOAD)
        m_ref[at, :] = dot(x_buf[j], g, TN) + m_ref[at, :]
    p_half(m_ref[...], s_ref[...], p_ref)
    for copy in copies[2 + 2 * steps:]:
        copy.wait()


def moment_of_other(core, x, g, e, s_rows):
    steps = HALF // LOAD
    return pl.pallas_call(
        moment_kernel,
        in_specs=[SMEM, HBM, HBM, HBM, HBM],
        out_specs=[VMEM] * 6,
        out_shape=[
            shape(HALF, KV),
            shape(BLOCKS, R, 128),
            shape(HALF, KV),
            shape(steps, TOK, LOAD, dtype=BF),
            shape(TOK, KV, dtype=BF),
            shape(R, KV),
        ],
        scratch_shapes=[pltpu.VMEM((steps, TOK, LOAD), BF), pltpu.SemaphoreType.DMA((2 + 4 * steps,))],
        compiler_params=LIMIT,
        name="moment_other",
    )(core.reshape(1), x, g, e, s_rows)


def own_kernel(x_ref, g_ref, e_ref, s_ref, m_ref, p_ref):
    g = g_ref[...]
    for j in range(HALF // LOAD):
        at = pl.ds(j * LOAD, LOAD)
        m_ref[at, :] = dot(x_ref[j], g, TN) + e_ref[at, :]
    p_half(m_ref[...], s_ref[...], p_ref)


def moment_of_own(x, g, e, s_rows):
    return pl.pallas_call(
        own_kernel,
        in_specs=[VMEM] * 4,
        out_specs=[VMEM] * 2,
        out_shape=[shape(HALF, KV), shape(BLOCKS, R, 128)],
        compiler_params=LIMIT,
        cost_estimate=BESIDE,
        name="moment_own",
    )(x, g, e, s_rows)


def inverse_factor(gram):
    rows = lax.broadcasted_iota(jnp.int32, (8, 128), 0)
    lanes = lax.broadcasted_iota(jnp.int32, (8, 128), 1)
    zero = jnp.zeros((8, R), F32)
    groups = [
        jnp.where(lanes == rows + R + 8 * i, 1.0, jnp.concatenate([gram[8 * i:8 * i + 8], zero], axis=1))
        for i in range(R // 8)
    ]
    pivots = []
    for b in range(R // 8):
        columns = [
            [jnp.broadcast_to(groups[i][:, 8 * b + c:8 * b + c + 1], (8, 128)) for i in range(b, R // 8)]
            for c in range(8)
        ]
        diagonal = jnp.zeros((8, 128), F32)
        for j in range(8):
            head = columns[j][0]
            pivot = jnp.broadcast_to(head[j:j + 1], (8, 128))
            inverse = 1.0 / pivot
            diagonal = jnp.where(rows == j, pivot, diagonal)
            factors = [column * inverse for column in columns[j]]
            factors[0] = jnp.where(rows > j, factors[0], 0.0)
            row = jnp.broadcast_to(groups[b][j:j + 1], (8, 128))
            for c in range(j + 1, 8):
                weight = jnp.broadcast_to(head[c:c + 1], (8, 128))
                columns[c] = [column - factor * weight for column, factor in zip(columns[c], factors)]
            for i in range(b, R // 8):
                groups[i] = groups[i] - factors[i - b] * row
        pivots.append(diagonal)
    return jnp.concatenate([(a * lax.rsqrt(d))[:, R:] for a, d in zip(groups, pivots)], axis=0)


def gram_matrix(rows):
    a1, a2, a3 = split3(rows)
    t = dot(jnp.concatenate([a1, a2, a3], 0), jnp.concatenate([a1, a2], 0), NT)
    t21, t31 = t[R:2 * R, :R], t[2 * R:, :R]
    return t[:R, :R] + ((t21 + t21.T) + (t[R:2 * R, R:] + (t31 + t31.T)))


def wide(blocks_ref):
    return jnp.concatenate([blocks_ref[j] for j in range(BLOCKS)], axis=1)


def product(p, m):
    p1, p2, p3 = split3(p)
    m1, m2, m3 = split3(m)
    t1 = dot(jnp.concatenate([p1, p2, p3], 0), m1)
    t2 = dot(jnp.concatenate([p1, p2], 0), m2)
    return t1[:R] + ((t1[R:2 * R] + t2[:R]) + ((t1[2 * R:] + t2[R:]) + dot(p1, m3)))


def own_term_kernel(core_ref, own_ref, m_ref, arrived_ref, w_own_ref, w_other_ref, w_ref):
    w_ref[...] = product(wide(own_ref), m_ref[...] + arrived_ref[...])
    mine = core_ref[0] * (R // 2)
    w_own_ref[...] = w_ref[lanes(mine, R // 2), :]
    w_other_ref[...] = w_ref[lanes(R // 2 - mine, R // 2), :]


def own_term(core, own, moment, arrived):
    return pl.pallas_call(
        own_term_kernel,
        in_specs=[SMEM] + [VMEM] * 3,
        out_specs=[VMEM] * 2,
        out_shape=[shape(R // 2, KV), shape(R // 2, KV)],
        scratch_shapes=[pltpu.VMEM((R, KV), F32)],
        compiler_params=LIMIT,
        cost_estimate=BESIDE,
        name="own_term",
    )(core.reshape(1), own, moment, arrived)


def own_gram_kernel(own_ref, after_ref, gram_ref):
    del after_ref
    gram_ref[...] = gram_matrix(wide(own_ref))


def own_gram(own, after):
    return pl.pallas_call(
        own_gram_kernel,
        in_specs=[VMEM, ANY],
        out_specs=VMEM,
        out_shape=shape(R, R),
        compiler_params=LIMIT,
        cost_estimate=BESIDE,
        name="own_gram",
    )(own, after)


def other_gram_kernel(other_ref, part_ref, gram_ref):
    gram_ref[...] = part_ref[...] + gram_matrix(wide(other_ref))


def other_gram(other, part):
    return pl.pallas_call(
        other_gram_kernel,
        in_specs=[VMEM, VMEM],
        out_specs=VMEM,
        out_shape=shape(R, R),
        compiler_params=LIMIT,
        cost_estimate=BESIDE,
        name="other_gram",
    )(other, part)


def first_round_kernel(core_ref, own_ref, other_ref, gram_ref, after_ref, b_ref, l_ref, part_ref):
    del after_ref
    core = core_ref[0]
    for j in range(BLOCKS):
        b_ref[:, lanes(core * HALF + j * 128, 128)] = own_ref[j]
        b_ref[:, lanes(HALF - core * HALF + j * 128, 128)] = other_ref[j]
    factor = inverse_factor(gram_ref[...])
    l_ref[...] = factor
    b_ref[...] = dot_high(factor, b_ref[...])
    part_ref[...] = gram_matrix(b_ref[:, :LOAD])


def first_round(core, own, other, gram, after):
    return pl.pallas_call(
        first_round_kernel,
        in_specs=[SMEM] + [VMEM] * 3 + [ANY],
        out_specs=[VMEM] * 3,
        out_shape=[shape(R, DW), shape(R, R), shape(R, R)],
        compiler_params=LIMIT,
        cost_estimate=BESIDE,
        name="first_round",
    )(core.reshape(1), own, other, gram, after)


def second_factor_kernel(b_ref, part_ref, after_ref, l_ref, bt_ref):
    del after_ref
    l_ref[...] = inverse_factor(part_ref[...] + gram_matrix(b_ref[:, LOAD:]))
    bt_ref[...] = jnp.concatenate(split2(b_ref[...]), 0).T


def second_factor(basis, part, after):
    return pl.pallas_call(
        second_factor_kernel,
        in_specs=[VMEM, VMEM, ANY],
        out_specs=[VMEM] * 2,
        out_shape=[shape(R, R), shape(DW, 2 * R, dtype=BF)],
        compiler_params=LIMIT,
        cost_estimate=BESIDE,
        name="second_factor",
    )(basis, part, after)


def finish_kernel(b_ref, l1_ref, l2_ref, after_ref, p_ref, f_ref):
    del after_ref
    factor = l2_ref[...]
    both = dot_high(factor, l1_ref[...]) * (1.0 / (NZ * NY * NC))
    f_ref[:R, :] = both
    f_ref[R:, :] = dot_high(factor, both, TN)
    f1, f2, f3 = split3(factor)
    b1, b2, b3 = split3(b_ref[...])
    f = jnp.concatenate([f1, f2, f3, f1, f2, f1], 1)
    p_ref[...] = dot(f, jnp.concatenate([b1, b1, b1, b2, b2, b3], 0))


def finish(basis, factor1, factor2, after):
    return pl.pallas_call(
        finish_kernel,
        in_specs=[VMEM] * 3 + [ANY],
        out_specs=[VMEM] * 2,
        out_shape=[shape(R, DW), shape(2 * R, R)],
        compiler_params=LIMIT,
        cost_estimate=BESIDE,
        name="finish",
    )(basis, factor1, factor2, after)


def update_kernel(core_ref, m_own_ref, m_other_ref, bt_ref, f_ref, w_own_ref, w_other_ref, p_ref, e_hbm, q_ref, p_hbm, w_ref, out, sems):
    core = core_ref[0]
    copies = [pltpu.make_async_copy(p_ref, p_hbm, sems.at[0])]
    copies[0].start()
    w_ref[lanes(core * (R // 2), R // 2), :] = w_own_ref[...]
    w_ref[lanes(R // 2 - core * (R // 2), R // 2), :] = w_other_ref[...]
    qr = dot_high(f_ref[...], w_ref[...])
    q_ref[...] = qr[:R]
    r1, r2 = split2(qr[R:])
    weights = jnp.concatenate([r1, r1, r2, jnp.zeros_like(r1)], 0)
    for part, (base, m_ref) in enumerate(((core * HALF, m_own_ref), (HALF - core * HALF, m_other_ref))):
        for t in range(0, HALF, COLS):
            at, here = lanes(base + t, COLS), pl.ds(part * HALF + t, COLS)
            bt = bt_ref[at, :]
            out[here, :] = m_ref[t:t + COLS, :] - dot(jnp.concatenate([bt, bt], 1), weights)
            copies.append(pltpu.make_async_copy(out.at[here, :], e_hbm.at[at, :], sems.at[len(copies)]))
            copies[-1].start()
    for copy in copies:
        copy.wait()


def update(core, m_own, m_other, basis_t, factors, w_own, w_other, p_rows):
    return pl.pallas_call(
        update_kernel,
        in_specs=[SMEM] + [VMEM] * 7,
        out_specs=[HBM, VMEM, HBM],
        out_shape=[shape(DW, KV), shape(R, KV), shape(R, DW)],
        scratch_shapes=[
            pltpu.VMEM((R, KV), F32),
            pltpu.VMEM((DW, KV), F32),
            pltpu.SemaphoreType.DMA((1 + DW // COLS,)),
        ],
        compiler_params=LIMIT,
        name="update",
    )(core.reshape(1), m_own, m_other, basis_t, factors, w_own, w_other, p_rows)


def pair_kernel(w_ref, arrived_ref, after_ref, out_ref):
    del after_ref
    total = w_ref[...] + arrived_ref[...]
    for i in range(out_ref.shape[0]):
        out_ref[i] = total


def sum_pair(w, arrived, after, copies):
    return pl.pallas_call(
        pair_kernel,
        in_specs=[VMEM] * 2 + [ANY],
        out_specs=VMEM,
        out_shape=shape(copies, *w.shape),
        compiler_params=SMALL,
        name="sum_pair",
    )(w, arrived, after)


def exchange(parts, axes):
    return lax.all_to_all(parts, axes, split_axis=0, concat_axis=0, tiled=True)


def sum_kernel(parts_ref, out_ref):
    total = parts_ref[0]
    for i in range(1, parts_ref.shape[0]):
        total = total + parts_ref[i]
    for i in range(out_ref.shape[0]):
        out_ref[i] = total


def sum_parts(parts, copies):
    return pl.pallas_call(
        sum_kernel,
        in_specs=[VMEM],
        out_specs=VMEM,
        out_shape=shape(copies, *parts.shape[1:]),
        compiler_params=SMALL,
        name="sum_parts",
    )(parts)


def swap(array):
    return lax.ppermute(array, "c", SWAP)


def swap_y(array, distance):
    return lax.ppermute(array, "y", [(i, i ^ distance) for i in range(NY)])


def shards(inputs, out_grads, error_buffer, start_basis):
    core = lax.axis_index("c")
    arguments = (inputs, out_grads, error_buffer[0], start_basis.T)
    x, g, e, s_rows = [pltpu.with_memory_space_constraint(array, pltpu.HBM) for array in arguments]
    m_other, p_other, *rest = moment_of_other(core, x, g, e, s_rows)
    arrived = swap(p_other)
    e_own, x_own, g, s_rows = rest
    m_own, p_own = moment_of_own(x_own, g, e_own, s_rows)
    m_arrived = swap(m_other)

    parts = exchange(p_own + arrived, ("y", "x"))
    parts = exchange(sum_parts(parts, NZ), "z")
    own = exchange(sum_parts(parts, NY * NX), ("y", "x"))
    other = swap(own)
    w_own, w_other = own_term(core, own, m_own, m_arrived)

    arrived = swap(w_other)
    gram = other_gram(other, own_gram(own, w_own))
    w = sum_pair(w_own, arrived, gram, 1)[0]
    arrived = swap_y(w, 1)
    basis, factor1, part = first_round(core, own, other, gram, w)
    w = sum_pair(w, arrived, factor1, 1)[0]
    arrived = swap_y(w, 2)
    factor2, basis_t = second_factor(basis, part, w)
    w = sum_parts(exchange(sum_pair(w, arrived, factor2, NZ), "z"), 1)[0]
    p_rows, factors = finish(basis, factor1, factor2, w)
    error, q_rows, p_rows = update(core, m_own, m_other, basis_t, factors, w, swap(w), p_rows)
    return (p_rows.T, q_rows.T, error[None])


def solution(mesh):
    fine = Mesh(mesh.devices.reshape(NZ, NY, NC, NX), ("z", "y", "c", "x"))
    dp = ("z", "y", "c")
    in_specs = (P(dp, None), P(dp, "x"), P(dp, None, "x"), P("x", None))
    out_specs = (P(), P("x", None), P(dp, None, "x"))
    return jax.shard_map(shards, mesh=fine, in_specs=in_specs, out_specs=out_specs, check_vma=False)
```

```python
import jax
import jax.numpy as jnp
from jax import lax
from jax.experimental import pallas as pl
from jax.experimental.pallas import tpu as pltpu
from jax.sharding import Mesh, PartitionSpec as P

HIGH = lax.Precision.HIGHEST
NZ, NY, NC, NX = 8, 4, 2, 4
DW, KV, R, TOK = 4096, 256, 64, 384
HALF, BLOCKS = DW // 2, DW // 256
BF, F32 = jnp.bfloat16, jnp.float32
SWAP = [(0, 1), (1, 0)]
NN = (((1,), (0,)), ((), ()))
NT = (((1,), (1,)), ((), ()))
TN = (((0,), (0,)), ((), ()))
VMEM = pl.BlockSpec(memory_space=pltpu.VMEM)
SMEM = pl.BlockSpec(memory_space=pltpu.SMEM)
HBM = pl.BlockSpec(memory_space=pltpu.HBM)
ANY = pl.BlockSpec(memory_space=pl.ANY)
BESIDE = pl.CostEstimate(flops=10 ** 9, bytes_accessed=4 << 20, transcendentals=0)
LIMIT = pltpu.CompilerParams(vmem_limit_bytes=24 << 20)
SMALL = pltpu.CompilerParams(vmem_limit_bytes=8 << 20)


def shape(*dims, dtype=F32):
    return jax.ShapeDtypeStruct(dims, dtype)


def dot(a, b, dims=NN):
    return lax.dot_general(a, b, dims, preferred_element_type=F32)


def dot_high(a, b, dims=NN):
    return lax.dot_general(a, b, dims, precision=HIGH, preferred_element_type=F32)


def lanes(start, size):
    return pl.ds(pl.multiple_of(start, size), size)


def split2(x):
    high = x.astype(BF)
    return high, (x - high.astype(F32)).astype(BF)


def split3(x):
    high = x.astype(BF)
    rest = x - high.astype(F32)
    middle = rest.astype(BF)
    return high, middle, (rest - middle.astype(F32)).astype(BF)


COLS = 512
LOAD = 1024


def p_half(moment, basis, p_ref):
    s1, s2, s3 = split3(basis)
    none = jnp.zeros_like(s1)
    orders = (s3, s2, s1), (s2, s1, none), (s1, none, none)
    weights = jnp.concatenate([jnp.concatenate(order, 1) for order in orders], 0)
    t = dot(jnp.concatenate(split3(moment), 1), weights, NT).T
    rows = (t[:R] + t[R:2 * R]) + t[2 * R:]
    for i in range(BLOCKS):
        p_ref[i] = rows[:, i * 128:(i + 1) * 128]


def moment_kernel(core_ref, x_hbm, g_hbm, e_hbm, s_hbm, m_ref, p_ref, e_ref, x_ref, g_ref, s_ref, x_buf, sems):
    core = core_ref[0]
    steps = HALF // LOAD
    copies = [pltpu.make_async_copy(g_hbm, g_ref, sems.at[0]), pltpu.make_async_copy(s_hbm, s_ref, sems.at[1])]
    for base, x_to, e_to in ((HALF - core * HALF, x_buf, m_ref), (core * HALF, x_ref, e_ref)):
        for j in range(steps):
            at, to = lanes(base + j * LOAD, LOAD), pl.ds(j * LOAD, LOAD)
            copies.append(pltpu.make_async_copy(x_hbm.at[:, at], x_to.at[j], sems.at[len(copies)]))
            copies.append(pltpu.make_async_copy(e_hbm.at[at, :], e_to.at[to, :], sems.at[len(copies)]))
    for copy in copies:
        copy.start()
    copies[0].wait()
    copies[1].wait()
    g = g_ref[...]
    for j in range(steps):
        copies[2 + 2 * j].wait()
        copies[3 + 2 * j].wait()
        at = pl.ds(j * LOAD, LOAD)
        m_ref[at, :] = dot(x_buf[j], g, TN) + m_ref[at, :]
    p_half(m_ref[...], s_ref[...], p_ref)
    for copy in copies[2 + 2 * steps:]:
        copy.wait()


def moment_of_other(core, x, g, e, s_rows):
    steps = HALF // LOAD
    return pl.pallas_call(
        moment_kernel,
        in_specs=[SMEM, HBM, HBM, HBM, HBM],
        out_specs=[VMEM] * 6,
        out_shape=[
            shape(HALF, KV),
            shape(BLOCKS, R, 128),
            shape(HALF, KV),
            shape(steps, TOK, LOAD, dtype=BF),
            shape(TOK, KV, dtype=BF),
            shape(R, KV),
        ],
        scratch_shapes=[pltpu.VMEM((steps, TOK, LOAD), BF), pltpu.SemaphoreType.DMA((2 + 4 * steps,))],
        compiler_params=LIMIT,
        name="moment_other",
    )(core.reshape(1), x, g, e, s_rows)


def own_kernel(x_ref, g_ref, e_ref, s_ref, m_ref, p_ref):
    g = g_ref[...]
    for j in range(HALF // LOAD):
        at = pl.ds(j * LOAD, LOAD)
        m_ref[at, :] = dot(x_ref[j], g, TN) + e_ref[at, :]
    p_half(m_ref[...], s_ref[...], p_ref)


def moment_of_own(x, g, e, s_rows):
    return pl.pallas_call(
        own_kernel,
        in_specs=[VMEM] * 4,
        out_specs=[VMEM] * 2,
        out_shape=[shape(HALF, KV), shape(BLOCKS, R, 128)],
        compiler_params=LIMIT,
        cost_estimate=BESIDE,
        name="moment_own",
    )(x, g, e, s_rows)


def inverse_factor(gram):
    rows = lax.broadcasted_iota(jnp.int32, (8, 128), 0)
    lanes = lax.broadcasted_iota(jnp.int32, (8, 128), 1)
    zero = jnp.zeros((8, R), F32)
    groups = [
        jnp.where(lanes == rows + R + 8 * i, 1.0, jnp.concatenate([gram[8 * i:8 * i + 8], zero], axis=1))
        for i in range(R // 8)
    ]
    pivots = []
    for b in range(R // 8):
        columns = [
            [jnp.broadcast_to(groups[i][:, 8 * b + c:8 * b + c + 1], (8, 128)) for i in range(b, R // 8)]
            for c in range(8)
        ]
        diagonal = jnp.zeros((8, 128), F32)
        for j in range(8):
            head = columns[j][0]
            pivot = jnp.broadcast_to(head[j:j + 1], (8, 128))
            inverse = 1.0 / pivot
            diagonal = jnp.where(rows == j, pivot, diagonal)
            factors = [column * inverse for column in columns[j]]
            factors[0] = jnp.where(rows > j, factors[0], 0.0)
            row = jnp.broadcast_to(groups[b][j:j + 1], (8, 128))
            for c in range(j + 1, 8):
                weight = jnp.broadcast_to(head[c:c + 1], (8, 128))
                columns[c] = [column - factor * weight for column, factor in zip(columns[c], factors)]
            for i in range(b, R // 8):
                groups[i] = groups[i] - factors[i - b] * row
        pivots.append(diagonal)
    return jnp.concatenate([(a * lax.rsqrt(d))[:, R:] for a, d in zip(groups, pivots)], axis=0)


def gram_matrix(rows):
    a1, a2, a3 = split3(rows)
    t = dot(jnp.concatenate([a1, a2, a3], 0), jnp.concatenate([a1, a2], 0), NT)
    t21, t31 = t[R:2 * R, :R], t[2 * R:, :R]
    return t[:R, :R] + ((t21 + t21.T) + (t[R:2 * R, R:] + (t31 + t31.T)))


def wide(blocks_ref):
    return jnp.concatenate([blocks_ref[j] for j in range(BLOCKS)], axis=1)


def product(p, m):
    p1, p2, p3 = split3(p)
    m1, m2, m3 = split3(m)
    t1 = dot(jnp.concatenate([p1, p2, p3], 0), m1)
    t2 = dot(jnp.concatenate([p1, p2], 0), m2)
    return t1[:R] + ((t1[R:2 * R] + t2[:R]) + ((t1[2 * R:] + t2[R:]) + dot(p1, m3)))


def own_term_kernel(core_ref, own_ref, m_ref, arrived_ref, w_own_ref, w_other_ref, w_ref):
    w_ref[...] = product(wide(own_ref), m_ref[...] + arrived_ref[...])
    mine = core_ref[0] * (R // 2)
    w_own_ref[...] = w_ref[lanes(mine, R // 2), :]
    w_other_ref[...] = w_ref[lanes(R // 2 - mine, R // 2), :]


def own_term(core, own, moment, arrived):
    return pl.pallas_call(
        own_term_kernel,
        in_specs=[SMEM] + [VMEM] * 3,
        out_specs=[VMEM] * 2,
        out_shape=[shape(R // 2, KV), shape(R // 2, KV)],
        scratch_shapes=[pltpu.VMEM((R, KV), F32)],
        compiler_params=LIMIT,
        cost_estimate=BESIDE,
        name="own_term",
    )(core.reshape(1), own, moment, arrived)


def own_gram_kernel(own_ref, after_ref, gram_ref):
    del after_ref
    gram_ref[...] = gram_matrix(wide(own_ref))


def own_gram(own, after):
    return pl.pallas_call(
        own_gram_kernel,
        in_specs=[VMEM, ANY],
        out_specs=VMEM,
        out_shape=shape(R, R),
        compiler_params=LIMIT,
        cost_estimate=BESIDE,
        name="own_gram",
    )(own, after)


def other_gram_kernel(other_ref, part_ref, gram_ref):
    gram_ref[...] = part_ref[...] + gram_matrix(wide(other_ref))


def other_gram(other, part):
    return pl.pallas_call(
        other_gram_kernel,
        in_specs=[VMEM, VMEM],
        out_specs=VMEM,
        out_shape=shape(R, R),
        compiler_params=LIMIT,
        cost_estimate=BESIDE,
        name="other_gram",
    )(other, part)


def first_round_kernel(core_ref, own_ref, other_ref, gram_ref, after_ref, b_ref, l_ref, part_ref):
    del after_ref
    core = core_ref[0]
    for j in range(BLOCKS):
        b_ref[:, lanes(core * HALF + j * 128, 128)] = own_ref[j]
        b_ref[:, lanes(HALF - core * HALF + j * 128, 128)] = other_ref[j]
    factor = inverse_factor(gram_ref[...])
    l_ref[...] = factor
    b_ref[...] = dot_high(factor, b_ref[...])
    part_ref[...] = gram_matrix(b_ref[:, :LOAD])


def first_round(core, own, other, gram, after):
    return pl.pallas_call(
        first_round_kernel,
        in_specs=[SMEM] + [VMEM] * 3 + [ANY],
        out_specs=[VMEM] * 3,
        out_shape=[shape(R, DW), shape(R, R), shape(R, R)],
        compiler_params=LIMIT,
        cost_estimate=BESIDE,
        name="first_round",
    )(core.reshape(1), own, other, gram, after)


def second_factor_kernel(b_ref, part_ref, after_ref, l_ref, bt_ref):
    del after_ref
    l_ref[...] = inverse_factor(part_ref[...] + gram_matrix(b_ref[:, LOAD:]))
    bt_ref[...] = jnp.concatenate(split2(b_ref[...]), 0).T


def second_factor(basis, part, after):
    return pl.pallas_call(
        second_factor_kernel,
        in_specs=[VMEM, VMEM, ANY],
        out_specs=[VMEM] * 2,
        out_shape=[shape(R, R), shape(DW, 2 * R, dtype=BF)],
        compiler_params=LIMIT,
        cost_estimate=BESIDE,
        name="second_factor",
    )(basis, part, after)


def finish_kernel(b_ref, l1_ref, l2_ref, after_ref, p_ref, f_ref):
    del after_ref
    factor = l2_ref[...]
    both = dot_high(factor, l1_ref[...]) * (1.0 / (NZ * NY * NC))
    f_ref[:R, :] = both
    f_ref[R:, :] = dot_high(factor, both, TN)
    f1, f2, f3 = split3(factor)
    b1, b2, b3 = split3(b_ref[...])
    f = jnp.concatenate([f1, f2, f3, f1, f2, f1], 1)
    p_ref[...] = dot(f, jnp.concatenate([b1, b1, b1, b2, b2, b3], 0))


def finish(basis, factor1, factor2, after):
    return pl.pallas_call(
        finish_kernel,
        in_specs=[VMEM] * 3 + [ANY],
        out_specs=[VMEM] * 2,
        out_shape=[shape(R, DW), shape(2 * R, R)],
        compiler_params=LIMIT,
        cost_estimate=BESIDE,
        name="finish",
    )(basis, factor1, factor2, after)


def update_kernel(core_ref, m_own_ref, m_other_ref, bt_ref, f_ref, w_own_ref, w_other_ref, p_ref, e_hbm, q_ref, p_hbm, w_ref, out, sems):
    core = core_ref[0]
    copies = [pltpu.make_async_copy(p_ref, p_hbm, sems.at[0])]
    copies[0].start()
    w_ref[lanes(core * (R // 2), R // 2), :] = w_own_ref[...]
    w_ref[lanes(R // 2 - core * (R // 2), R // 2), :] = w_other_ref[...]
    qr = dot_high(f_ref[...], w_ref[...])
    q_ref[...] = qr[:R]
    r1, r2 = split2(qr[R:])
    weights = jnp.concatenate([r1, r1, r2, jnp.zeros_like(r1)], 0)
    for part, (base, m_ref) in enumerate(((core * HALF, m_own_ref), (HALF - core * HALF, m_other_ref))):
        for t in range(0, HALF, COLS):
            at, here = lanes(base + t, COLS), pl.ds(part * HALF + t, COLS)
            bt = bt_ref[at, :]
            out[here, :] = m_ref[t:t + COLS, :] - dot(jnp.concatenate([bt, bt], 1), weights)
            copies.append(pltpu.make_async_copy(out.at[here, :], e_hbm.at[at, :], sems.at[len(copies)]))
            copies[-1].start()
    for copy in copies:
        copy.wait()


def update(core, m_own, m_other, basis_t, factors, w_own, w_other, p_rows):
    return pl.pallas_call(
        update_kernel,
        in_specs=[SMEM] + [VMEM] * 7,
        out_specs=[HBM, VMEM, HBM],
        out_shape=[shape(DW, KV), shape(R, KV), shape(R, DW)],
        scratch_shapes=[
            pltpu.VMEM((R, KV), F32),
            pltpu.VMEM((DW, KV), F32),
            pltpu.SemaphoreType.DMA((1 + DW // COLS,)),
        ],
        compiler_params=LIMIT,
        name="update",
    )(core.reshape(1), m_own, m_other, basis_t, factors, w_own, w_other, p_rows)


def pair_kernel(w_ref, arrived_ref, after_ref, out_ref):
    del after_ref
    total = w_ref[...] + arrived_ref[...]
    for i in range(out_ref.shape[0]):
        out_ref[i] = total


def sum_pair(w, arrived, after, copies):
    return pl.pallas_call(
        pair_kernel,
        in_specs=[VMEM] * 2 + [ANY],
        out_specs=VMEM,
        out_shape=shape(copies, *w.shape),
        compiler_params=SMALL,
        name="sum_pair",
    )(w, arrived, after)


def exchange(parts, axes):
    return lax.all_to_all(parts, axes, split_axis=0, concat_axis=0, tiled=True)


def sum_kernel(parts_ref, out_ref):
    total = parts_ref[0]
    for i in range(1, parts_ref.shape[0]):
        total = total + parts_ref[i]
    for i in range(out_ref.shape[0]):
        out_ref[i] = total


def sum_parts(parts, copies):
    return pl.pallas_call(
        sum_kernel,
        in_specs=[VMEM],
        out_specs=VMEM,
        out_shape=shape(copies, *parts.shape[1:]),
        compiler_params=SMALL,
        name="sum_parts",
    )(parts)


def swap(array):
    return lax.ppermute(array, "c", SWAP)


def swap_y(array, mask):
    return lax.ppermute(array, "y", [(i, i ^ mask) for i in range(NY)])


def shards(inputs, out_grads, error_buffer, start_basis):
    core = lax.axis_index("c")
    arguments = (inputs, out_grads, error_buffer[0], start_basis.T)
    x, g, e, s_rows = [pltpu.with_memory_space_constraint(array, pltpu.HBM) for array in arguments]
    m_other, p_other, *rest = moment_of_other(core, x, g, e, s_rows)
    arrived = swap(p_other)
    e_own, x_own, g, s_rows = rest
    m_own, p_own = moment_of_own(x_own, g, e_own, s_rows)
    m_arrived = swap(m_other)

    parts = exchange(p_own + arrived, ("y", "x"))
    parts = exchange(sum_parts(parts, NZ), "z")
    own = exchange(sum_parts(parts, NY * NX), ("y", "x"))
    other = swap(own)
    w_own, w_other = own_term(core, own, m_own, m_arrived)

    arrived = swap(w_other)
    gram = other_gram(other, own_gram(own, w_own))
    w = sum_pair(w_own, arrived, gram, 1)[0]
    arrived = swap_y(w, 1)
    basis, factor1, part = first_round(core, own, other, gram, w)
    w = sum_pair(w, arrived, factor1, 1)[0]
    arrived = swap_y(w, 3)
    factor2, basis_t = second_factor(basis, part, w)
    w = sum_parts(exchange(sum_pair(w, arrived, factor2, NZ), "z"), 1)[0]
    p_rows, factors = finish(basis, factor1, factor2, w)
    error, q_rows, p_rows = update(core, m_own, m_other, basis_t, factors, w, swap(w), p_rows)
    return (p_rows.T, q_rows.T, error[None])


def solution(mesh):
    fine = Mesh(mesh.devices.reshape(NZ, NY, NC, NX), ("z", "y", "c", "x"))
    dp = ("z", "y", "c")
    in_specs = (P(dp, None), P(dp, "x"), P(dp, None, "x"), P("x", None))
    out_specs = (P(), P("x", None), P(dp, None, "x"))
    return jax.shard_map(shards, mesh=fine, in_specs=in_specs, out_specs=out_specs, check_vma=False)
```

```python
import jax
import jax.numpy as jnp
from jax import lax
from jax.experimental import pallas as pl
from jax.experimental.pallas import tpu as pltpu
from jax.sharding import Mesh, PartitionSpec as P

HIGH = lax.Precision.HIGHEST
NZ, NY, NC, NX = 8, 4, 2, 4
DW, KV, R, TOK = 4096, 256, 64, 384
HALF, BLOCKS = DW // 2, DW // 256
BF, F32 = jnp.bfloat16, jnp.float32
SWAP = [(0, 1), (1, 0)]
NN = (((1,), (0,)), ((), ()))
NT = (((1,), (1,)), ((), ()))
TN = (((0,), (0,)), ((), ()))
VMEM = pl.BlockSpec(memory_space=pltpu.VMEM)
SMEM = pl.BlockSpec(memory_space=pltpu.SMEM)
HBM = pl.BlockSpec(memory_space=pltpu.HBM)
ANY = pl.BlockSpec(memory_space=pl.ANY)
BESIDE = pl.CostEstimate(flops=10 ** 9, bytes_accessed=4 << 20, transcendentals=0)
LIMIT = pltpu.CompilerParams(vmem_limit_bytes=24 << 20)
SMALL = pltpu.CompilerParams(vmem_limit_bytes=8 << 20)


def shape(*dims, dtype=F32):
    return jax.ShapeDtypeStruct(dims, dtype)


def dot(a, b, dims=NN):
    return lax.dot_general(a, b, dims, preferred_element_type=F32)


def dot_high(a, b, dims=NN):
    return lax.dot_general(a, b, dims, precision=HIGH, preferred_element_type=F32)


def lanes(start, size):
    return pl.ds(pl.multiple_of(start, size), size)


def split2(x):
    high = x.astype(BF)
    return high, (x - high.astype(F32)).astype(BF)


def split3(x):
    high = x.astype(BF)
    rest = x - high.astype(F32)
    middle = rest.astype(BF)
    return high, middle, (rest - middle.astype(F32)).astype(BF)


COLS = 512
LOAD = 1024


def p_half(moment, basis, p_ref):
    s1, s2, s3 = split3(basis)
    none = jnp.zeros_like(s1)
    orders = (s3, s2, s1), (s2, s1, none), (s1, none, none)
    weights = jnp.concatenate([jnp.concatenate(order, 1) for order in orders], 0)
    t = dot(jnp.concatenate(split3(moment), 1), weights, NT).T
    rows = (t[:R] + t[R:2 * R]) + t[2 * R:]
    for i in range(BLOCKS):
        p_ref[i] = rows[:, i * 128:(i + 1) * 128]


def moment_kernel(core_ref, x_hbm, g_hbm, e_hbm, s_hbm, m_ref, p_ref, e_ref, x_ref, g_ref, s_ref, x_buf, sems):
    core = core_ref[0]
    steps = HALF // LOAD
    copies = [pltpu.make_async_copy(g_hbm, g_ref, sems.at[0]), pltpu.make_async_copy(s_hbm, s_ref, sems.at[1])]
    for base, x_to, e_to in ((HALF - core * HALF, x_buf, m_ref), (core * HALF, x_ref, e_ref)):
        for j in range(steps):
            at, to = lanes(base + j * LOAD, LOAD), pl.ds(j * LOAD, LOAD)
            copies.append(pltpu.make_async_copy(x_hbm.at[:, at], x_to.at[j], sems.at[len(copies)]))
            copies.append(pltpu.make_async_copy(e_hbm.at[at, :], e_to.at[to, :], sems.at[len(copies)]))
    for copy in copies:
        copy.start()
    copies[0].wait()
    copies[1].wait()
    g = g_ref[...]
    for j in range(steps):
        copies[2 + 2 * j].wait()
        copies[3 + 2 * j].wait()
        at = pl.ds(j * LOAD, LOAD)
        m_ref[at, :] = dot(x_buf[j], g, TN) + m_ref[at, :]
    p_half(m_ref[...], s_ref[...], p_ref)
    for copy in copies[2 + 2 * steps:]:
        copy.wait()


def moment_of_other(core, x, g, e, s_rows):
    steps = HALF // LOAD
    return pl.pallas_call(
        moment_kernel,
        in_specs=[SMEM, HBM, HBM, HBM, HBM],
        out_specs=[VMEM] * 6,
        out_shape=[
            shape(HALF, KV),
            shape(BLOCKS, R, 128),
            shape(HALF, KV),
            shape(steps, TOK, LOAD, dtype=BF),
            shape(TOK, KV, dtype=BF),
            shape(R, KV),
        ],
        scratch_shapes=[pltpu.VMEM((steps, TOK, LOAD), BF), pltpu.SemaphoreType.DMA((2 + 4 * steps,))],
        compiler_params=LIMIT,
        name="moment_other",
    )(core.reshape(1), x, g, e, s_rows)


def own_kernel(x_ref, g_ref, e_ref, s_ref, m_ref, p_ref):
    g = g_ref[...]
    for j in range(HALF // LOAD):
        at = pl.ds(j * LOAD, LOAD)
        m_ref[at, :] = dot(x_ref[j], g, TN) + e_ref[at, :]
    p_half(m_ref[...], s_ref[...], p_ref)


def moment_of_own(x, g, e, s_rows):
    return pl.pallas_call(
        own_kernel,
        in_specs=[VMEM] * 4,
        out_specs=[VMEM] * 2,
        out_shape=[shape(HALF, KV), shape(BLOCKS, R, 128)],
        compiler_params=LIMIT,
        cost_estimate=BESIDE,
        name="moment_own",
    )(x, g, e, s_rows)


def inverse_factor(gram):
    rows = lax.broadcasted_iota(jnp.int32, (8, 128), 0)
    lanes = lax.broadcasted_iota(jnp.int32, (8, 128), 1)
    zero = jnp.zeros((8, R), F32)
    groups = [
        jnp.where(lanes == rows + R + 8 * i, 1.0, jnp.concatenate([gram[8 * i:8 * i + 8], zero], axis=1))
        for i in range(R // 8)
    ]
    pivots = []
    for b in range(R // 8):
        columns = [
            [jnp.broadcast_to(groups[i][:, 8 * b + c:8 * b + c + 1], (8, 128)) for i in range(b, R // 8)]
            for c in range(8)
        ]
        diagonal = jnp.zeros((8, 128), F32)
        for j in range(8):
            head = columns[j][0]
            pivot = jnp.broadcast_to(head[j:j + 1], (8, 128))
            inverse = 1.0 / pivot
            diagonal = jnp.where(rows == j, pivot, diagonal)
            factors = [column * inverse for column in columns[j]]
            factors[0] = jnp.where(rows > j, factors[0], 0.0)
            row = jnp.broadcast_to(groups[b][j:j + 1], (8, 128))
            for c in range(j + 1, 8):
                weight = jnp.broadcast_to(head[c:c + 1], (8, 128))
                columns[c] = [column - factor * weight for column, factor in zip(columns[c], factors)]
            for i in range(b, R // 8):
                groups[i] = groups[i] - factors[i - b] * row
        pivots.append(diagonal)
    return jnp.concatenate([(a * lax.rsqrt(d))[:, R:] for a, d in zip(groups, pivots)], axis=0)


def gram_matrix(rows):
    a1, a2, a3 = split3(rows)
    t = dot(jnp.concatenate([a1, a2, a3], 0), jnp.concatenate([a1, a2], 0), NT)
    t21, t31 = t[R:2 * R, :R], t[2 * R:, :R]
    return t[:R, :R] + ((t21 + t21.T) + (t[R:2 * R, R:] + (t31 + t31.T)))


def wide(blocks_ref):
    return jnp.concatenate([blocks_ref[j] for j in range(BLOCKS)], axis=1)


def product(p, m):
    p1, p2, p3 = split3(p)
    m1, m2, m3 = split3(m)
    t1 = dot(jnp.concatenate([p1, p2, p3], 0), m1)
    t2 = dot(jnp.concatenate([p1, p2], 0), m2)
    return t1[:R] + ((t1[R:2 * R] + t2[:R]) + ((t1[2 * R:] + t2[R:]) + dot(p1, m3)))


def own_term_kernel(core_ref, own_ref, m_ref, arrived_ref, w_own_ref, w_other_ref, w_ref):
    w_ref[...] = product(wide(own_ref), m_ref[...] + arrived_ref[...])
    mine = core_ref[0] * (R // 2)
    w_own_ref[...] = w_ref[lanes(mine, R // 2), :]
    w_other_ref[...] = w_ref[lanes(R // 2 - mine, R // 2), :]


def own_term(core, own, moment, arrived):
    return pl.pallas_call(
        own_term_kernel,
        in_specs=[SMEM] + [VMEM] * 3,
        out_specs=[VMEM] * 2,
        out_shape=[shape(R // 2, KV), shape(R // 2, KV)],
        scratch_shapes=[pltpu.VMEM((R, KV), F32)],
        compiler_params=LIMIT,
        cost_estimate=BESIDE,
        name="own_term",
    )(core.reshape(1), own, moment, arrived)


def own_gram_kernel(own_ref, after_ref, gram_ref):
    del after_ref
    gram_ref[...] = gram_matrix(wide(own_ref))


def own_gram(own, after):
    return pl.pallas_call(
        own_gram_kernel,
        in_specs=[VMEM, ANY],
        out_specs=VMEM,
        out_shape=shape(R, R),
        compiler_params=LIMIT,
        cost_estimate=BESIDE,
        name="own_gram",
    )(own, after)


def other_gram_kernel(other_ref, part_ref, gram_ref):
    gram_ref[...] = part_ref[...] + gram_matrix(wide(other_ref))


def other_gram(other, part):
    return pl.pallas_call(
        other_gram_kernel,
        in_specs=[VMEM, VMEM],
        out_specs=VMEM,
        out_shape=shape(R, R),
        compiler_params=LIMIT,
        cost_estimate=BESIDE,
        name="other_gram",
    )(other, part)


def first_round_kernel(core_ref, own_ref, other_ref, gram_ref, after_ref, b_ref, l_ref, part_ref):
    del after_ref
    core = core_ref[0]
    for j in range(BLOCKS):
        b_ref[:, lanes(core * HALF + j * 128, 128)] = own_ref[j]
        b_ref[:, lanes(HALF - core * HALF + j * 128, 128)] = other_ref[j]
    factor = inverse_factor(gram_ref[...])
    l_ref[...] = factor
    f1, f2, f3 = split3(factor)
    p1, p2, p3 = split3(b_ref[...])
    small = dot(jnp.concatenate([f2, f1, f2, f3, f1], 1), jnp.concatenate([p1, p2, p2, p1, p3], 0))
    b_ref[...] = dot(f1, p1) + small
    part_ref[...] = gram_matrix(b_ref[:, :LOAD])


def first_round(core, own, other, gram, after):
    return pl.pallas_call(
        first_round_kernel,
        in_specs=[SMEM] + [VMEM] * 3 + [ANY],
        out_specs=[VMEM] * 3,
        out_shape=[shape(R, DW), shape(R, R), shape(R, R)],
        compiler_params=LIMIT,
        cost_estimate=BESIDE,
        name="first_round",
    )(core.reshape(1), own, other, gram, after)


def second_factor_kernel(b_ref, part_ref, after_ref, l_ref, bt_ref):
    del after_ref
    l_ref[...] = inverse_factor(part_ref[...] + gram_matrix(b_ref[:, LOAD:]))
    bt_ref[...] = jnp.concatenate(split2(b_ref[...]), 0).T


def second_factor(basis, part, after):
    return pl.pallas_call(
        second_factor_kernel,
        in_specs=[VMEM, VMEM, ANY],
        out_specs=[VMEM] * 2,
        out_shape=[shape(R, R), shape(DW, 2 * R, dtype=BF)],
        compiler_params=LIMIT,
        cost_estimate=BESIDE,
        name="second_factor",
    )(basis, part, after)


def finish_kernel(b_ref, l1_ref, l2_ref, after_ref, p_ref, f_ref):
    del after_ref
    factor = l2_ref[...]
    both = dot_high(factor, l1_ref[...]) * (1.0 / (NZ * NY * NC))
    f_ref[:R, :] = both
    f_ref[R:, :] = dot_high(factor, both, TN)
    f1, f2, f3 = split3(factor)
    b1, b2, b3 = split3(b_ref[...])
    f = jnp.concatenate([f1, f2, f3, f1, f2, f1], 1)
    p_ref[...] = dot(f, jnp.concatenate([b1, b1, b1, b2, b2, b3], 0))


def finish(basis, factor1, factor2, after):
    return pl.pallas_call(
        finish_kernel,
        in_specs=[VMEM] * 3 + [ANY],
        out_specs=[VMEM] * 2,
        out_shape=[shape(R, DW), shape(2 * R, R)],
        compiler_params=LIMIT,
        cost_estimate=BESIDE,
        name="finish",
    )(basis, factor1, factor2, after)


def update_kernel(core_ref, m_own_ref, m_other_ref, bt_ref, f_ref, w_own_ref, w_other_ref, p_ref, e_hbm, q_hbm, p_hbm, w_ref, q_ref, out, sems):
    core = core_ref[0]
    copies = [pltpu.make_async_copy(p_ref, p_hbm, sems.at[0]), pltpu.make_async_copy(q_ref, q_hbm, sems.at[1])]
    copies[0].start()
    w_ref[lanes(core * (R // 2), R // 2), :] = w_own_ref[...]
    w_ref[lanes(R // 2 - core * (R // 2), R // 2), :] = w_other_ref[...]
    qr = dot_high(f_ref[...], w_ref[...])
    q_ref[...] = qr[:R]
    copies[1].start()
    r1, r2 = split2(qr[R:])
    weights = jnp.concatenate([r1, r1, r2, jnp.zeros_like(r1)], 0)
    for part, (base, m_ref) in enumerate(((core * HALF, m_own_ref), (HALF - core * HALF, m_other_ref))):
        for t in range(0, HALF, COLS):
            at, here = lanes(base + t, COLS), pl.ds(part * HALF + t, COLS)
            bt = bt_ref[at, :]
            out[here, :] = m_ref[t:t + COLS, :] - dot(jnp.concatenate([bt, bt], 1), weights)
            copies.append(pltpu.make_async_copy(out.at[here, :], e_hbm.at[at, :], sems.at[len(copies)]))
            copies[-1].start()
    for copy in copies:
        copy.wait()


def update(core, m_own, m_other, basis_t, factors, w_own, w_other, p_rows):
    return pl.pallas_call(
        update_kernel,
        in_specs=[SMEM] + [VMEM] * 7,
        out_specs=[HBM] * 3,
        out_shape=[shape(DW, KV), shape(R, KV), shape(R, DW)],
        scratch_shapes=[
            pltpu.VMEM((R, KV), F32),
            pltpu.VMEM((R, KV), F32),
            pltpu.VMEM((DW, KV), F32),
            pltpu.SemaphoreType.DMA((2 + DW // COLS,)),
        ],
        compiler_params=LIMIT,
        name="update",
    )(core.reshape(1), m_own, m_other, basis_t, factors, w_own, w_other, p_rows)


def pair_kernel(w_ref, arrived_ref, after_ref, out_ref):
    del after_ref
    total = w_ref[...] + arrived_ref[...]
    for i in range(out_ref.shape[0]):
        out_ref[i] = total


def sum_pair(w, arrived, after, copies):
    return pl.pallas_call(
        pair_kernel,
        in_specs=[VMEM] * 2 + [ANY],
        out_specs=VMEM,
        out_shape=shape(copies, *w.shape),
        compiler_params=SMALL,
        name="sum_pair",
    )(w, arrived, after)


def exchange(parts, axes):
    return lax.all_to_all(parts, axes, split_axis=0, concat_axis=0, tiled=True)


def sum_kernel(parts_ref, out_ref):
    total = parts_ref[0]
    for i in range(1, parts_ref.shape[0]):
        total = total + parts_ref[i]
    for i in range(out_ref.shape[0]):
        out_ref[i] = total


def sum_parts(parts, copies):
    return pl.pallas_call(
        sum_kernel,
        in_specs=[VMEM],
        out_specs=VMEM,
        out_shape=shape(copies, *parts.shape[1:]),
        compiler_params=SMALL,
        name="sum_parts",
    )(parts)


def swap(array):
    return lax.ppermute(array, "c", SWAP)


def swap_y(array, mask):
    return lax.ppermute(array, "y", [(i, i ^ mask) for i in range(NY)])


def shards(inputs, out_grads, error_buffer, start_basis):
    core = lax.axis_index("c")
    arguments = (inputs, out_grads, error_buffer[0], start_basis.T)
    x, g, e, s_rows = [pltpu.with_memory_space_constraint(array, pltpu.HBM) for array in arguments]
    m_other, p_other, *rest = moment_of_other(core, x, g, e, s_rows)
    arrived = swap(p_other)
    e_own, x_own, g, s_rows = rest
    m_own, p_own = moment_of_own(x_own, g, e_own, s_rows)
    m_arrived = swap(m_other)

    parts = exchange(p_own + arrived, ("y", "x"))
    parts = exchange(sum_parts(parts, NZ), "z")
    own = exchange(sum_parts(parts, NY * NX), ("y", "x"))
    other = swap(own)
    w_own, w_other = own_term(core, own, m_own, m_arrived)

    arrived = swap(w_other)
    gram = other_gram(other, own_gram(own, w_own))
    w = sum_pair(w_own, arrived, gram, 1)[0]
    arrived = swap_y(w, 1)
    basis, factor1, part = first_round(core, own, other, gram, w)
    w = sum_pair(w, arrived, factor1, 1)[0]
    arrived = swap_y(w, 3)
    factor2, basis_t = second_factor(basis, part, w)
    w = sum_parts(exchange(sum_pair(w, arrived, factor2, NZ), "z"), 1)[0]
    p_rows, factors = finish(basis, factor1, factor2, w)
    error, q_rows, p_rows = update(core, m_own, m_other, basis_t, factors, w, swap(w), p_rows)
    return (p_rows.T, q_rows.T, error[None])


def solution(mesh):
    fine = Mesh(mesh.devices.reshape(NZ, NY, NC, NX), ("z", "y", "c", "x"))
    dp = ("z", "y", "c")
    in_specs = (P(dp, None), P(dp, "x"), P(dp, None, "x"), P("x", None))
    out_specs = (P(), P("x", None), P(dp, None, "x"))
    return jax.shard_map(shards, mesh=fine, in_specs=in_specs, out_specs=out_specs, check_vma=False)
```

```python
import jax
import jax.numpy as jnp
from jax import lax
from jax.experimental import pallas as pl
from jax.experimental.pallas import tpu as pltpu
from jax.sharding import Mesh, PartitionSpec as P

HIGH = lax.Precision.HIGHEST
NZ, NY, NC, NX = 8, 4, 2, 4
DW, KV, R, TOK = 4096, 256, 64, 384
HALF, BLOCKS = DW // 2, DW // 256
BF, F32 = jnp.bfloat16, jnp.float32
SWAP = [(0, 1), (1, 0)]
NN = (((1,), (0,)), ((), ()))
NT = (((1,), (1,)), ((), ()))
TN = (((0,), (0,)), ((), ()))
VMEM = pl.BlockSpec(memory_space=pltpu.VMEM)
HBM = pl.BlockSpec(memory_space=pltpu.HBM)
ANY = pl.BlockSpec(memory_space=pl.ANY)
BESIDE = pl.CostEstimate(flops=10 ** 9, bytes_accessed=4 << 20, transcendentals=0)
LIMIT = pltpu.CompilerParams(vmem_limit_bytes=24 << 20)
SMALL = pltpu.CompilerParams(vmem_limit_bytes=8 << 20)


def shape(*dims, dtype=F32):
    return jax.ShapeDtypeStruct(dims, dtype)


def dot(a, b, dims=NN):
    return lax.dot_general(a, b, dims, preferred_element_type=F32)


def dot_high(a, b, dims=NN):
    return lax.dot_general(a, b, dims, precision=HIGH, preferred_element_type=F32)


def lanes(start, size):
    return pl.ds(pl.multiple_of(start, size), size)


def split2(x):
    high = x.astype(BF)
    return high, (x - high.astype(F32)).astype(BF)


def split3(x):
    high = x.astype(BF)
    rest = x - high.astype(F32)
    middle = rest.astype(BF)
    return high, middle, (rest - middle.astype(F32)).astype(BF)


COLS = 512
LOAD = 1024


def p_half(moment, basis, p_ref):
    s1, s2, s3 = split3(basis)
    none = jnp.zeros_like(s1)
    orders = (s3, s2, s1), (s2, s1, none), (s1, none, none)
    weights = jnp.concatenate([jnp.concatenate(order, 1) for order in orders], 0)
    t = dot(jnp.concatenate(split3(moment), 1), weights, NT).T
    rows = (t[:R] + t[R:2 * R]) + t[2 * R:]
    for i in range(BLOCKS):
        p_ref[i] = rows[:, i * 128:(i + 1) * 128]


def moment_kernel(x_hbm, g_hbm, e_hbm, s_hbm, m_ref, p_ref, e_ref, x_ref, g_ref, s_ref, x_buf, sems):
    core = lax.axis_index("c")
    steps = HALF // LOAD
    copies = [pltpu.make_async_copy(g_hbm, g_ref, sems.at[0]), pltpu.make_async_copy(s_hbm, s_ref, sems.at[1])]
    for base, x_to, e_to in ((HALF - core * HALF, x_buf, m_ref), (core * HALF, x_ref, e_ref)):
        for j in range(steps):
            at, to = lanes(base + j * LOAD, LOAD), pl.ds(j * LOAD, LOAD)
            copies.append(pltpu.make_async_copy(x_hbm.at[:, at], x_to.at[j], sems.at[len(copies)]))
            copies.append(pltpu.make_async_copy(e_hbm.at[at, :], e_to.at[to, :], sems.at[len(copies)]))
    for copy in copies:
        copy.start()
    copies[0].wait()
    copies[1].wait()
    g = g_ref[...]
    for j in range(steps):
        copies[2 + 2 * j].wait()
        copies[3 + 2 * j].wait()
        at = pl.ds(j * LOAD, LOAD)
        m_ref[at, :] = dot(x_buf[j], g, TN) + m_ref[at, :]
    p_half(m_ref[...], s_ref[...], p_ref)
    for copy in copies[2 + 2 * steps:]:
        copy.wait()


def moment_of_other(x, g, e, s_rows):
    steps = HALF // LOAD
    return pl.pallas_call(
        moment_kernel,
        in_specs=[HBM] * 4,
        out_specs=[VMEM] * 6,
        out_shape=[
            shape(HALF, KV),
            shape(BLOCKS, R, 128),
            shape(HALF, KV),
            shape(steps, TOK, LOAD, dtype=BF),
            shape(TOK, KV, dtype=BF),
            shape(R, KV),
        ],
        scratch_shapes=[pltpu.VMEM((steps, TOK, LOAD), BF), pltpu.SemaphoreType.DMA((2 + 4 * steps,))],
        compiler_params=LIMIT,
        name="moment_other",
    )(x, g, e, s_rows)


def own_kernel(x_ref, g_ref, e_ref, s_ref, m_ref, p_ref):
    g = g_ref[...]
    for j in range(HALF // LOAD):
        at = pl.ds(j * LOAD, LOAD)
        m_ref[at, :] = dot(x_ref[j], g, TN) + e_ref[at, :]
    p_half(m_ref[...], s_ref[...], p_ref)


def moment_of_own(x, g, e, s_rows):
    return pl.pallas_call(
        own_kernel,
        in_specs=[VMEM] * 4,
        out_specs=[VMEM] * 2,
        out_shape=[shape(HALF, KV), shape(BLOCKS, R, 128)],
        compiler_params=LIMIT,
        cost_estimate=BESIDE,
        name="moment_own",
    )(x, g, e, s_rows)


def inverse_factor(gram):
    rows = lax.broadcasted_iota(jnp.int32, (8, 128), 0)
    lanes = lax.broadcasted_iota(jnp.int32, (8, 128), 1)
    zero = jnp.zeros((8, R), F32)
    groups = [
        jnp.where(lanes == rows + R + 8 * i, 1.0, jnp.concatenate([gram[8 * i:8 * i + 8], zero], axis=1))
        for i in range(R // 8)
    ]
    pivots = []
    for b in range(R // 8):
        columns = [
            [jnp.broadcast_to(groups[i][:, 8 * b + c:8 * b + c + 1], (8, 128)) for i in range(b, R // 8)]
            for c in range(8)
        ]
        diagonal = jnp.zeros((8, 128), F32)
        for j in range(8):
            head = columns[j][0]
            pivot = jnp.broadcast_to(head[j:j + 1], (8, 128))
            inverse = 1.0 / pivot
            diagonal = jnp.where(rows == j, pivot, diagonal)
            factors = [column * inverse for column in columns[j]]
            factors[0] = jnp.where(rows > j, factors[0], 0.0)
            row = jnp.broadcast_to(groups[b][j:j + 1], (8, 128))
            for c in range(j + 1, 8):
                weight = jnp.broadcast_to(head[c:c + 1], (8, 128))
                columns[c] = [column - factor * weight for column, factor in zip(columns[c], factors)]
            for i in range(b, R // 8):
                groups[i] = groups[i] - factors[i - b] * row
        pivots.append(diagonal)
    return jnp.concatenate([(a * lax.rsqrt(d))[:, R:] for a, d in zip(groups, pivots)], axis=0)


def gram_matrix(rows):
    a1, a2, a3 = split3(rows)
    t = dot(jnp.concatenate([a1, a2, a3], 0), jnp.concatenate([a1, a2], 0), NT)
    t21, t31 = t[R:2 * R, :R], t[2 * R:, :R]
    return t[:R, :R] + ((t21 + t21.T) + (t[R:2 * R, R:] + (t31 + t31.T)))


def wide(blocks_ref):
    return jnp.concatenate([blocks_ref[j] for j in range(BLOCKS)], axis=1)


def product(p, m):
    p1, p2, p3 = split3(p)
    m1, m2, m3 = split3(m)
    t1 = dot(jnp.concatenate([p1, p2, p3], 0), m1)
    t2 = dot(jnp.concatenate([p1, p2], 0), m2)
    return t1[:R] + ((t1[R:2 * R] + t2[:R]) + ((t1[2 * R:] + t2[R:]) + dot(p1, m3)))


def own_term_kernel(own_ref, m_ref, arrived_ref, w_own_ref, w_other_ref, w_ref):
    w_ref[...] = product(wide(own_ref), m_ref[...] + arrived_ref[...])
    mine = lax.axis_index("c") * (R // 2)
    w_own_ref[...] = w_ref[lanes(mine, R // 2), :]
    w_other_ref[...] = w_ref[lanes(R // 2 - mine, R // 2), :]


def own_term(own, moment, arrived):
    return pl.pallas_call(
        own_term_kernel,
        in_specs=[VMEM] * 3,
        out_specs=[VMEM] * 2,
        out_shape=[shape(R // 2, KV), shape(R // 2, KV)],
        scratch_shapes=[pltpu.VMEM((R, KV), F32)],
        compiler_params=LIMIT,
        cost_estimate=BESIDE,
        name="own_term",
    )(own, moment, arrived)


def own_gram_kernel(own_ref, after_ref, gram_ref):
    del after_ref
    gram_ref[...] = gram_matrix(wide(own_ref))


def own_gram(own, after):
    return pl.pallas_call(
        own_gram_kernel,
        in_specs=[VMEM, ANY],
        out_specs=VMEM,
        out_shape=shape(R, R),
        compiler_params=LIMIT,
        cost_estimate=BESIDE,
        name="own_gram",
    )(own, after)


def other_gram_kernel(other_ref, part_ref, gram_ref):
    gram_ref[...] = part_ref[...] + gram_matrix(wide(other_ref))


def other_gram(other, part):
    return pl.pallas_call(
        other_gram_kernel,
        in_specs=[VMEM, VMEM],
        out_specs=VMEM,
        out_shape=shape(R, R),
        compiler_params=LIMIT,
        cost_estimate=BESIDE,
        name="other_gram",
    )(other, part)


def first_round_kernel(own_ref, other_ref, gram_ref, after_ref, b_ref, l_ref, part_ref):
    del after_ref
    core = lax.axis_index("c")
    for j in range(BLOCKS):
        b_ref[:, lanes(core * HALF + j * 128, 128)] = own_ref[j]
        b_ref[:, lanes(HALF - core * HALF + j * 128, 128)] = other_ref[j]
    factor = inverse_factor(gram_ref[...])
    l_ref[...] = factor
    f1, f2, f3 = split3(factor)
    p1, p2, p3 = split3(b_ref[...])
    small = dot(jnp.concatenate([f2, f1, f2, f3, f1], 1), jnp.concatenate([p1, p2, p2, p1, p3], 0))
    b_ref[...] = dot(f1, p1) + small
    part_ref[...] = gram_matrix(b_ref[:, :LOAD])


def first_round(own, other, gram, after):
    return pl.pallas_call(
        first_round_kernel,
        in_specs=[VMEM] * 3 + [ANY],
        out_specs=[VMEM] * 3,
        out_shape=[shape(R, DW), shape(R, R), shape(R, R)],
        compiler_params=LIMIT,
        cost_estimate=BESIDE,
        name="first_round",
    )(own, other, gram, after)


def second_factor_kernel(b_ref, part_ref, after_ref, l_ref, bt_ref):
    del after_ref
    l_ref[...] = inverse_factor(part_ref[...] + gram_matrix(b_ref[:, LOAD:]))
    bt_ref[...] = jnp.concatenate(split2(b_ref[...]), 0).T


def second_factor(basis, part, after):
    return pl.pallas_call(
        second_factor_kernel,
        in_specs=[VMEM, VMEM, ANY],
        out_specs=[VMEM] * 2,
        out_shape=[shape(R, R), shape(DW, 2 * R, dtype=BF)],
        compiler_params=LIMIT,
        cost_estimate=BESIDE,
        name="second_factor",
    )(basis, part, after)


def finish_kernel(b_ref, l1_ref, l2_ref, after_ref, p_ref, f_ref):
    del after_ref
    factor = l2_ref[...]
    both = dot_high(factor, l1_ref[...]) * (1.0 / (NZ * NY * NC))
    f_ref[:R, :] = both
    f_ref[R:, :] = dot_high(factor, both, TN)
    f1, f2, f3 = split3(factor)
    b1, b2, b3 = split3(b_ref[...])
    f = jnp.concatenate([f1, f2, f3, f1, f2, f1], 1)
    p_ref[...] = dot(f, jnp.concatenate([b1, b1, b1, b2, b2, b3], 0))


def finish(basis, factor1, factor2, after):
    return pl.pallas_call(
        finish_kernel,
        in_specs=[VMEM] * 3 + [ANY],
        out_specs=[VMEM] * 2,
        out_shape=[shape(R, DW), shape(2 * R, R)],
        compiler_params=LIMIT,
        cost_estimate=BESIDE,
        name="finish",
    )(basis, factor1, factor2, after)


def update_kernel(m_own_ref, m_other_ref, bt_ref, f_ref, w_own_ref, w_other_ref, p_ref, e_hbm, q_hbm, p_hbm, w_ref, q_ref, out, sems):
    core = lax.axis_index("c")
    copies = [pltpu.make_async_copy(p_ref, p_hbm, sems.at[0]), pltpu.make_async_copy(q_ref, q_hbm, sems.at[1])]
    copies[0].start()
    w_ref[lanes(core * (R // 2), R // 2), :] = w_own_ref[...]
    w_ref[lanes(R // 2 - core * (R // 2), R // 2), :] = w_other_ref[...]
    qr = dot_high(f_ref[...], w_ref[...])
    q_ref[...] = qr[:R]
    copies[1].start()
    r1, r2 = split2(qr[R:])
    weights = jnp.concatenate([r1, r1, r2, jnp.zeros_like(r1)], 0)
    for part, (base, m_ref) in enumerate(((core * HALF, m_own_ref), (HALF - core * HALF, m_other_ref))):
        for t in range(0, HALF, COLS):
            at, here = lanes(base + t, COLS), pl.ds(part * HALF + t, COLS)
            bt = bt_ref[at, :]
            out[here, :] = m_ref[t:t + COLS, :] - dot(jnp.concatenate([bt, bt], 1), weights)
            copies.append(pltpu.make_async_copy(out.at[here, :], e_hbm.at[at, :], sems.at[len(copies)]))
            copies[-1].start()
    for copy in copies:
        copy.wait()


def update(m_own, m_other, basis_t, factors, w_own, w_other, p_rows):
    return pl.pallas_call(
        update_kernel,
        in_specs=[VMEM] * 7,
        out_specs=[HBM] * 3,
        out_shape=[shape(DW, KV), shape(R, KV), shape(R, DW)],
        scratch_shapes=[
            pltpu.VMEM((R, KV), F32),
            pltpu.VMEM((R, KV), F32),
            pltpu.VMEM((DW, KV), F32),
            pltpu.SemaphoreType.DMA((2 + DW // COLS,)),
        ],
        compiler_params=LIMIT,
        name="update",
    )(m_own, m_other, basis_t, factors, w_own, w_other, p_rows)


def pair_kernel(w_ref, arrived_ref, after_ref, out_ref):
    del after_ref
    total = w_ref[...] + arrived_ref[...]
    for i in range(out_ref.shape[0]):
        out_ref[i] = total


def sum_pair(w, arrived, after, copies):
    return pl.pallas_call(
        pair_kernel,
        in_specs=[VMEM] * 2 + [ANY],
        out_specs=VMEM,
        out_shape=shape(copies, *w.shape),
        compiler_params=SMALL,
        name="sum_pair",
    )(w, arrived, after)


def exchange(parts, axes):
    return lax.all_to_all(parts, axes, split_axis=0, concat_axis=0, tiled=True)


def sum_kernel(parts_ref, out_ref):
    total = parts_ref[0]
    for i in range(1, parts_ref.shape[0]):
        total = total + parts_ref[i]
    for i in range(out_ref.shape[0]):
        out_ref[i] = total


def sum_parts(parts, copies):
    return pl.pallas_call(
        sum_kernel,
        in_specs=[VMEM],
        out_specs=VMEM,
        out_shape=shape(copies, *parts.shape[1:]),
        compiler_params=SMALL,
        name="sum_parts",
    )(parts)


def swap(array):
    return lax.ppermute(array, "c", SWAP)


def swap_y(array, mask):
    return lax.ppermute(array, "y", [(i, i ^ mask) for i in range(NY)])


def shards(inputs, out_grads, error_buffer, start_basis):
    arguments = (inputs, out_grads, error_buffer[0], start_basis.T)
    x, g, e, s_rows = [pltpu.with_memory_space_constraint(array, pltpu.HBM) for array in arguments]
    m_other, p_other, *rest = moment_of_other(x, g, e, s_rows)
    arrived = swap(p_other)
    e_own, x_own, g, s_rows = rest
    m_own, p_own = moment_of_own(x_own, g, e_own, s_rows)
    m_arrived = swap(m_other)

    parts = exchange(p_own + arrived, ("y", "x"))
    parts = exchange(sum_parts(parts, NZ), "z")
    own = exchange(sum_parts(parts, NY * NX), ("y", "x"))
    other = swap(own)
    w_own, w_other = own_term(own, m_own, m_arrived)

    arrived = swap(w_other)
    gram = other_gram(other, own_gram(own, w_own))
    w = sum_pair(w_own, arrived, gram, 1)[0]
    arrived = swap_y(w, 1)
    basis, factor1, part = first_round(own, other, gram, w)
    w = sum_pair(w, arrived, factor1, 1)[0]
    arrived = swap_y(w, 3)
    factor2, basis_t = second_factor(basis, part, w)
    w = sum_parts(exchange(sum_pair(w, arrived, factor2, NZ), "z"), 1)[0]
    p_rows, factors = finish(basis, factor1, factor2, w)
    error, q_rows, p_rows = update(m_own, m_other, basis_t, factors, w, swap(w), p_rows)
    return (p_rows.T, q_rows.T, error[None])


def solution(mesh):
    fine = Mesh(mesh.devices.reshape(NZ, NY, NC, NX), ("z", "y", "c", "x"))
    dp = ("z", "y", "c")
    in_specs = (P(dp, None), P(dp, "x"), P(dp, None, "x"), P("x", None))
    out_specs = (P(), P("x", None), P(dp, None, "x"))
    return jax.shard_map(shards, mesh=fine, in_specs=in_specs, out_specs=out_specs, check_vma=False)
```

```python
import functools

import jax
import jax.numpy as jnp
from jax import lax
from jax.experimental import pallas as pl
from jax.experimental.pallas import tpu as pltpu
from jax.sharding import Mesh, PartitionSpec as P

HIGH = lax.Precision.HIGHEST
NZ, NY, NC, NX = 8, 4, 2, 4
DW, KV, R, TOK = 4096, 256, 64, 384
HALF, BLOCKS = DW // 2, DW // 256
BF, F32 = jnp.bfloat16, jnp.float32
SWAP = [(0, 1), (1, 0)]
NN = (((1,), (0,)), ((), ()))
NT = (((1,), (1,)), ((), ()))
TN = (((0,), (0,)), ((), ()))
VMEM = pl.BlockSpec(memory_space=pltpu.VMEM)
HBM = pl.BlockSpec(memory_space=pltpu.HBM)
ANY = pl.BlockSpec(memory_space=pl.ANY)
BESIDE = pl.CostEstimate(flops=10 ** 9, bytes_accessed=4 << 20, transcendentals=0)
LIMIT = pltpu.CompilerParams(vmem_limit_bytes=24 << 20)
SMALL = pltpu.CompilerParams(vmem_limit_bytes=8 << 20)


def shape(*dims, dtype=F32):
    return jax.ShapeDtypeStruct(dims, dtype)


def dot(a, b, dims=NN):
    return lax.dot_general(a, b, dims, preferred_element_type=F32)


def dot_high(a, b, dims=NN):
    return lax.dot_general(a, b, dims, precision=HIGH, preferred_element_type=F32)


def lanes(start, size):
    return pl.ds(pl.multiple_of(start, size), size)


def split2(x):
    high = x.astype(BF)
    return high, (x - high.astype(F32)).astype(BF)


def split3(x):
    high = x.astype(BF)
    rest = x - high.astype(F32)
    middle = rest.astype(BF)
    return high, middle, (rest - middle.astype(F32)).astype(BF)


COLS = 512
LOAD = 1024


def p_half(moment, basis, p_ref):
    s1, s2, s3 = split3(basis)
    none = jnp.zeros_like(s1)
    orders = (s3, s2, s1), (s2, s1, none), (s1, none, none)
    weights = jnp.concatenate([jnp.concatenate(order, 1) for order in orders], 0)
    t = dot(jnp.concatenate(split3(moment), 1), weights, NT).T
    rows = (t[:R] + t[R:2 * R]) + t[2 * R:]
    for i in range(BLOCKS):
        p_ref[i] = rows[:, i * 128:(i + 1) * 128]


def moment_kernel(x_hbm, g_hbm, e_hbm, s_hbm, m_ref, p_ref, e_ref, x_ref, g_ref, s_ref, x_buf, sems):
    core = lax.axis_index("c")
    steps = HALF // LOAD
    copies = [pltpu.make_async_copy(g_hbm, g_ref, sems.at[0]), pltpu.make_async_copy(s_hbm, s_ref, sems.at[1])]
    for base, x_to, e_to in ((HALF - core * HALF, x_buf, m_ref), (core * HALF, x_ref, e_ref)):
        for j in range(steps):
            at, to = lanes(base + j * LOAD, LOAD), pl.ds(j * LOAD, LOAD)
            copies.append(pltpu.make_async_copy(x_hbm.at[:, at], x_to.at[j], sems.at[len(copies)]))
            copies.append(pltpu.make_async_copy(e_hbm.at[at, :], e_to.at[to, :], sems.at[len(copies)]))
    for copy in copies:
        copy.start()
    copies[0].wait()
    copies[1].wait()
    g = g_ref[...]
    for j in range(steps):
        copies[2 + 2 * j].wait()
        copies[3 + 2 * j].wait()
        at = pl.ds(j * LOAD, LOAD)
        m_ref[at, :] = dot(x_buf[j], g, TN) + m_ref[at, :]
    p_half(m_ref[...], s_ref[...], p_ref)
    for copy in copies[2 + 2 * steps:]:
        copy.wait()


def moment_of_other(x, g, e, s_rows):
    steps = HALF // LOAD
    return pl.pallas_call(
        moment_kernel,
        in_specs=[HBM] * 4,
        out_specs=[VMEM] * 6,
        out_shape=[
            shape(HALF, KV),
            shape(BLOCKS, R, 128),
            shape(HALF, KV),
            shape(steps, TOK, LOAD, dtype=BF),
            shape(TOK, KV, dtype=BF),
            shape(R, KV),
        ],
        scratch_shapes=[pltpu.VMEM((steps, TOK, LOAD), BF), pltpu.SemaphoreType.DMA((2 + 4 * steps,))],
        compiler_params=LIMIT,
        name="moment_other",
    )(x, g, e, s_rows)


def own_kernel(x_ref, g_ref, e_ref, s_ref, m_ref, p_ref):
    g = g_ref[...]
    for j in range(HALF // LOAD):
        at = pl.ds(j * LOAD, LOAD)
        m_ref[at, :] = dot(x_ref[j], g, TN) + e_ref[at, :]
    p_half(m_ref[...], s_ref[...], p_ref)


def moment_of_own(x, g, e, s_rows):
    return pl.pallas_call(
        own_kernel,
        in_specs=[VMEM] * 4,
        out_specs=[VMEM] * 2,
        out_shape=[shape(HALF, KV), shape(BLOCKS, R, 128)],
        compiler_params=LIMIT,
        cost_estimate=BESIDE,
        name="moment_own",
    )(x, g, e, s_rows)


def inverse_factor(gram):
    rows = lax.broadcasted_iota(jnp.int32, (8, 128), 0)
    lanes = lax.broadcasted_iota(jnp.int32, (8, 128), 1)
    zero = jnp.zeros((8, R), F32)
    groups = [
        jnp.where(lanes == rows + R + 8 * i, 1.0, jnp.concatenate([gram[8 * i:8 * i + 8], zero], axis=1))
        for i in range(R // 8)
    ]
    pivots = []
    for b in range(R // 8):
        columns = [
            [jnp.broadcast_to(groups[i][:, 8 * b + c:8 * b + c + 1], (8, 128)) for i in range(b, R // 8)]
            for c in range(8)
        ]
        diagonal = jnp.zeros((8, 128), F32)
        for j in range(8):
            head = columns[j][0]
            pivot = jnp.broadcast_to(head[j:j + 1], (8, 128))
            inverse = 1.0 / pivot
            diagonal = jnp.where(rows == j, pivot, diagonal)
            factors = [column * inverse for column in columns[j]]
            factors[0] = jnp.where(rows > j, factors[0], 0.0)
            row = jnp.broadcast_to(groups[b][j:j + 1], (8, 128))
            for c in range(j + 1, 8):
                weight = jnp.broadcast_to(head[c:c + 1], (8, 128))
                columns[c] = [column - factor * weight for column, factor in zip(columns[c], factors)]
            for i in range(b, R // 8):
                groups[i] = groups[i] - factors[i - b] * row
        pivots.append(diagonal)
    return jnp.concatenate([(a * lax.rsqrt(d))[:, R:] for a, d in zip(groups, pivots)], axis=0)


def gram_matrix(rows):
    a1, a2, a3 = split3(rows)
    t = dot(jnp.concatenate([a1, a2, a3], 0), jnp.concatenate([a1, a2], 0), NT)
    t21, t31 = t[R:2 * R, :R], t[2 * R:, :R]
    return t[:R, :R] + ((t21 + t21.T) + (t[R:2 * R, R:] + (t31 + t31.T)))


def wide(blocks_ref):
    return jnp.concatenate([blocks_ref[j] for j in range(BLOCKS)], axis=1)


def product(p, m):
    p1, p2, p3 = split3(p)
    m1, m2, m3 = split3(m)
    t1 = dot(jnp.concatenate([p1, p2, p3], 0), m1)
    t2 = dot(jnp.concatenate([p1, p2], 0), m2)
    return t1[:R] + ((t1[R:2 * R] + t2[:R]) + ((t1[2 * R:] + t2[R:]) + dot(p1, m3)))


def term_kernel(own_ref, m_ref, arrived_ref, *rest, partner):
    w_ref = rest[-1]
    core = lax.axis_index("c")
    at = lanes((1 - core if partner else core) * (KV // 2), KV // 2)
    w_ref[...] = product(wide(own_ref), m_ref[:, at] + arrived_ref[:, at])


def term(own, moment, arrived, *after):
    return pl.pallas_call(
        functools.partial(term_kernel, partner=not after),
        in_specs=[VMEM] * 3 + [ANY] * len(after),
        out_specs=VMEM,
        out_shape=shape(R, KV // 2),
        compiler_params=LIMIT,
        cost_estimate=BESIDE,
        name="own_term" if after else "partner_term",
    )(own, moment, arrived, *after)


def own_gram_kernel(own_ref, after_ref, gram_ref):
    del after_ref
    gram_ref[...] = gram_matrix(wide(own_ref))


def own_gram(own, after):
    return pl.pallas_call(
        own_gram_kernel,
        in_specs=[VMEM, ANY],
        out_specs=VMEM,
        out_shape=shape(R, R),
        compiler_params=LIMIT,
        cost_estimate=BESIDE,
        name="own_gram",
    )(own, after)


def first_round_kernel(own_ref, other_ref, own_gram_ref, gram_ref, after_ref, b_ref, l_ref, part_ref):
    del after_ref
    core = lax.axis_index("c")
    for j in range(BLOCKS):
        b_ref[:, lanes(core * HALF + j * 128, 128)] = own_ref[j]
        b_ref[:, lanes(HALF - core * HALF + j * 128, 128)] = other_ref[j]
    factor = inverse_factor(own_gram_ref[...] + gram_ref[...])
    l_ref[...] = factor
    f1, f2, f3 = split3(factor)
    p1, p2, p3 = split3(b_ref[...])
    small = dot(jnp.concatenate([f2, f1, f2, f3, f1], 1), jnp.concatenate([p1, p2, p2, p1, p3], 0))
    b_ref[...] = dot(f1, p1) + small
    part_ref[...] = gram_matrix(b_ref[:, :LOAD])


def first_round(own, other, gram, other_gram, after):
    return pl.pallas_call(
        first_round_kernel,
        in_specs=[VMEM] * 4 + [ANY],
        out_specs=[VMEM] * 3,
        out_shape=[shape(R, DW), shape(R, R), shape(R, R)],
        compiler_params=LIMIT,
        cost_estimate=BESIDE,
        name="first_round",
    )(own, other, gram, other_gram, after)


def second_factor_kernel(b_ref, part_ref, after_ref, l_ref, bt_ref):
    del after_ref
    l_ref[...] = inverse_factor(part_ref[...] + gram_matrix(b_ref[:, LOAD:]))
    bt_ref[...] = jnp.concatenate(split2(b_ref[...]), 0).T


def second_factor(basis, part, after):
    return pl.pallas_call(
        second_factor_kernel,
        in_specs=[VMEM, VMEM, ANY],
        out_specs=[VMEM] * 2,
        out_shape=[shape(R, R), shape(DW, 2 * R, dtype=BF)],
        compiler_params=LIMIT,
        cost_estimate=BESIDE,
        name="second_factor",
    )(basis, part, after)


def finish_kernel(b_ref, l1_ref, l2_ref, after_ref, p_ref, f_ref):
    del after_ref
    factor = l2_ref[...]
    both = dot_high(factor, l1_ref[...]) * (1.0 / (NZ * NY * NC))
    f_ref[:R, :] = both
    f_ref[R:, :] = dot_high(factor, both, TN)
    f1, f2, f3 = split3(factor)
    b1, b2, b3 = split3(b_ref[...])
    f = jnp.concatenate([f1, f2, f3, f1, f2, f1], 1)
    p_ref[...] = dot(f, jnp.concatenate([b1, b1, b1, b2, b2, b3], 0))


def finish(basis, factor1, factor2, after):
    return pl.pallas_call(
        finish_kernel,
        in_specs=[VMEM] * 3 + [ANY],
        out_specs=[VMEM] * 2,
        out_shape=[shape(R, DW), shape(2 * R, R)],
        compiler_params=LIMIT,
        cost_estimate=BESIDE,
        name="finish",
    )(basis, factor1, factor2, after)


def update_kernel(m_own_ref, m_other_ref, bt_ref, f_ref, w_own_ref, w_other_ref, p_ref, e_hbm, q_hbm, p_hbm, w_ref, q_ref, out, sems):
    core = lax.axis_index("c")
    copies = [pltpu.make_async_copy(p_ref, p_hbm, sems.at[0]), pltpu.make_async_copy(q_ref, q_hbm, sems.at[1])]
    copies[0].start()
    w_ref[:, lanes(core * (KV // 2), KV // 2)] = w_own_ref[...]
    w_ref[:, lanes((1 - core) * (KV // 2), KV // 2)] = w_other_ref[...]
    qr = dot_high(f_ref[...], w_ref[...])
    q_ref[...] = qr[:R]
    copies[1].start()
    r1, r2 = split2(qr[R:])
    weights = jnp.concatenate([r1, r1, r2, jnp.zeros_like(r1)], 0)
    for part, (base, m_ref) in enumerate(((core * HALF, m_own_ref), (HALF - core * HALF, m_other_ref))):
        for t in range(0, HALF, COLS):
            at, here = lanes(base + t, COLS), pl.ds(part * HALF + t, COLS)
            bt = bt_ref[at, :]
            out[here, :] = m_ref[t:t + COLS, :] - dot(jnp.concatenate([bt, bt], 1), weights)
            copies.append(pltpu.make_async_copy(out.at[here, :], e_hbm.at[at, :], sems.at[len(copies)]))
            copies[-1].start()
    for copy in copies:
        copy.wait()


def update(m_own, m_other, basis_t, factors, w_own, w_other, p_rows):
    return pl.pallas_call(
        update_kernel,
        in_specs=[VMEM] * 7,
        out_specs=[HBM] * 3,
        out_shape=[shape(DW, KV), shape(R, KV), shape(R, DW)],
        scratch_shapes=[
            pltpu.VMEM((R, KV), F32),
            pltpu.VMEM((R, KV), F32),
            pltpu.VMEM((DW, KV), F32),
            pltpu.SemaphoreType.DMA((2 + DW // COLS,)),
        ],
        compiler_params=LIMIT,
        name="update",
    )(m_own, m_other, basis_t, factors, w_own, w_other, p_rows)


def pair_kernel(w_ref, arrived_ref, after_ref, out_ref):
    del after_ref
    total = w_ref[...] + arrived_ref[...]
    for i in range(out_ref.shape[0]):
        out_ref[i] = total


def sum_pair(w, arrived, after, copies):
    return pl.pallas_call(
        pair_kernel,
        in_specs=[VMEM] * 2 + [ANY],
        out_specs=VMEM,
        out_shape=shape(copies, *w.shape),
        compiler_params=SMALL,
        name="sum_pair",
    )(w, arrived, after)


def exchange(parts, axes):
    return lax.all_to_all(parts, axes, split_axis=0, concat_axis=0, tiled=True)


def sum_kernel(parts_ref, out_ref):
    total = parts_ref[0]
    for i in range(1, parts_ref.shape[0]):
        total = total + parts_ref[i]
    for i in range(out_ref.shape[0]):
        out_ref[i] = total


def sum_parts(parts, copies):
    return pl.pallas_call(
        sum_kernel,
        in_specs=[VMEM],
        out_specs=VMEM,
        out_shape=shape(copies, *parts.shape[1:]),
        compiler_params=SMALL,
        name="sum_parts",
    )(parts)


def swap(array):
    return lax.ppermute(array, "c", SWAP)


def swap_y(array, mask):
    return lax.ppermute(array, "y", [(i, i ^ mask) for i in range(NY)])


def shards(inputs, out_grads, error_buffer, start_basis):
    arguments = (inputs, out_grads, error_buffer[0], start_basis.T)
    x, g, e, s_rows = [pltpu.with_memory_space_constraint(array, pltpu.HBM) for array in arguments]
    m_other, p_other, *rest = moment_of_other(x, g, e, s_rows)
    arrived = swap(p_other)
    e_own, x_own, g, s_rows = rest
    m_own, p_own = moment_of_own(x_own, g, e_own, s_rows)
    m_arrived = swap(m_other)

    parts = exchange(p_own + arrived, ("y", "x"))
    parts = exchange(sum_parts(parts, NZ), "z")
    own = exchange(sum_parts(parts, NY * NX), ("y", "x"))
    other = swap(own)
    w = term(own, m_own, m_arrived)
    arrived = swap(w)
    w = term(own, m_own, m_arrived, w)
    gram = own_gram(own, w)
    w = sum_pair(w, arrived, gram, 1)[0]
    arrived = swap_y(w, 1)
    basis, factor1, part = first_round(own, other, gram, swap(gram), w)
    w = sum_pair(w, arrived, factor1, 1)[0]
    arrived = swap_y(w, 3)
    factor2, basis_t = second_factor(basis, part, w)
    w = sum_parts(exchange(sum_pair(w, arrived, factor2, NZ), "z"), 1)[0]
    p_rows, factors = finish(basis, factor1, factor2, w)
    error, q_rows, p_rows = update(m_own, m_other, basis_t, factors, w, swap(w), p_rows)
    return (p_rows.T, q_rows.T, error[None])


def solution(mesh):
    fine = Mesh(mesh.devices.reshape(NZ, NY, NC, NX), ("z", "y", "c", "x"))
    dp = ("z", "y", "c")
    in_specs = (P(dp, None), P(dp, "x"), P(dp, None, "x"), P("x", None))
    out_specs = (P(), P("x", None), P(dp, None, "x"))
    return jax.shard_map(shards, mesh=fine, in_specs=in_specs, out_specs=out_specs, check_vma=False)
```

```python
import jax
import jax.numpy as jnp
from jax import lax
from jax.experimental import pallas as pl
from jax.experimental.pallas import tpu as pltpu
from jax.sharding import Mesh, PartitionSpec as P

HIGH = lax.Precision.HIGHEST
NZ, NY, NC, NX = 8, 4, 2, 4
DW, KV, R, TOK = 4096, 256, 64, 384
HALF, BLOCKS = DW // 2, DW // 256
BF, F32 = jnp.bfloat16, jnp.float32
SWAP = [(0, 1), (1, 0)]
NN = (((1,), (0,)), ((), ()))
NT = (((1,), (1,)), ((), ()))
TN = (((0,), (0,)), ((), ()))
VMEM = pl.BlockSpec(memory_space=pltpu.VMEM)
SMEM = pl.BlockSpec(memory_space=pltpu.SMEM)
HBM = pl.BlockSpec(memory_space=pltpu.HBM)
ANY = pl.BlockSpec(memory_space=pl.ANY)
BESIDE = pl.CostEstimate(flops=10 ** 9, bytes_accessed=4 << 20, transcendentals=0)
LIMIT = pltpu.CompilerParams(vmem_limit_bytes=24 << 20)
SMALL = pltpu.CompilerParams(vmem_limit_bytes=8 << 20)


def shape(*dims, dtype=F32):
    return jax.ShapeDtypeStruct(dims, dtype)


def dot(a, b, dims=NN):
    return lax.dot_general(a, b, dims, preferred_element_type=F32)


def dot_high(a, b, dims=NN):
    return lax.dot_general(a, b, dims, precision=HIGH, preferred_element_type=F32)


def lanes(start, size):
    return pl.ds(pl.multiple_of(start, size), size)


def split2(x):
    high = x.astype(BF)
    return high, (x - high.astype(F32)).astype(BF)


def split3(x):
    high = x.astype(BF)
    rest = x - high.astype(F32)
    middle = rest.astype(BF)
    return high, middle, (rest - middle.astype(F32)).astype(BF)


COLS = 512
LOAD = 1024


def p_blocks(moment, basis, p_ref, first):
    s1, s2, s3 = split3(basis)
    none = jnp.zeros_like(s1)
    orders = (s3, s2, s1), (s2, s1, none), (s1, none, none)
    weights = jnp.concatenate([jnp.concatenate(order, 1) for order in orders], 0)
    t = dot(jnp.concatenate(split3(moment), 1), weights, NT).T
    rows = (t[:R] + t[R:2 * R]) + t[2 * R:]
    for i in range(moment.shape[0] // 128):
        p_ref[first + i] = rows[:, i * 128:(i + 1) * 128]


def moment_kernel(core_ref, x_hbm, g_hbm, e_hbm, s_hbm, m_ref, p_ref, e_ref, x_ref, g_ref, s_ref, x_buf, sems):
    core = core_ref[0]
    steps = HALF // LOAD
    copies = [pltpu.make_async_copy(g_hbm, g_ref, sems.at[0]), pltpu.make_async_copy(s_hbm, s_ref, sems.at[1])]
    for base, x_to, e_to in ((HALF - core * HALF, x_buf, m_ref), (core * HALF, x_ref, e_ref)):
        for j in range(steps):
            at, to = lanes(base + j * LOAD, LOAD), pl.ds(j * LOAD, LOAD)
            copies.append(pltpu.make_async_copy(x_hbm.at[:, at], x_to.at[j], sems.at[len(copies)]))
            copies.append(pltpu.make_async_copy(e_hbm.at[at, :], e_to.at[to, :], sems.at[len(copies)]))
    for copy in copies:
        copy.start()
    copies[0].wait()
    copies[1].wait()
    g = g_ref[...]
    for j in range(steps):
        copies[2 + 2 * j].wait()
        copies[3 + 2 * j].wait()
        at = pl.ds(j * LOAD, LOAD)
        moment = dot(x_buf[j], g, TN) + m_ref[at, :]
        m_ref[at, :] = moment
        p_blocks(moment, s_ref[...], p_ref, j * (LOAD // 128))
    for copy in copies[2 + 2 * steps:]:
        copy.wait()


def moment_of_other(core, x, g, e, s_rows):
    steps = HALF // LOAD
    return pl.pallas_call(
        moment_kernel,
        in_specs=[SMEM, HBM, HBM, HBM, HBM],
        out_specs=[VMEM] * 6,
        out_shape=[
            shape(HALF, KV),
            shape(BLOCKS, R, 128),
            shape(HALF, KV),
            shape(steps, TOK, LOAD, dtype=BF),
            shape(TOK, KV, dtype=BF),
            shape(R, KV),
        ],
        scratch_shapes=[pltpu.VMEM((steps, TOK, LOAD), BF), pltpu.SemaphoreType.DMA((2 + 4 * steps,))],
        compiler_params=LIMIT,
        name="moment_other",
    )(core.reshape(1), x, g, e, s_rows)


def own_kernel(x_ref, g_ref, e_ref, s_ref, m_ref, p_ref):
    g = g_ref[...]
    for j in range(HALF // LOAD):
        at = pl.ds(j * LOAD, LOAD)
        m_ref[at, :] = dot(x_ref[j], g, TN) + e_ref[at, :]
    p_blocks(m_ref[...], s_ref[...], p_ref, 0)


def moment_of_own(x, g, e, s_rows):
    return pl.pallas_call(
        own_kernel,
        in_specs=[VMEM] * 4,
        out_specs=[VMEM] * 2,
        out_shape=[shape(HALF, KV), shape(BLOCKS, R, 128)],
        compiler_params=LIMIT,
        cost_estimate=BESIDE,
        name="moment_own",
    )(x, g, e, s_rows)


def inverse_factor(gram):
    rows = lax.broadcasted_iota(jnp.int32, (8, 128), 0)
    lanes = lax.broadcasted_iota(jnp.int32, (8, 128), 1)
    zero = jnp.zeros((8, R), F32)
    groups = [
        jnp.where(lanes == rows + R + 8 * i, 1.0, jnp.concatenate([gram[8 * i:8 * i + 8], zero], axis=1))
        for i in range(R // 8)
    ]
    pivots = []
    for b in range(R // 8):
        columns = [
            [jnp.broadcast_to(groups[i][:, 8 * b + c:8 * b + c + 1], (8, 128)) for i in range(b, R // 8)]
            for c in range(8)
        ]
        diagonal = jnp.zeros((8, 128), F32)
        for j in range(8):
            head = columns[j][0]
            pivot = jnp.broadcast_to(head[j:j + 1], (8, 128))
            inverse = 1.0 / pivot
            diagonal = jnp.where(rows == j, pivot, diagonal)
            factors = [column * inverse for column in columns[j]]
            factors[0] = jnp.where(rows > j, factors[0], 0.0)
            row = jnp.broadcast_to(groups[b][j:j + 1], (8, 128))
            for c in range(j + 1, 8):
                weight = jnp.broadcast_to(head[c:c + 1], (8, 128))
                columns[c] = [column - factor * weight for column, factor in zip(columns[c], factors)]
            for i in range(b, R // 8):
                groups[i] = groups[i] - factors[i - b] * row
        pivots.append(diagonal)
    return jnp.concatenate([(a * lax.rsqrt(d))[:, R:] for a, d in zip(groups, pivots)], axis=0)


def gram_matrix(rows):
    a1, a2, a3 = split3(rows)
    t = dot(jnp.concatenate([a1, a2, a3], 0), jnp.concatenate([a1, a2], 0), NT)
    t21, t31 = t[R:2 * R, :R], t[2 * R:, :R]
    return t[:R, :R] + ((t21 + t21.T) + (t[R:2 * R, R:] + (t31 + t31.T)))


def wide(blocks_ref):
    return jnp.concatenate([blocks_ref[j] for j in range(BLOCKS)], axis=1)


def product(p, m):
    p1, p2, p3 = split3(p)
    m1, m2, m3 = split3(m)
    t1 = dot(jnp.concatenate([p1, p2, p3], 0), m1)
    t2 = dot(jnp.concatenate([p1, p2], 0), m2)
    return t1[:R] + ((t1[R:2 * R] + t2[:R]) + ((t1[2 * R:] + t2[R:]) + dot(p1, m3)))


def own_term_kernel(core_ref, own_ref, m_ref, arrived_ref, w_own_ref, w_other_ref, w_ref):
    w_ref[...] = product(wide(own_ref), m_ref[...] + arrived_ref[...])
    mine = core_ref[0] * (R // 2)
    w_own_ref[...] = w_ref[lanes(mine, R // 2), :]
    w_other_ref[...] = w_ref[lanes(R // 2 - mine, R // 2), :]


def own_term(core, own, moment, arrived):
    return pl.pallas_call(
        own_term_kernel,
        in_specs=[SMEM] + [VMEM] * 3,
        out_specs=[VMEM] * 2,
        out_shape=[shape(R // 2, KV), shape(R // 2, KV)],
        scratch_shapes=[pltpu.VMEM((R, KV), F32)],
        compiler_params=LIMIT,
        cost_estimate=BESIDE,
        name="own_term",
    )(core.reshape(1), own, moment, arrived)


def own_gram_kernel(own_ref, after_ref, gram_ref):
    del after_ref
    gram_ref[...] = gram_matrix(wide(own_ref))


def own_gram(own, after):
    return pl.pallas_call(
        own_gram_kernel,
        in_specs=[VMEM, ANY],
        out_specs=VMEM,
        out_shape=shape(R, R),
        compiler_params=LIMIT,
        cost_estimate=BESIDE,
        name="own_gram",
    )(own, after)


def other_gram_kernel(other_ref, part_ref, gram_ref):
    gram_ref[...] = part_ref[...] + gram_matrix(wide(other_ref))


def other_gram(other, part):
    return pl.pallas_call(
        other_gram_kernel,
        in_specs=[VMEM, VMEM],
        out_specs=VMEM,
        out_shape=shape(R, R),
        compiler_params=LIMIT,
        cost_estimate=BESIDE,
        name="other_gram",
    )(other, part)


def first_round_kernel(core_ref, own_ref, other_ref, gram_ref, after_ref, b_ref, l_ref, part_ref):
    del after_ref
    core = core_ref[0]
    for j in range(BLOCKS):
        b_ref[:, lanes(core * HALF + j * 128, 128)] = own_ref[j]
        b_ref[:, lanes(HALF - core * HALF + j * 128, 128)] = other_ref[j]
    factor = inverse_factor(gram_ref[...])
    l_ref[...] = factor
    f1, f2, f3 = split3(factor)
    p1, p2, p3 = split3(b_ref[...])
    small = dot(jnp.concatenate([f2, f1, f2, f3, f1], 1), jnp.concatenate([p1, p2, p2, p1, p3], 0))
    b_ref[...] = dot(f1, p1) + small
    part_ref[...] = gram_matrix(b_ref[:, :LOAD])


def first_round(core, own, other, gram, after):
    return pl.pallas_call(
        first_round_kernel,
        in_specs=[SMEM] + [VMEM] * 3 + [ANY],
        out_specs=[VMEM] * 3,
        out_shape=[shape(R, DW), shape(R, R), shape(R, R)],
        compiler_params=LIMIT,
        cost_estimate=BESIDE,
        name="first_round",
    )(core.reshape(1), own, other, gram, after)


def second_factor_kernel(b_ref, part_ref, after_ref, l_ref, bt_ref):
    del after_ref
    l_ref[...] = inverse_factor(part_ref[...] + gram_matrix(b_ref[:, LOAD:]))
    bt_ref[...] = jnp.concatenate(split2(b_ref[...]), 0).T


def second_factor(basis, part, after):
    return pl.pallas_call(
        second_factor_kernel,
        in_specs=[VMEM, VMEM, ANY],
        out_specs=[VMEM] * 2,
        out_shape=[shape(R, R), shape(DW, 2 * R, dtype=BF)],
        compiler_params=LIMIT,
        cost_estimate=BESIDE,
        name="second_factor",
    )(basis, part, after)


def finish_kernel(b_ref, l1_ref, l2_ref, after_ref, p_ref, f_ref):
    del after_ref
    factor = l2_ref[...]
    both = dot_high(factor, l1_ref[...]) * (1.0 / (NZ * NY * NC))
    f_ref[:R, :] = both
    f_ref[R:, :] = dot_high(factor, both, TN)
    f1, f2, f3 = split3(factor)
    b1, b2, b3 = split3(b_ref[...])
    f = jnp.concatenate([f1, f2, f3, f1, f2, f1], 1)
    p_ref[...] = dot(f, jnp.concatenate([b1, b1, b1, b2, b2, b3], 0))


def finish(basis, factor1, factor2, after):
    return pl.pallas_call(
        finish_kernel,
        in_specs=[VMEM] * 3 + [ANY],
        out_specs=[VMEM] * 2,
        out_shape=[shape(R, DW), shape(2 * R, R)],
        compiler_params=LIMIT,
        cost_estimate=BESIDE,
        name="finish",
    )(basis, factor1, factor2, after)


def update_kernel(core_ref, m_own_ref, m_other_ref, bt_ref, f_ref, w_own_ref, w_other_ref, p_ref, e_hbm, q_hbm, p_hbm, w_ref, q_ref, out, sems):
    core = core_ref[0]
    copies = [pltpu.make_async_copy(p_ref, p_hbm, sems.at[0]), pltpu.make_async_copy(q_ref, q_hbm, sems.at[1])]
    copies[0].start()
    w_ref[lanes(core * (R // 2), R // 2), :] = w_own_ref[...]
    w_ref[lanes(R // 2 - core * (R // 2), R // 2), :] = w_other_ref[...]
    qr = dot_high(f_ref[...], w_ref[...])
    q_ref[...] = qr[:R]
    copies[1].start()
    r1, r2 = split2(qr[R:])
    weights = jnp.concatenate([r1, r1, r2, jnp.zeros_like(r1)], 0)
    for part, (base, m_ref) in enumerate(((core * HALF, m_own_ref), (HALF - core * HALF, m_other_ref))):
        for t in range(0, HALF, COLS):
            at, here = lanes(base + t, COLS), pl.ds(part * HALF + t, COLS)
            bt = bt_ref[at, :]
            out[here, :] = m_ref[t:t + COLS, :] - dot(jnp.concatenate([bt, bt], 1), weights)
            copies.append(pltpu.make_async_copy(out.at[here, :], e_hbm.at[at, :], sems.at[len(copies)]))
            copies[-1].start()
    for copy in copies:
        copy.wait()


def update(core, m_own, m_other, basis_t, factors, w_own, w_other, p_rows):
    return pl.pallas_call(
        update_kernel,
        in_specs=[SMEM] + [VMEM] * 7,
        out_specs=[HBM] * 3,
        out_shape=[shape(DW, KV), shape(R, KV), shape(R, DW)],
        scratch_shapes=[
            pltpu.VMEM((R, KV), F32),
            pltpu.VMEM((R, KV), F32),
            pltpu.VMEM((DW, KV), F32),
            pltpu.SemaphoreType.DMA((2 + DW // COLS,)),
        ],
        compiler_params=LIMIT,
        name="update",
    )(core.reshape(1), m_own, m_other, basis_t, factors, w_own, w_other, p_rows)


def pair_kernel(w_ref, arrived_ref, after_ref, out_ref):
    del after_ref
    total = w_ref[...] + arrived_ref[...]
    for i in range(out_ref.shape[0]):
        out_ref[i] = total


def sum_pair(w, arrived, after, copies):
    return pl.pallas_call(
        pair_kernel,
        in_specs=[VMEM] * 2 + [ANY],
        out_specs=VMEM,
        out_shape=shape(copies, *w.shape),
        compiler_params=SMALL,
        name="sum_pair",
    )(w, arrived, after)


def exchange(parts, axes):
    return lax.all_to_all(parts, axes, split_axis=0, concat_axis=0, tiled=True)


def sum_kernel(parts_ref, out_ref):
    total = parts_ref[0]
    for i in range(1, parts_ref.shape[0]):
        total = total + parts_ref[i]
    for i in range(out_ref.shape[0]):
        out_ref[i] = total


def sum_parts(parts, copies):
    return pl.pallas_call(
        sum_kernel,
        in_specs=[VMEM],
        out_specs=VMEM,
        out_shape=shape(copies, *parts.shape[1:]),
        compiler_params=SMALL,
        name="sum_parts",
    )(parts)


def swap(array):
    return lax.ppermute(array, "c", SWAP)


def swap_y(array, mask):
    return lax.ppermute(array, "y", [(i, i ^ mask) for i in range(NY)])


def shards(inputs, out_grads, error_buffer, start_basis):
    core = lax.axis_index("c")
    arguments = (inputs, out_grads, error_buffer[0], start_basis.T)
    x, g, e, s_rows = [pltpu.with_memory_space_constraint(array, pltpu.HBM) for array in arguments]
    m_other, p_other, *rest = moment_of_other(core, x, g, e, s_rows)
    arrived = swap(p_other)
    e_own, x_own, g, s_rows = rest
    m_own, p_own = moment_of_own(x_own, g, e_own, s_rows)
    m_arrived = swap(m_other)

    parts = exchange(p_own + arrived, ("y", "x"))
    parts = exchange(sum_parts(parts, NZ), "z")
    own = exchange(sum_parts(parts, NY * NX), ("y", "x"))
    other = swap(own)
    w_own, w_other = own_term(core, own, m_own, m_arrived)

    arrived = swap(w_other)
    gram = other_gram(other, own_gram(own, w_own))
    w = sum_pair(w_own, arrived, gram, 1)[0]
    arrived = swap_y(w, 1)
    basis, factor1, part = first_round(core, own, other, gram, w)
    w = sum_pair(w, arrived, factor1, 1)[0]
    arrived = swap_y(w, 3)
    factor2, basis_t = second_factor(basis, part, w)
    w = sum_parts(exchange(sum_pair(w, arrived, factor2, NZ), "z"), 1)[0]
    p_rows, factors = finish(basis, factor1, factor2, w)
    error, q_rows, p_rows = update(core, m_own, m_other, basis_t, factors, w, swap(w), p_rows)
    return (p_rows.T, q_rows.T, error[None])


def solution(mesh):
    fine = Mesh(mesh.devices.reshape(NZ, NY, NC, NX), ("z", "y", "c", "x"))
    dp = ("z", "y", "c")
    in_specs = (P(dp, None), P(dp, "x"), P(dp, None, "x"), P("x", None))
    out_specs = (P(), P("x", None), P(dp, None, "x"))
    return jax.shard_map(shards, mesh=fine, in_specs=in_specs, out_specs=out_specs, check_vma=False)
```

```python
import jax
import jax.numpy as jnp
from jax import lax
from jax.experimental import pallas as pl
from jax.experimental.pallas import tpu as pltpu
from jax.sharding import Mesh, PartitionSpec as P

HIGH = lax.Precision.HIGHEST
NZ, NY, NC, NX = 8, 4, 2, 4
DW, KV, R, TOK = 4096, 256, 64, 384
HALF, BLOCKS = DW // 2, DW // 256
BF, F32 = jnp.bfloat16, jnp.float32
SWAP = [(0, 1), (1, 0)]
NN = (((1,), (0,)), ((), ()))
NT = (((1,), (1,)), ((), ()))
TN = (((0,), (0,)), ((), ()))
VMEM = pl.BlockSpec(memory_space=pltpu.VMEM)
SMEM = pl.BlockSpec(memory_space=pltpu.SMEM)
HBM = pl.BlockSpec(memory_space=pltpu.HBM)
ANY = pl.BlockSpec(memory_space=pl.ANY)
BESIDE = pl.CostEstimate(flops=10 ** 9, bytes_accessed=4 << 20, transcendentals=0)
LIMIT = pltpu.CompilerParams(vmem_limit_bytes=24 << 20)
SMALL = pltpu.CompilerParams(vmem_limit_bytes=8 << 20)


def shape(*dims, dtype=F32):
    return jax.ShapeDtypeStruct(dims, dtype)


def dot(a, b, dims=NN):
    return lax.dot_general(a, b, dims, preferred_element_type=F32)


def dot_high(a, b, dims=NN):
    return lax.dot_general(a, b, dims, precision=HIGH, preferred_element_type=F32)


def lanes(start, size):
    return pl.ds(pl.multiple_of(start, size), size)


def split2(x):
    high = x.astype(BF)
    return high, (x - high.astype(F32)).astype(BF)


def split3(x):
    high = x.astype(BF)
    rest = x - high.astype(F32)
    middle = rest.astype(BF)
    return high, middle, (rest - middle.astype(F32)).astype(BF)


COLS = 512
LOAD = 1024


def p_half(moment, basis, p_ref):
    s1, s2, s3 = split3(basis)
    none = jnp.zeros_like(s1)
    orders = (s3, s2, s1), (s2, s1, none), (s1, none, none)
    weights = jnp.concatenate([jnp.concatenate(order, 1) for order in orders], 0)
    t = dot(jnp.concatenate(split3(moment), 1), weights, NT).T
    rows = (t[:R] + t[R:2 * R]) + t[2 * R:]
    for i in range(BLOCKS):
        p_ref[i] = rows[:, i * 128:(i + 1) * 128]


def moment_kernel(core_ref, x_hbm, g_hbm, e_hbm, s_hbm, m_ref, p_ref, e_ref, x_ref, g_ref, s_ref, x_buf, sems):
    core = core_ref[0]
    steps = HALF // LOAD
    copies = [pltpu.make_async_copy(g_hbm, g_ref, sems.at[0]), pltpu.make_async_copy(s_hbm, s_ref, sems.at[1])]
    for base, x_to, e_to in ((HALF - core * HALF, x_buf, m_ref), (core * HALF, x_ref, e_ref)):
        for j in range(steps):
            at, to = lanes(base + j * LOAD, LOAD), pl.ds(j * LOAD, LOAD)
            copies.append(pltpu.make_async_copy(x_hbm.at[:, at], x_to.at[j], sems.at[len(copies)]))
            copies.append(pltpu.make_async_copy(e_hbm.at[at, :], e_to.at[to, :], sems.at[len(copies)]))
    for copy in copies[:2 + 2 * steps]:
        copy.start()
    copies[0].wait()
    copies[1].wait()
    g = g_ref[...]
    for j in range(steps):
        copies[2 + 2 * j].wait()
        copies[3 + 2 * j].wait()
        for copy in copies[2 + 2 * steps:] if j == 0 else ():
            copy.start()
        at = pl.ds(j * LOAD, LOAD)
        m_ref[at, :] = dot(x_buf[j], g, TN) + m_ref[at, :]
    p_half(m_ref[...], s_ref[...], p_ref)
    for copy in copies[2 + 2 * steps:]:
        copy.wait()


def moment_of_other(core, x, g, e, s_rows):
    steps = HALF // LOAD
    return pl.pallas_call(
        moment_kernel,
        in_specs=[SMEM, HBM, HBM, HBM, HBM],
        out_specs=[VMEM] * 6,
        out_shape=[
            shape(HALF, KV),
            shape(BLOCKS, R, 128),
            shape(HALF, KV),
            shape(steps, TOK, LOAD, dtype=BF),
            shape(TOK, KV, dtype=BF),
            shape(R, KV),
        ],
        scratch_shapes=[pltpu.VMEM((steps, TOK, LOAD), BF), pltpu.SemaphoreType.DMA((2 + 4 * steps,))],
        compiler_params=LIMIT,
        name="moment_other",
    )(core.reshape(1), x, g, e, s_rows)


def own_kernel(x_ref, g_ref, e_ref, s_ref, m_ref, p_ref):
    g = g_ref[...]
    for j in range(HALF // LOAD):
        at = pl.ds(j * LOAD, LOAD)
        m_ref[at, :] = dot(x_ref[j], g, TN) + e_ref[at, :]
    p_half(m_ref[...], s_ref[...], p_ref)


def moment_of_own(x, g, e, s_rows):
    return pl.pallas_call(
        own_kernel,
        in_specs=[VMEM] * 4,
        out_specs=[VMEM] * 2,
        out_shape=[shape(HALF, KV), shape(BLOCKS, R, 128)],
        compiler_params=LIMIT,
        cost_estimate=BESIDE,
        name="moment_own",
    )(x, g, e, s_rows)


def inverse_factor(gram):
    rows = lax.broadcasted_iota(jnp.int32, (8, 128), 0)
    lanes = lax.broadcasted_iota(jnp.int32, (8, 128), 1)
    zero = jnp.zeros((8, R), F32)
    groups = [
        jnp.where(lanes == rows + R + 8 * i, 1.0, jnp.concatenate([gram[8 * i:8 * i + 8], zero], axis=1))
        for i in range(R // 8)
    ]
    pivots = []
    for b in range(R // 8):
        columns = [
            [jnp.broadcast_to(groups[i][:, 8 * b + c:8 * b + c + 1], (8, 128)) for i in range(b, R // 8)]
            for c in range(8)
        ]
        diagonal = jnp.zeros((8, 128), F32)
        for j in range(8):
            head = columns[j][0]
            pivot = jnp.broadcast_to(head[j:j + 1], (8, 128))
            inverse = 1.0 / pivot
            diagonal = jnp.where(rows == j, pivot, diagonal)
            factors = [column * inverse for column in columns[j]]
            factors[0] = jnp.where(rows > j, factors[0], 0.0)
            row = jnp.broadcast_to(groups[b][j:j + 1], (8, 128))
            for c in range(j + 1, 8):
                weight = jnp.broadcast_to(head[c:c + 1], (8, 128))
                columns[c] = [column - factor * weight for column, factor in zip(columns[c], factors)]
            for i in range(b, R // 8):
                groups[i] = groups[i] - factors[i - b] * row
        pivots.append(diagonal)
    return jnp.concatenate([(a * lax.rsqrt(d))[:, R:] for a, d in zip(groups, pivots)], axis=0)


def gram_matrix(rows):
    a1, a2, a3 = split3(rows)
    t = dot(jnp.concatenate([a1, a2, a3], 0), jnp.concatenate([a1, a2], 0), NT)
    t21, t31 = t[R:2 * R, :R], t[2 * R:, :R]
    return t[:R, :R] + ((t21 + t21.T) + (t[R:2 * R, R:] + (t31 + t31.T)))


def wide(blocks_ref):
    return jnp.concatenate([blocks_ref[j] for j in range(BLOCKS)], axis=1)


def product(p, m):
    p1, p2, p3 = split3(p)
    m1, m2, m3 = split3(m)
    t1 = dot(jnp.concatenate([p1, p2, p3], 0), m1)
    t2 = dot(jnp.concatenate([p1, p2], 0), m2)
    return t1[:R] + ((t1[R:2 * R] + t2[:R]) + ((t1[2 * R:] + t2[R:]) + dot(p1, m3)))


def own_term_kernel(core_ref, own_ref, m_ref, arrived_ref, w_own_ref, w_other_ref, w_ref):
    w_ref[...] = product(wide(own_ref), m_ref[...] + arrived_ref[...])
    mine = core_ref[0] * (R // 2)
    w_own_ref[...] = w_ref[lanes(mine, R // 2), :]
    w_other_ref[...] = w_ref[lanes(R // 2 - mine, R // 2), :]


def own_term(core, own, moment, arrived):
    return pl.pallas_call(
        own_term_kernel,
        in_specs=[SMEM] + [VMEM] * 3,
        out_specs=[VMEM] * 2,
        out_shape=[shape(R // 2, KV), shape(R // 2, KV)],
        scratch_shapes=[pltpu.VMEM((R, KV), F32)],
        compiler_params=LIMIT,
        cost_estimate=BESIDE,
        name="own_term",
    )(core.reshape(1), own, moment, arrived)


def own_gram_kernel(own_ref, after_ref, gram_ref):
    del after_ref
    gram_ref[...] = gram_matrix(wide(own_ref))


def own_gram(own, after):
    return pl.pallas_call(
        own_gram_kernel,
        in_specs=[VMEM, ANY],
        out_specs=VMEM,
        out_shape=shape(R, R),
        compiler_params=LIMIT,
        cost_estimate=BESIDE,
        name="own_gram",
    )(own, after)


def other_gram_kernel(other_ref, part_ref, gram_ref):
    gram_ref[...] = part_ref[...] + gram_matrix(wide(other_ref))


def other_gram(other, part):
    return pl.pallas_call(
        other_gram_kernel,
        in_specs=[VMEM, VMEM],
        out_specs=VMEM,
        out_shape=shape(R, R),
        compiler_params=LIMIT,
        cost_estimate=BESIDE,
        name="other_gram",
    )(other, part)


def first_round_kernel(core_ref, own_ref, other_ref, gram_ref, after_ref, b_ref, l_ref, part_ref):
    del after_ref
    core = core_ref[0]
    for j in range(BLOCKS):
        b_ref[:, lanes(core * HALF + j * 128, 128)] = own_ref[j]
        b_ref[:, lanes(HALF - core * HALF + j * 128, 128)] = other_ref[j]
    factor = inverse_factor(gram_ref[...])
    l_ref[...] = factor
    f1, f2, f3 = split3(factor)
    p1, p2, p3 = split3(b_ref[...])
    small = dot(jnp.concatenate([f2, f1, f2, f3, f1], 1), jnp.concatenate([p1, p2, p2, p1, p3], 0))
    b_ref[...] = dot(f1, p1) + small
    part_ref[...] = gram_matrix(b_ref[:, :LOAD])


def first_round(core, own, other, gram, after):
    return pl.pallas_call(
        first_round_kernel,
        in_specs=[SMEM] + [VMEM] * 3 + [ANY],
        out_specs=[VMEM] * 3,
        out_shape=[shape(R, DW), shape(R, R), shape(R, R)],
        compiler_params=LIMIT,
        cost_estimate=BESIDE,
        name="first_round",
    )(core.reshape(1), own, other, gram, after)


def second_factor_kernel(b_ref, part_ref, after_ref, l_ref, bt_ref):
    del after_ref
    l_ref[...] = inverse_factor(part_ref[...] + gram_matrix(b_ref[:, LOAD:]))
    bt_ref[...] = jnp.concatenate(split2(b_ref[...]), 0).T


def second_factor(basis, part, after):
    return pl.pallas_call(
        second_factor_kernel,
        in_specs=[VMEM, VMEM, ANY],
        out_specs=[VMEM] * 2,
        out_shape=[shape(R, R), shape(DW, 2 * R, dtype=BF)],
        compiler_params=LIMIT,
        cost_estimate=BESIDE,
        name="second_factor",
    )(basis, part, after)


def finish_kernel(b_ref, l1_ref, l2_ref, after_ref, p_ref, f_ref):
    del after_ref
    factor = l2_ref[...]
    both = dot_high(factor, l1_ref[...]) * (1.0 / (NZ * NY * NC))
    f_ref[:R, :] = both
    f_ref[R:, :] = dot_high(factor, both, TN)
    f1, f2, f3 = split3(factor)
    b1, b2, b3 = split3(b_ref[...])
    f = jnp.concatenate([f1, f2, f3, f1, f2, f1], 1)
    p_ref[...] = dot(f, jnp.concatenate([b1, b1, b1, b2, b2, b3], 0))


def finish(basis, factor1, factor2, after):
    return pl.pallas_call(
        finish_kernel,
        in_specs=[VMEM] * 3 + [ANY],
        out_specs=[VMEM] * 2,
        out_shape=[shape(R, DW), shape(2 * R, R)],
        compiler_params=LIMIT,
        cost_estimate=BESIDE,
        name="finish",
    )(basis, factor1, factor2, after)


def update_kernel(core_ref, m_own_ref, m_other_ref, bt_ref, f_ref, w_own_ref, w_other_ref, p_ref, e_hbm, q_hbm, p_hbm, w_ref, q_ref, out, sems):
    core = core_ref[0]
    copies = [pltpu.make_async_copy(p_ref, p_hbm, sems.at[0]), pltpu.make_async_copy(q_ref, q_hbm, sems.at[1])]
    copies[0].start()
    w_ref[lanes(core * (R // 2), R // 2), :] = w_own_ref[...]
    w_ref[lanes(R // 2 - core * (R // 2), R // 2), :] = w_other_ref[...]
    qr = dot_high(f_ref[...], w_ref[...])
    q_ref[...] = qr[:R]
    copies[1].start()
    r1, r2 = split2(qr[R:])
    weights = jnp.concatenate([r1, r1, r2, jnp.zeros_like(r1)], 0)
    for part, (base, m_ref) in enumerate(((core * HALF, m_own_ref), (HALF - core * HALF, m_other_ref))):
        for t in range(0, HALF, COLS):
            at, here = lanes(base + t, COLS), pl.ds(part * HALF + t, COLS)
            bt = bt_ref[at, :]
            out[here, :] = m_ref[t:t + COLS, :] - dot(jnp.concatenate([bt, bt], 1), weights)
            copies.append(pltpu.make_async_copy(out.at[here, :], e_hbm.at[at, :], sems.at[len(copies)]))
            copies[-1].start()
    for copy in copies:
        copy.wait()


def update(core, m_own, m_other, basis_t, factors, w_own, w_other, p_rows):
    return pl.pallas_call(
        update_kernel,
        in_specs=[SMEM] + [VMEM] * 7,
        out_specs=[HBM] * 3,
        out_shape=[shape(DW, KV), shape(R, KV), shape(R, DW)],
        scratch_shapes=[
            pltpu.VMEM((R, KV), F32),
            pltpu.VMEM((R, KV), F32),
            pltpu.VMEM((DW, KV), F32),
            pltpu.SemaphoreType.DMA((2 + DW // COLS,)),
        ],
        compiler_params=LIMIT,
        name="update",
    )(core.reshape(1), m_own, m_other, basis_t, factors, w_own, w_other, p_rows)


def pair_kernel(w_ref, arrived_ref, after_ref, out_ref):
    del after_ref
    total = w_ref[...] + arrived_ref[...]
    for i in range(out_ref.shape[0]):
        out_ref[i] = total


def sum_pair(w, arrived, after, copies):
    return pl.pallas_call(
        pair_kernel,
        in_specs=[VMEM] * 2 + [ANY],
        out_specs=VMEM,
        out_shape=shape(copies, *w.shape),
        compiler_params=SMALL,
        name="sum_pair",
    )(w, arrived, after)


def exchange(parts, axes):
    return lax.all_to_all(parts, axes, split_axis=0, concat_axis=0, tiled=True)


def sum_kernel(parts_ref, out_ref):
    total = parts_ref[0]
    for i in range(1, parts_ref.shape[0]):
        total = total + parts_ref[i]
    for i in range(out_ref.shape[0]):
        out_ref[i] = total


def sum_parts(parts, copies):
    return pl.pallas_call(
        sum_kernel,
        in_specs=[VMEM],
        out_specs=VMEM,
        out_shape=shape(copies, *parts.shape[1:]),
        compiler_params=SMALL,
        name="sum_parts",
    )(parts)


def swap(array):
    return lax.ppermute(array, "c", SWAP)


def swap_y(array, mask):
    return lax.ppermute(array, "y", [(i, i ^ mask) for i in range(NY)])


def shards(inputs, out_grads, error_buffer, start_basis):
    core = lax.axis_index("c")
    arguments = (inputs, out_grads, error_buffer[0], start_basis.T)
    x, g, e, s_rows = [pltpu.with_memory_space_constraint(array, pltpu.HBM) for array in arguments]
    m_other, p_other, *rest = moment_of_other(core, x, g, e, s_rows)
    arrived = swap(p_other)
    e_own, x_own, g, s_rows = rest
    m_own, p_own = moment_of_own(x_own, g, e_own, s_rows)
    m_arrived = swap(m_other)

    parts = exchange(p_own + arrived, ("y", "x"))
    parts = exchange(sum_parts(parts, NZ), "z")
    own = exchange(sum_parts(parts, NY * NX), ("y", "x"))
    other = swap(own)
    w_own, w_other = own_term(core, own, m_own, m_arrived)

    arrived = swap(w_other)
    gram = other_gram(other, own_gram(own, w_own))
    w = sum_pair(w_own, arrived, gram, 1)[0]
    arrived = swap_y(w, 1)
    basis, factor1, part = first_round(core, own, other, gram, w)
    w = sum_pair(w, arrived, factor1, 1)[0]
    arrived = swap_y(w, 3)
    factor2, basis_t = second_factor(basis, part, w)
    w = sum_parts(exchange(sum_pair(w, arrived, factor2, NZ), "z"), 1)[0]
    p_rows, factors = finish(basis, factor1, factor2, w)
    error, q_rows, p_rows = update(core, m_own, m_other, basis_t, factors, w, swap(w), p_rows)
    return (p_rows.T, q_rows.T, error[None])


def solution(mesh):
    fine = Mesh(mesh.devices.reshape(NZ, NY, NC, NX), ("z", "y", "c", "x"))
    dp = ("z", "y", "c")
    in_specs = (P(dp, None), P(dp, "x"), P(dp, None, "x"), P("x", None))
    out_specs = (P(), P("x", None), P(dp, None, "x"))
    return jax.shard_map(shards, mesh=fine, in_specs=in_specs, out_specs=out_specs, check_vma=False)
```
